32 devices in a mesh: img: 8 (over z, y), grp: 4 (over x, core).
Axes of the slice: x: 2, y: 2, z: 4, core: 2. Of those that a mesh axis runs over, the one named last changes fastest.
Arguments:
- images: bfloat16 [1024, 128, 512], P(('img', 'grp')), may hold values from -18 to 18
- group_ids: int32 [1024], P(('img', 'grp')), may hold values from 0 to 7
- counts: int32 [128], replicated, may hold values from 1 to 128, as said below
- radial_basis: bfloat16 [128, 128, 128], replicated, may hold values from -0.5 to 0.5
- ctf_gain: float32 [8, 128], replicated, may hold values from 0.2 to 2
- noise_var: float32 [128], replicated, may hold values from 0.25 to 2
Outputs:
- denoised: bfloat16 [1024, 128, 512], P(('img', 'grp'))
The draws below stay inside these ranges and needn't reach their ends.
Inputs may be any that keep to these rules, and one draw needn't show every extreme that they name: In every aligned block of 16 frequencies the counts sum to exactly 1280 and the largest is exactly 128.
All inputs are finite; a program needn't handle non-finite values.
Results may differ from the reference program's by a relative error of at most 0.0063.
The reference program's roundings to bfloat16 on the way (of `basis_used`, `spectrum`, `coeffs`, `scaled`, `filters`, `cleaned` and `back`) count: a program that leaves them out, or rounds other values in their place, can miss the bound.
Values may be sent and summed in bfloat16 or wider, within the bound.
No kernel may reach another device: no remote copies, remote signals or barrier semaphores. Data moves between devices by JAX's collectives and lax.ppermute only.
A program may use at most 128 MiB of HBM per device.

```python
import math
import jax
import jax.numpy as jnp
from jax import lax

R = 128
A = 512
K = 128
PMAX = 128
G = 8
NS_ITERS = 7
IMG_DEV = 32
IMAGES = 1024
OWNED = 16
SLOTS = 1280
N_GRP = 4


def draw_images(key, part):
    image_index = jnp.arange(IMAGES, dtype=jnp.int32)
    column = image_index // IMG_DEV % N_GRP
    power = column.astype(jnp.float32) / (N_GRP - 1.0)
    amplitude = jnp.exp(power * jnp.log(3.0))
    values = jnp.clip(jax.random.normal(key, (IMAGES, R, A), jnp.float32), -6.0, 6.0)
    return (values * amplitude[:, None, None]).astype(jnp.bfloat16)


def draw_counts(key, part):
    blocks = K // OWNED
    others = OWNED - 1
    rest = SLOTS - PMAX
    even = rest // others
    extra = rest % others
    index = jnp.arange(others, dtype=jnp.int32)
    base = even + (index < extra).astype(jnp.int32)
    half = others // 2
    first = base[0:2 * half:2]
    second = base[1:2 * half:2]
    limit = jnp.minimum(jnp.minimum(first - 1, PMAX - first), jnp.minimum(second - 1, PMAX - second))
    key_shift = jax.random.fold_in(key, 11)
    key_perm = jax.random.fold_in(key, 23)
    shift = jax.random.randint(key_shift, (blocks, half), -limit[None, :], limit[None, :] + 1)
    paired = jnp.stack([first[None, :] + shift, second[None, :] - shift], -1).reshape(blocks, 2 * half)
    tail = jnp.broadcast_to(base[2 * half:][None, :], (blocks, others - 2 * half))
    peak = jnp.full((blocks, 1), PMAX, dtype=jnp.int32)
    whole = jnp.concatenate([paired, tail, peak], 1).astype(jnp.int32)
    perms = jax.vmap(lambda single: jax.random.permutation(single, OWNED))(jax.random.split(key_perm, blocks))
    placed = jnp.take_along_axis(whole, perms.astype(jnp.int32), 1)
    return placed.reshape(K).astype(jnp.int32)


def with_ends(drawn, stream_key, low, largest):
    longest = drawn.shape.index(max(drawn.shape))
    spots = []
    for shift in (0, 1):
        where = [jax.random.randint(jax.random.fold_in(stream_key, axis), (), 0, length) for axis, length in enumerate(drawn.shape)]
        where[longest] = (where[longest] + shift) % drawn.shape[longest]
        spots.append(tuple(where))
    return drawn.at[spots[0]].set(low).at[spots[1]].set(largest)


def normal_values(stream_key, extent, scale, reach, kind=jnp.bfloat16):
    return jnp.clip(scale * jax.random.normal(stream_key, extent, jnp.float32), -reach, reach).astype(kind)


def setup_inputs(seed: int = 0) -> dict:
    arg_keys = jax.random.split(jax.random.key(seed), 7)
    images = draw_images(jax.random.fold_in(arg_keys[6], 71), 0)
    group_ids = with_ends(jax.random.randint(arg_keys[1], (IMAGES,), 0, G), jax.random.fold_in(arg_keys[1], 1), 0, G - 1).astype(jnp.int32)
    counts = draw_counts(jax.random.fold_in(arg_keys[6], 71), 0)
    radial_basis = normal_values(arg_keys[3], (K, R, PMAX), R ** -0.5, 0.5)
    ctf_gain = jnp.clip(jnp.exp(jax.random.uniform(arg_keys[4], (G, K), jnp.float32, math.log(0.2), math.log(2.0))), 0.2, 2.0)
    noise_var = jnp.clip(jnp.exp(jax.random.uniform(arg_keys[5], (K,), jnp.float32, math.log(0.25), math.log(2.0))), 0.25, 2.0)
    return dict(images=images, group_ids=group_ids, counts=counts, radial_basis=radial_basis, ctf_gain=ctf_gain, noise_var=noise_var)


def dft_tables(angles, freqs):
    angle_index = jnp.arange(angles, dtype=jnp.int32)
    freq_index = jnp.arange(freqs, dtype=jnp.int32)
    turns = angle_index[:, None] * freq_index[None, :] % angles
    phases = turns.astype(jnp.float32) * (2.0 * math.pi / angles)
    factor = 1.0 / math.sqrt(angles)
    cosine = jnp.cos(phases) * factor
    sine = -jnp.sin(phases) * factor
    forward = jnp.concatenate([cosine, sine], 1).astype(jnp.bfloat16)
    doubling = jnp.where(freq_index == 0, 1.0, 2.0).astype(jnp.float32)
    inverse = jnp.concatenate([cosine * doubling[None, :], sine * doubling[None, :]], 1).T.astype(jnp.bfloat16)
    return (forward, inverse)

def shrink_cov(gram, fourth, total, used, image_total):
    sample = gram / total[:, None, None]
    ident = used[:, :, None] * jnp.eye(used.shape[1], dtype=jnp.float32)[None]
    level = jnp.trace(sample, axis1=1, axis2=2) / lax.optimization_barrier(jnp.sum(used, 1))
    spread = lax.optimization_barrier(jnp.sum((sample - level[:, None, None] * ident) ** 2, (1, 2)))
    excess = (fourth / total - lax.optimization_barrier(jnp.sum(sample * sample, (1, 2)))) / (2.0 * image_total)
    weight = excess / (excess + spread)
    return (1.0 - weight)[:, None, None] * sample + (weight * level)[:, None, None] * ident

def wiener_filters(cov, gain, noise_level, steps_count):
    identity = jnp.eye(cov.shape[1], dtype=jnp.float32)[None]
    system = (gain * gain)[:, None, None] * cov + noise_level[:, None, None] * identity
    frobenius = jnp.sqrt(lax.optimization_barrier(jnp.sum(system * system, (1, 2))))
    approx = identity / frobenius[:, None, None]
    for sweep in range(steps_count):
        middle = jnp.matmul(approx, system, precision=lax.Precision.HIGHEST)
        approx = 2.0 * approx - jnp.matmul(middle, approx, precision=lax.Precision.HIGHEST)
    product = jnp.matmul(cov, approx, precision=lax.Precision.HIGHEST)
    return (gain[:, None, None] * product).astype(jnp.bfloat16)

def reference(images, group_ids, counts, radial_basis, ctf_gain, noise_var):
    forward, inverse = dft_tables(A, K)
    used = (jnp.arange(PMAX, dtype=jnp.int32)[None, :] < counts[:, None]).astype(jnp.float32)
    basis_used = (radial_basis.astype(jnp.float32) * used[:, None, :]).astype(jnp.bfloat16)
    spectrum = jnp.dot(images.reshape(IMAGES * R, A), forward, preferred_element_type=jnp.float32)
    spectrum = spectrum.astype(jnp.bfloat16).reshape(IMAGES, R, 2, K)
    coeffs = jnp.einsum('nrck,krp->kcnp', spectrum.astype(jnp.float32), basis_used.astype(jnp.float32)).astype(jnp.bfloat16)
    coeff_wide = coeffs.astype(jnp.float32)
    gains_kn = jnp.take(ctf_gain, group_ids, axis=0).T
    scaled = (coeff_wide * gains_kn[:, None, :, None]).astype(jnp.bfloat16).astype(jnp.float32)
    gram = jnp.einsum('kcnp,kcnq->kpq', scaled, scaled)
    norms = lax.optimization_barrier(jnp.sum(coeff_wide * coeff_wide, -1))
    squares = gains_kn * gains_kn
    fourth = lax.optimization_barrier(jnp.sum(squares[:, None, :] * norms * norms, (1, 2)))
    total = 2.0 * lax.optimization_barrier(jnp.sum(squares, 1))
    cov = shrink_cov(gram, fourth, total, used, IMAGES)
    cov_all = jnp.broadcast_to(cov[None], (G, K, PMAX, PMAX)).reshape(G * K, PMAX, PMAX)
    filters = wiener_filters(cov_all, ctf_gain.reshape(G * K), jnp.tile(noise_var, G), NS_ITERS)
    filters = filters.reshape(G, K, PMAX, PMAX).astype(jnp.float32)
    result = jnp.zeros((K, 2, IMAGES, PMAX), jnp.float32)
    for which_group in range(G):
        part = jnp.einsum('kcnq,kpq->kcnp', coeff_wide, filters[which_group])
        result = result + jnp.where((group_ids == which_group)[None, None, :, None], part, 0.0)
    cleaned = result.astype(jnp.bfloat16).astype(jnp.float32)
    back = jnp.einsum('kcnp,krp->nrck', cleaned, basis_used.astype(jnp.float32)).astype(jnp.bfloat16)
    back = back.reshape(IMAGES * R, 2 * K)
    denoised = jnp.dot(back, inverse, preferred_element_type=jnp.float32).astype(jnp.bfloat16)
    return denoised.reshape(IMAGES, R, A)
```

```python
import functools
import math

import jax
import jax.numpy as jnp
import numpy as np
from jax import lax
from jax.experimental import pallas as pl
from jax.experimental.pallas import tpu as pltpu
from jax.sharding import PartitionSpec as P

NS_ITERS = 7


def dft_tables(angles, freqs):
    angle_index = jnp.arange(angles, dtype=jnp.int32)
    freq_index = jnp.arange(freqs, dtype=jnp.int32)
    turns = angle_index[:, None] * freq_index[None, :] % angles
    phases = turns.astype(jnp.float32) * (2.0 * math.pi / angles)
    factor = 1.0 / math.sqrt(angles)
    cosine = jnp.cos(phases) * factor
    sine = -jnp.sin(phases) * factor
    forward = jnp.concatenate([cosine, sine], 1).astype(jnp.bfloat16)
    doubling = jnp.where(freq_index == 0, 1.0, 2.0).astype(jnp.float32)
    inverse = jnp.concatenate([cosine * doubling[None, :], sine * doubling[None, :]], 1).T.astype(
        jnp.bfloat16
    )
    return (forward, inverse)


def shrink_cov(gram, fourth, total, used, image_total):
    sample = gram / total[:, None, None]
    ident = used[:, :, None] * jnp.eye(used.shape[1], dtype=jnp.float32)[None]
    level = jnp.trace(sample, axis1=1, axis2=2) / jnp.sum(used, 1)
    spread = jnp.sum((sample - level[:, None, None] * ident) ** 2, (1, 2))
    excess = (fourth / total - jnp.sum(sample * sample, (1, 2))) / (2.0 * image_total)
    weight = excess / (excess + spread)
    return (1.0 - weight)[:, None, None] * sample + (weight * level)[:, None, None] * ident


def wiener_filters(cov, gain, noise_level, steps_count):
    identity = jnp.eye(cov.shape[1], dtype=jnp.float32)[None]
    system = (gain * gain)[:, None, None] * cov + noise_level[:, None, None] * identity
    frobenius = jnp.sqrt(jnp.sum(system * system, (1, 2)))
    approx = identity / frobenius[:, None, None]
    for sweep in range(steps_count):
        middle = jnp.matmul(approx, system, precision=lax.Precision.HIGHEST)
        approx = 2.0 * approx - jnp.matmul(middle, approx, precision=lax.Precision.HIGHEST)
    product = jnp.matmul(cov, approx, precision=lax.Precision.HIGHEST)
    return (gain[:, None, None] * product).astype(jnp.bfloat16)


def general_body(images, group_ids, counts, radial_basis, ctf_gain, noise_var):
    local_images = images.shape[0]
    radii = images.shape[1]
    angles = images.shape[2]
    freqs = radial_basis.shape[0]
    pmax = radial_basis.shape[2]
    groups_count = ctf_gain.shape[0]
    owners = lax.axis_size("img")
    owned = freqs // owners
    forward, inverse = dft_tables(angles, freqs)
    used = (jnp.arange(pmax, dtype=jnp.int32)[None, :] < counts[:, None]).astype(jnp.float32)
    basis_used = (radial_basis.astype(jnp.float32) * used[:, None, :]).astype(jnp.bfloat16)
    spectrum = jnp.dot(
        images.reshape(local_images * radii, angles), forward, preferred_element_type=jnp.float32
    )
    spectrum = spectrum.astype(jnp.bfloat16).reshape(local_images, radii, 2, freqs)
    coeffs = jnp.einsum(
        "nrck,krp->kcnp", spectrum, basis_used, preferred_element_type=jnp.float32
    ).astype(jnp.bfloat16)
    first = lax.axis_index("img") * owned
    arrived = lax.all_to_all(coeffs, "img", split_axis=0, concat_axis=2, tiled=True)
    all_ids = lax.all_gather(group_ids, "img", axis=0, tiled=True)
    gains_local = lax.dynamic_slice_in_dim(ctf_gain, first, owned, 1)
    noise_local = lax.dynamic_slice_in_dim(noise_var, first, owned, 0)
    used_local = lax.dynamic_slice_in_dim(used, first, owned, 0)
    onehot = (all_ids[:, None] == jnp.arange(groups_count, dtype=jnp.int32)[None, :]).astype(
        jnp.float32
    )
    gains_kn = jnp.dot(onehot, gains_local, precision=lax.Precision.HIGHEST).T
    scaled = (arrived * gains_kn[:, None, :, None]).astype(jnp.bfloat16)
    gram_part = jnp.einsum("kcnp,kcnq->kpq", scaled, scaled, preferred_element_type=jnp.float32)
    norms = jnp.einsum("kcnp,kcnp->kcn", arrived, arrived, preferred_element_type=jnp.float32)
    squares = gains_kn * gains_kn
    fourth_part = jnp.sum(squares[:, None, :] * norms * norms, (1, 2))
    total_part = 2.0 * jnp.sum(squares, 1)
    gram, fourth, total = lax.psum((gram_part, fourth_part, total_part), "grp")
    image_total = arrived.shape[2] * lax.axis_size("grp")
    cov = shrink_cov(gram, fourth, total, used_local, image_total)
    combos = groups_count * owned
    cov_all = jnp.broadcast_to(cov[None], (groups_count, owned, pmax, pmax)).reshape(
        combos, pmax, pmax
    )
    gain_all = gains_local.reshape(combos)
    noise_all = jnp.tile(noise_local, groups_count)
    share = combos // lax.axis_size("grp")
    start = lax.axis_index("grp") * share
    mine = wiener_filters(
        lax.dynamic_slice_in_dim(cov_all, start, share, 0),
        lax.dynamic_slice_in_dim(gain_all, start, share, 0),
        lax.dynamic_slice_in_dim(noise_all, start, share, 0),
        NS_ITERS,
    )
    filters = lax.all_gather(mine, "grp", axis=0, tiled=True)
    filters = filters.reshape(groups_count, owned, pmax, pmax)
    result = jnp.zeros(arrived.shape, jnp.float32)
    for which_group in range(groups_count):
        part = jnp.einsum(
            "kcnq,kpq->kcnp", arrived, filters[which_group], preferred_element_type=jnp.float32
        )
        result = result + jnp.where((all_ids == which_group)[None, None, :, None], part, 0.0)
    cleaned = result.astype(jnp.bfloat16)
    returned = lax.all_to_all(cleaned, "img", split_axis=2, concat_axis=0, tiled=True)
    back = jnp.einsum(
        "kcnp,krp->nrck", returned, basis_used, preferred_element_type=jnp.float32
    ).astype(jnp.bfloat16)
    back = back.reshape(local_images * radii, 2 * freqs)
    denoised = jnp.dot(back, inverse, preferred_element_type=jnp.float32).astype(jnp.bfloat16)
    return denoised.reshape(local_images, radii, angles)


RANKS = ((0, 4, 8, 15), (1, 5, 9, 14), (2, 6, 10, 13), (3, 7, 11, 12))
OWN = 4
BLOCK = 16
ROWS = 208
ID_ROW = ROWS - 1
VMEM_LIMIT = 48 * 1024 * 1024

f32 = jnp.float32
bf16 = jnp.bfloat16


def fixed_tables(angles, freqs):
    turns = np.arange(angles)[:, None] * np.arange(freqs)[None, :] % angles
    phases = turns * (2.0 * math.pi / angles)
    cosine = np.cos(phases) / math.sqrt(angles)
    sine = -np.sin(phases) / math.sqrt(angles)
    forward = np.concatenate([cosine, sine], 1)
    doubling = np.where(np.arange(freqs) == 0, 1.0, 2.0)[None, :]
    inverse = np.concatenate([cosine * doubling, sine * doubling], 1).T
    return forward.T.astype(np.float32).astype(jnp.bfloat16), inverse.astype(np.float32).astype(jnp.bfloat16)


def owner_tables(counts):
    blocks = counts.reshape(-1, BLOCK)
    index = jnp.arange(BLOCK, dtype=jnp.int32)
    mine, other = blocks[:, :, None], blocks[:, None, :]
    before = (other > mine) | ((other == mine) & (index[None, None, :] < index[None, :, None]))
    rank = jnp.sum(before.astype(jnp.int32), 2)
    wanted = jnp.array(RANKS, jnp.int32).reshape(BLOCK)
    hit = (rank[:, None, :] == wanted[None, :, None]).astype(jnp.int32)
    first = (jnp.arange(blocks.shape[0], dtype=jnp.int32) * BLOCK)[:, None, None]
    freq = jnp.sum(hit * (index[None, None, :] + first), 2)
    count = jnp.sum(hit * blocks[:, None, :], 2)
    rows = ((count + 1) // 2).reshape(-1, OWN)
    earlier = jnp.array(np.tril(np.ones((OWN, OWN), np.int32), -1))
    offset = jnp.sum(rows[:, None, :] * earlier[None], 2)
    return jnp.concatenate([freq.reshape(-1), count.reshape(-1), offset.reshape(-1)])


def low_half(shape):
    return lax.broadcasted_iota(jnp.int32, shape, 1) < 64


def swap_halves(value):
    return pltpu.roll(value, 64, 1)


def front_kernel(freqs, image_steps, tab, images, forward, basis, ids, out, spec, turned, rows):
    step = pl.program_id(0)
    per_step = images.shape[0]
    wide = 2 * freqs
    local = spec.shape[0] // wide

    @pl.when(step < image_steps)
    def _():
        for pair in range(per_step // 2):
            both = images[2 * pair:2 * pair + 2].reshape(256, images.shape[2])
            part = lax.dot_general(forward[...], both, (((1,), (1,)), ((), ())), preferred_element_type=f32)
            part = part.astype(bf16).astype(f32)
            for which in range(2):
                start = pl.multiple_of((step * per_step + 2 * pair + which) * wide, wide)
                spec[pl.ds(start, wide), :] = part[:, 128 * which:128 * (which + 1)]

    @pl.when(step >= image_steps)
    def _():
        block = step - image_steps
        low = low_half((64, 128))
        for dest in range(OWN):
            for pair in range(2):
                parts = []
                for which in range(2):
                    freq = tab[(block * OWN + dest) * OWN + 2 * pair + which]
                    real = spec[pl.ds(freq, local, stride=wide), :]
                    imag = spec[pl.ds(freq + freqs, local, stride=wide), :]
                    lhs = jnp.concatenate([real, imag], 0).astype(bf16)
                    value = jnp.dot(lhs, basis[freq - block * BLOCK], preferred_element_type=f32)
                    parts.append(value.astype(bf16).astype(f32))
                slot = dest * 2 + pair
                turned[slot] = jnp.concatenate(parts, 0).T
                even = turned[slot, pl.ds(0, 64, stride=2), :]
                odd = turned[slot, pl.ds(1, 64, stride=2), :]
                for which in range(2):
                    where = tab[2 * freqs + (block * OWN + dest) * OWN + 2 * pair + which]
                    if which == 0:
                        value = jnp.where(low, even, swap_halves(odd))
                    else:
                        value = jnp.where(low, swap_halves(even), odd)
                    rows[dest, pl.ds(where, 64), :] = value
            rows[dest, pl.ds(ID_ROW, 1), :] = ids[...]
            out[dest] = rows[dest, 0:ROWS, :].astype(bf16)


def split(value):
    high = value.astype(bf16)
    return high, (value - high.astype(f32)).astype(bf16)


def block_diagonal(pair):
    zero = jnp.zeros((128, 128), pair.dtype)
    top = jnp.concatenate([pair[:, :128], zero], 1)
    bottom = jnp.concatenate([zero, pair[:, 128:]], 1)
    return jnp.concatenate([top, bottom], 0)


def three_pass(high, low, right_high, right_low):
    rows = high.shape[0]
    first = jnp.dot(jnp.concatenate([high, low], 0), right_high, preferred_element_type=f32)
    return first[:rows] + first[rows:] + jnp.dot(high, right_low, preferred_element_type=f32)


def total_of(value):
    return jnp.sum(jnp.sum(value, 1, keepdims=True), 0, keepdims=True)


def middle_kernel(freqs, image_total, me, tab, gain, noise, arrived, out, wide, coeff, clean, filters):
    devices = arrived.shape[0]
    groups_count = gain.shape[0]
    columns = devices * 64
    low = low_half((64, 128))
    wide[:, 0:ROWS, :] = arrived[...].astype(f32)
    pieces = [
        jnp.where(low_half((1, 128)), wide[2 * m, pl.ds(ID_ROW, 1), :], wide[2 * m + 1, pl.ds(ID_ROW, 1), :])
        for m in range(devices // 2)
    ]
    ids = jnp.concatenate(pieces, 1)
    row = lax.broadcasted_iota(jnp.int32, (128, 128), 0)
    column = lax.broadcasted_iota(jnp.int32, (128, 128), 1)
    slot_row = jnp.where(row < 64, 2 * row, 2 * row - 127)
    eye = (row == column).astype(f32)

    def each(own, carry):
        place = me[0] * OWN + own
        freq = tab[place]
        count = tab[freqs + place]
        where = tab[2 * freqs + place]
        used = slot_row < count
        for m in range(devices // 2):
            first = wide[2 * m, pl.ds(where, 64), :]
            second = wide[2 * m + 1, pl.ds(where, 64), :]
            even = jnp.where(low, first, swap_halves(second))
            odd = jnp.where(low, swap_halves(first), second)
            both = jnp.where(used, jnp.concatenate([even, odd], 0), 0.0)
            coeff[:, 128 * m:128 * (m + 1)] = both
        value = coeff[...]
        scale = jnp.zeros((1, columns), f32)
        for g in range(groups_count):
            scale = jnp.where(ids == float(g), gain[g, freq], scale)
        squares = scale * scale
        norms = jnp.sum(value * value, 0, keepdims=True)
        fourth = jnp.sum(squares * norms * norms, 1, keepdims=True)
        total = jnp.sum(squares, 1, keepdims=True)
        scaled = (value * scale).astype(bf16)
        gram = lax.dot_general(scaled, scaled, (((1,), (1,)), ((), ())), preferred_element_type=f32)
        sample = gram / total
        ident = jnp.where(used, eye, 0.0)
        level = total_of(sample * eye) / count.astype(f32)
        spread = total_of((sample - level * ident) ** 2)
        excess = (fourth / total - total_of(sample * sample)) / (2.0 * image_total)
        weight = excess / (excess + spread)
        cov = (1.0 - weight) * sample + (weight * level) * ident

        cov_high, cov_low = split(cov)
        pairs = groups_count // 2
        power, series, norm = [], [], []
        for pair in range(pairs):
            start, size = [], []
            for g in (2 * pair, 2 * pair + 1):
                system = (gain[g, freq] * gain[g, freq]) * cov + noise[freq] * eye
                size.append(jnp.sqrt(total_of(system * system)))
                start.append(eye - system / size[-1])
            power.append(jnp.concatenate(start, 1))
            norm.append(size)
            series.append(jnp.concatenate([eye, eye], 1) + power[-1])
        for sweep in range(NS_ITERS):
            for pair in range(pairs):
                high, less = split(power[pair])
                right_high, right_low = block_diagonal(high), block_diagonal(less)
                if sweep == 0:
                    power[pair] = three_pass(high, less, right_high, right_low)
                    continue
                sum_high, sum_less = split(series[pair])
                if sweep == NS_ITERS - 1:
                    series[pair] = series[pair] + three_pass(sum_high, sum_less, right_high, right_low)
                    continue
                both = three_pass(
                    jnp.concatenate([high, sum_high], 0), jnp.concatenate([less, sum_less], 0), right_high, right_low
                )
                power[pair] = both[:128]
                series[pair] = series[pair] + both[128:]
        for pair in range(pairs):
            right_high, right_low = split(series[pair])
            product = three_pass(cov_high, cov_low, right_high, right_low)
            for side in range(2):
                g = 2 * pair + side
                piece = product[:, 128 * side:128 * (side + 1)] * (gain[g, freq] / norm[pair][side])
                filters[128 * g:128 * (g + 1), :] = piece.astype(bf16)
        for chunk in range(columns // 256):
            span = slice(256 * chunk, 256 * (chunk + 1))
            every = jnp.dot(filters[...], coeff[:, span].astype(bf16), preferred_element_type=f32)
            chosen = every[:128]
            for g in range(1, groups_count):
                chosen = jnp.where(ids[:, span] == float(g), every[128 * g:128 * (g + 1)], chosen)
            for m in range(2):
                even = chosen[:64, 128 * m:128 * (m + 1)]
                odd = chosen[64:, 128 * m:128 * (m + 1)]
                clean[4 * chunk + 2 * m, pl.ds(where, 64), :] = jnp.where(low, even, swap_halves(odd))
                clean[4 * chunk + 2 * m + 1, pl.ds(where, 64), :] = jnp.where(low, swap_halves(even), odd)
        return carry

    lax.fori_loop(0, OWN, each, 0)
    out[...] = clean[:, 0:ROWS, :].astype(bf16)


def back_kernel(freqs, block_steps, tab, returned, basis, inverse, out, rows, turned, back):
    step = pl.program_id(0)
    wide = 2 * freqs
    local = back.shape[0] // wide

    @pl.when(step < block_steps)
    def _():
        low = low_half((64, 128))
        pair_row = lax.broadcasted_iota(jnp.int32, (64, 128), 0) * 2
        for dest in range(OWN):
            rows[dest, 0:ROWS, :] = returned[dest].astype(f32)
            for pair in range(2):
                place = (step * OWN + dest) * OWN + 2 * pair
                first = rows[dest, pl.ds(tab[2 * freqs + place], 64), :]
                second = rows[dest, pl.ds(tab[2 * freqs + place + 1], 64), :]
                count = jnp.where(low, tab[freqs + place], tab[freqs + place + 1])
                even = jnp.where(low, first, swap_halves(second))
                odd = jnp.where(low, swap_halves(first), second)
                slot = dest * 2 + pair
                turned[slot, pl.ds(0, 64, stride=2), :] = jnp.where(pair_row < count, even, 0.0)
                turned[slot, pl.ds(1, 64, stride=2), :] = jnp.where(pair_row + 1 < count, odd, 0.0)
                lhs = turned[slot].T.astype(bf16)
                for which in range(2):
                    freq = tab[place + which]
                    value = lax.dot_general(
                        lhs[64 * which:64 * (which + 1)], basis[freq - step * BLOCK],
                        (((1,), (1,)), ((), ())), preferred_element_type=f32,
                    )
                    value = value.astype(bf16).astype(f32)
                    back[pl.ds(freq, local, stride=wide), :] = value[:local]
                    back[pl.ds(freq + freqs, local, stride=wide), :] = value[local:]

    @pl.when(step >= block_steps)
    def _():
        per_step = out.shape[0]
        for image in range(per_step):
            start = pl.multiple_of(((step - block_steps) * per_step + image) * wide, wide)
            lhs = back[pl.ds(start, wide), :].astype(bf16)
            value = lax.dot_general(lhs, inverse[...], (((0,), (0,)), ((), ())), preferred_element_type=f32)
            out[image] = value.astype(bf16)


def owned_body(images, group_ids, counts, radial_basis, ctf_gain, noise_var):
    axes = ("img", "grp")
    local, radii, angles = images.shape
    freqs, _, pmax = radial_basis.shape
    devices = lax.axis_size(axes)
    blocks = freqs // BLOCK
    image_total = local * devices
    forward, inverse = fixed_tables(angles, freqs)
    tab = owner_tables(counts)
    per_step = 4
    image_steps = local // per_step
    id_row = jnp.tile(group_ids.astype(f32), 128 // local)[None, :]
    packed = pl.pallas_call(
        functools.partial(front_kernel, freqs, image_steps),
        grid=(image_steps + blocks,),
        in_specs=[
            pl.BlockSpec(memory_space=pltpu.SMEM),
            pl.BlockSpec((per_step, radii, angles), lambda i: (jnp.minimum(i, image_steps - 1), 0, 0)),
            pl.BlockSpec((2 * freqs, angles), lambda i: (0, 0)),
            pl.BlockSpec((BLOCK, radii, pmax), lambda i: (jnp.maximum(i - image_steps, 0), 0, 0)),
            pl.BlockSpec((1, 128), lambda i: (0, 0)),
        ],
        out_specs=pl.BlockSpec((OWN, ROWS, 128), lambda i: (jnp.maximum(i - image_steps, 0), 0, 0)),
        out_shape=jax.ShapeDtypeStruct((devices, ROWS, 128), bf16),
        scratch_shapes=[
            pltpu.VMEM((local * 2 * freqs, 128), f32),
            pltpu.VMEM((2 * OWN, 128, 128), f32),
            pltpu.VMEM((OWN, ROWS + 64, 128), f32),
        ],
        compiler_params=pltpu.CompilerParams(vmem_limit_bytes=VMEM_LIMIT),
        name="front",
    )(tab, images, jnp.asarray(forward), radial_basis, id_row)
    arrived = lax.all_to_all(packed, axes, split_axis=0, concat_axis=0, tiled=True)
    me = lax.axis_index(axes).astype(jnp.int32).reshape(1)
    smem = pl.BlockSpec(memory_space=pltpu.SMEM)
    vmem = pl.BlockSpec(memory_space=pltpu.VMEM)
    cleaned = pl.pallas_call(
        functools.partial(middle_kernel, freqs, float(image_total)),
        in_specs=[smem, smem, smem, smem, vmem],
        out_specs=vmem,
        out_shape=jax.ShapeDtypeStruct((devices, ROWS, 128), bf16),
        scratch_shapes=[
            pltpu.VMEM((devices, ROWS + 64, 128), f32),
            pltpu.VMEM((128, devices * 64), f32),
            pltpu.VMEM((devices, ROWS + 64, 128), f32),
            pltpu.VMEM((ctf_gain.shape[0] * 128, 128), bf16),
        ],
        compiler_params=pltpu.CompilerParams(vmem_limit_bytes=VMEM_LIMIT),
        name="middle",
    )(me, tab, ctf_gain, noise_var, arrived)
    returned = lax.all_to_all(cleaned, axes, split_axis=0, concat_axis=0, tiled=True)
    return pl.pallas_call(
        functools.partial(back_kernel, freqs, blocks),
        grid=(blocks + image_steps,),
        in_specs=[
            smem,
            pl.BlockSpec((OWN, ROWS, 128), lambda i: (jnp.minimum(i, blocks - 1), 0, 0)),
            pl.BlockSpec((BLOCK, radii, pmax), lambda i: (jnp.minimum(i, blocks - 1), 0, 0)),
            pl.BlockSpec((2 * freqs, angles), lambda i: (0, 0)),
        ],
        out_specs=pl.BlockSpec((per_step, radii, angles), lambda i: (jnp.maximum(i - blocks, 0), 0, 0)),
        out_shape=jax.ShapeDtypeStruct(images.shape, bf16),
        scratch_shapes=[
            pltpu.VMEM((OWN, ROWS + 64, 128), f32),
            pltpu.VMEM((2 * OWN, 128, 128), f32),
            pltpu.VMEM((local * 2 * freqs, 128), f32),
        ],
        compiler_params=pltpu.CompilerParams(vmem_limit_bytes=VMEM_LIMIT),
        name="back",
    )(tab, returned, radial_basis, jnp.asarray(inverse))


def body(images, group_ids, counts, radial_basis, ctf_gain, noise_var):
    devices = lax.axis_size("img") * lax.axis_size("grp")
    freqs = radial_basis.shape[0]
    fits = (
        freqs == OWN * devices
        and lax.axis_size("grp") * OWN == BLOCK
        and images.shape[0] == 32
        and radial_basis.shape[1:] == (128, 128)
        and freqs % 128 == 0
        and images.shape[2] % 128 == 0
        and ctf_gain.shape[0] % 2 == 0
    )
    chosen = owned_body if fits else general_body
    return chosen(images, group_ids, counts, radial_basis, ctf_gain, noise_var)


def solution(mesh):
    placed = (P(("img", "grp"), None, None), P(("img", "grp")), P(), P(), P(), P())
    return jax.shard_map(
        body, mesh=mesh, in_specs=placed, out_specs=P(("img", "grp"), None, None), check_vma=False
    )
```

```python
import functools
import math

import jax
import jax.numpy as jnp
import numpy as np
from jax import lax
from jax.experimental import pallas as pl
from jax.experimental.pallas import tpu as pltpu
from jax.sharding import PartitionSpec as P

NS_ITERS = 7


def dft_tables(angles, freqs):
    angle_index = jnp.arange(angles, dtype=jnp.int32)
    freq_index = jnp.arange(freqs, dtype=jnp.int32)
    turns = angle_index[:, None] * freq_index[None, :] % angles
    phases = turns.astype(jnp.float32) * (2.0 * math.pi / angles)
    factor = 1.0 / math.sqrt(angles)
    cosine = jnp.cos(phases) * factor
    sine = -jnp.sin(phases) * factor
    forward = jnp.concatenate([cosine, sine], 1).astype(jnp.bfloat16)
    doubling = jnp.where(freq_index == 0, 1.0, 2.0).astype(jnp.float32)
    inverse = jnp.concatenate([cosine * doubling[None, :], sine * doubling[None, :]], 1).T.astype(
        jnp.bfloat16
    )
    return (forward, inverse)


def shrink_cov(gram, fourth, total, used, image_total):
    sample = gram / total[:, None, None]
    ident = used[:, :, None] * jnp.eye(used.shape[1], dtype=jnp.float32)[None]
    level = jnp.trace(sample, axis1=1, axis2=2) / jnp.sum(used, 1)
    spread = jnp.sum((sample - level[:, None, None] * ident) ** 2, (1, 2))
    excess = (fourth / total - jnp.sum(sample * sample, (1, 2))) / (2.0 * image_total)
    weight = excess / (excess + spread)
    return (1.0 - weight)[:, None, None] * sample + (weight * level)[:, None, None] * ident


def wiener_filters(cov, gain, noise_level, steps_count):
    identity = jnp.eye(cov.shape[1], dtype=jnp.float32)[None]
    system = (gain * gain)[:, None, None] * cov + noise_level[:, None, None] * identity
    frobenius = jnp.sqrt(jnp.sum(system * system, (1, 2)))
    approx = identity / frobenius[:, None, None]
    for sweep in range(steps_count):
        middle = jnp.matmul(approx, system, precision=lax.Precision.HIGHEST)
        approx = 2.0 * approx - jnp.matmul(middle, approx, precision=lax.Precision.HIGHEST)
    product = jnp.matmul(cov, approx, precision=lax.Precision.HIGHEST)
    return (gain[:, None, None] * product).astype(jnp.bfloat16)


def general_body(images, group_ids, counts, radial_basis, ctf_gain, noise_var):
    local_images = images.shape[0]
    radii = images.shape[1]
    angles = images.shape[2]
    freqs = radial_basis.shape[0]
    pmax = radial_basis.shape[2]
    groups_count = ctf_gain.shape[0]
    owners = lax.axis_size("img")
    owned = freqs // owners
    forward, inverse = dft_tables(angles, freqs)
    used = (jnp.arange(pmax, dtype=jnp.int32)[None, :] < counts[:, None]).astype(jnp.float32)
    basis_used = (radial_basis.astype(jnp.float32) * used[:, None, :]).astype(jnp.bfloat16)
    spectrum = jnp.dot(
        images.reshape(local_images * radii, angles), forward, preferred_element_type=jnp.float32
    )
    spectrum = spectrum.astype(jnp.bfloat16).reshape(local_images, radii, 2, freqs)
    coeffs = jnp.einsum(
        "nrck,krp->kcnp", spectrum, basis_used, preferred_element_type=jnp.float32
    ).astype(jnp.bfloat16)
    first = lax.axis_index("img") * owned
    arrived = lax.all_to_all(coeffs, "img", split_axis=0, concat_axis=2, tiled=True)
    all_ids = lax.all_gather(group_ids, "img", axis=0, tiled=True)
    gains_local = lax.dynamic_slice_in_dim(ctf_gain, first, owned, 1)
    noise_local = lax.dynamic_slice_in_dim(noise_var, first, owned, 0)
    used_local = lax.dynamic_slice_in_dim(used, first, owned, 0)
    onehot = (all_ids[:, None] == jnp.arange(groups_count, dtype=jnp.int32)[None, :]).astype(
        jnp.float32
    )
    gains_kn = jnp.dot(onehot, gains_local, precision=lax.Precision.HIGHEST).T
    scaled = (arrived * gains_kn[:, None, :, None]).astype(jnp.bfloat16)
    gram_part = jnp.einsum("kcnp,kcnq->kpq", scaled, scaled, preferred_element_type=jnp.float32)
    norms = jnp.einsum("kcnp,kcnp->kcn", arrived, arrived, preferred_element_type=jnp.float32)
    squares = gains_kn * gains_kn
    fourth_part = jnp.sum(squares[:, None, :] * norms * norms, (1, 2))
    total_part = 2.0 * jnp.sum(squares, 1)
    gram, fourth, total = lax.psum((gram_part, fourth_part, total_part), "grp")
    image_total = arrived.shape[2] * lax.axis_size("grp")
    cov = shrink_cov(gram, fourth, total, used_local, image_total)
    combos = groups_count * owned
    cov_all = jnp.broadcast_to(cov[None], (groups_count, owned, pmax, pmax)).reshape(
        combos, pmax, pmax
    )
    gain_all = gains_local.reshape(combos)
    noise_all = jnp.tile(noise_local, groups_count)
    share = combos // lax.axis_size("grp")
    start = lax.axis_index("grp") * share
    mine = wiener_filters(
        lax.dynamic_slice_in_dim(cov_all, start, share, 0),
        lax.dynamic_slice_in_dim(gain_all, start, share, 0),
        lax.dynamic_slice_in_dim(noise_all, start, share, 0),
        NS_ITERS,
    )
    filters = lax.all_gather(mine, "grp", axis=0, tiled=True)
    filters = filters.reshape(groups_count, owned, pmax, pmax)
    result = jnp.zeros(arrived.shape, jnp.float32)
    for which_group in range(groups_count):
        part = jnp.einsum(
            "kcnq,kpq->kcnp", arrived, filters[which_group], preferred_element_type=jnp.float32
        )
        result = result + jnp.where((all_ids == which_group)[None, None, :, None], part, 0.0)
    cleaned = result.astype(jnp.bfloat16)
    returned = lax.all_to_all(cleaned, "img", split_axis=2, concat_axis=0, tiled=True)
    back = jnp.einsum(
        "kcnp,krp->nrck", returned, basis_used, preferred_element_type=jnp.float32
    ).astype(jnp.bfloat16)
    back = back.reshape(local_images * radii, 2 * freqs)
    denoised = jnp.dot(back, inverse, preferred_element_type=jnp.float32).astype(jnp.bfloat16)
    return denoised.reshape(local_images, radii, angles)


RANKS = ((0, 4, 8, 15), (1, 5, 9, 14), (2, 6, 10, 13), (3, 7, 11, 12))
OWN = 4
BLOCK = 16
ROWS = 208
ID_ROW = ROWS - 1
IMAGE_CHUNKS = 8
PITCH_PAD = 8
VMEM_LIMIT = 48 * 1024 * 1024
FRONT_VMEM = 121 * 512 * 1024

f32 = jnp.float32
bf16 = jnp.bfloat16


def fixed_tables(angles, freqs):
    turns = np.arange(angles)[:, None] * np.arange(freqs)[None, :] % angles
    phases = turns * (2.0 * math.pi / angles)
    cosine = np.cos(phases) / math.sqrt(angles)
    sine = -np.sin(phases) / math.sqrt(angles)
    forward = np.concatenate([cosine, sine], 1)
    doubling = np.where(np.arange(freqs) == 0, 1.0, 2.0)[None, :]
    inverse = np.concatenate([cosine * doubling, sine * doubling], 1).T
    return forward.T.astype(np.float32).astype(jnp.bfloat16), inverse.astype(np.float32).astype(jnp.bfloat16)


def owner_tables(row_of_counts, blocks):
    every = jnp.broadcast_to(row_of_counts, (blocks, row_of_counts.shape[1]))
    block = lax.broadcasted_iota(jnp.int32, every.shape, 0)
    counts = every
    for which in range(1, blocks):
        counts = jnp.where(block == which, pltpu.roll(every, every.shape[1] - BLOCK * which, 1), counts)
    counts = counts[:, :BLOCK]
    lane = lax.broadcasted_iota(jnp.int32, counts.shape, 1)
    rank = jnp.zeros(counts.shape, jnp.int32)
    for other in range(BLOCK):
        column = counts[:, other:other + 1]
        before = (column > counts) | ((column == counts) & (lane > other))
        rank = rank + before.astype(jnp.int32)
    full = lax.broadcasted_iota(jnp.int32, (counts.shape[0], 128), 1)
    first = lax.broadcasted_iota(jnp.int32, (counts.shape[0], 1), 0) * BLOCK
    table = jnp.zeros(full.shape, jnp.int32)
    for dest in range(OWN):
        offset = jnp.zeros((counts.shape[0], 1), jnp.int32)
        for own in range(OWN):
            place = dest * OWN + own
            hit = rank == RANKS[dest][own]
            freq = jnp.sum(jnp.where(hit, lane, 0).astype(f32), 1, keepdims=True).astype(jnp.int32) + first
            count = jnp.sum(jnp.where(hit, counts, 0).astype(f32), 1, keepdims=True).astype(jnp.int32)
            table = jnp.where(full == place, freq, table)
            table = jnp.where(full == place + BLOCK, count, table)
            table = jnp.where(full == place + 2 * BLOCK, offset, table)
            offset = offset + (count + 1) // 2
    return table


def low_half(shape):
    return lax.broadcasted_iota(jnp.int32, shape, 1) < 64


def swap_halves(value):
    return pltpu.roll(value, 64, 1)


def front_kernel(freqs, counts, ids, images_any, forward_any, basis_any, packed, tab,
                 images, forward, basis, spec, turned, rows, table, image_sems, sems, basis_sems):
    wide = 2 * freqs
    pitch = wide + PITCH_PAD
    local = images.shape[0]
    blocks = freqs // BLOCK
    per_chunk = local // IMAGE_CHUNKS

    def image_copy(chunk):
        span = pl.ds(chunk * per_chunk, per_chunk)
        return pltpu.make_async_copy(images_any.at[span], images.at[span], image_sems.at[chunk])

    def basis_copy(block):
        span = pl.ds(block * BLOCK, BLOCK)
        return pltpu.make_async_copy(basis_any.at[span], basis.at[span], basis_sems.at[block])

    forward_copy = pltpu.make_async_copy(forward_any, forward, sems.at[0])
    table_copy = pltpu.make_async_copy(table, tab, sems.at[1])
    forward_copy.start()
    for chunk in range(IMAGE_CHUNKS):
        image_copy(chunk).start()
    table[...] = owner_tables(counts[...], blocks)
    table_copy.start()
    id_row = jnp.concatenate([ids[...].astype(f32)] * (128 // local), 1)
    forward_copy.wait()

    def transform(chunk, carry):
        image_copy(chunk).wait()
        basis_copy(chunk).start()
        for pair in range(per_chunk // 2):
            first = chunk * per_chunk + 2 * pair
            both = images[pl.ds(first, 2)].reshape(256, images.shape[2])
            part = lax.dot_general(forward[...], both, (((1,), (1,)), ((), ())), preferred_element_type=f32)
            part = part.astype(bf16).astype(f32)
            for which in range(2):
                start = pl.multiple_of((first + which) * pitch, 8)
                spec[pl.ds(start, wide), :] = part[:, 128 * which:128 * (which + 1)]
        return carry

    lax.fori_loop(0, IMAGE_CHUNKS, transform, 0)
    table_copy.wait()
    low = low_half((64, 128))

    def pack(block, carry):
        basis_copy(block).wait()
        for dest in range(OWN):
            for pair in range(2):
                place = dest * OWN + 2 * pair
                parts = []
                for which in range(2):
                    freq = tab[block, place + which]
                    real = spec[pl.ds(freq, local, stride=pitch), :]
                    imag = spec[pl.ds(freq + freqs, local, stride=pitch), :]
                    lhs = jnp.concatenate([real, imag], 0).astype(bf16)
                    parts.append(jnp.dot(lhs, basis[freq], preferred_element_type=f32).astype(bf16))
                slot = dest * 2 + pair
                turned[slot] = jnp.concatenate(parts, 0).T.astype(f32)
                even = turned[slot, pl.ds(0, 64, stride=2), :]
                odd = turned[slot, pl.ds(1, 64, stride=2), :]
                rows[dest, pl.ds(tab[block, place + 2 * BLOCK], 64), :] = jnp.where(low, even, swap_halves(odd))
                rows[dest, pl.ds(tab[block, place + 1 + 2 * BLOCK], 64), :] = jnp.where(low, swap_halves(even), odd)
            rows[dest, pl.ds(ID_ROW, 1), :] = id_row
            packed[block * OWN + dest] = rows[dest, 0:ROWS, :].astype(bf16)
        return carry

    lax.fori_loop(0, blocks, pack, 0)


def split(value):
    high = value.astype(bf16)
    return high, (value - high.astype(f32)).astype(bf16)


def side_by_side(value):
    high, low = split(value)
    return jnp.concatenate([high, low], 1)


def wide_product(left, right):
    both = jnp.dot(left, jnp.concatenate([right, right], 0), preferred_element_type=f32)
    return both[:, :128] + both[:, 128:]


def total_of(value):
    return jnp.sum(jnp.sum(value, 1, keepdims=True), 0, keepdims=True)


def middle_kernel(image_total, me, tab, gain, noise, arrived, out, wide, coeff, scaled, covs, filters, clean):
    devices = arrived.shape[0]
    groups_count = gain.shape[0]
    columns = devices * 64
    low = low_half((64, 128))
    block = me[0] // OWN
    first_place = lax.rem(me[0], OWN) * OWN
    wide[:, 0:ROWS, :] = arrived[...].astype(f32)
    pieces = [
        jnp.where(low_half((1, 128)), wide[2 * m, pl.ds(ID_ROW, 1), :], wide[2 * m + 1, pl.ds(ID_ROW, 1), :])
        for m in range(devices // 2)
    ]
    ids = jnp.concatenate(pieces, 1)
    row = lax.broadcasted_iota(jnp.int32, (128, 128), 0)
    column = lax.broadcasted_iota(jnp.int32, (128, 128), 1)
    slot_row = jnp.where(row < 64, 2 * row, 2 * row - 127)
    eye = (row == column).astype(f32)

    for own in range(OWN):
        place = first_place + own
        freq = tab[block, place]
        count = tab[block, place + BLOCK]
        where = tab[block, place + 2 * BLOCK]
        used = slot_row < count
        scale = jnp.zeros((1, columns), f32)
        for g in range(groups_count):
            scale = jnp.where(ids == float(g), gain[g, freq], scale)
        squares = scale * scale
        norms = []
        for m in range(devices // 2):
            span = slice(128 * m, 128 * (m + 1))
            first = wide[2 * m, pl.ds(where, 64), :]
            second = wide[2 * m + 1, pl.ds(where, 64), :]
            even = jnp.where(low, first, swap_halves(second))
            odd = jnp.where(low, swap_halves(first), second)
            value = jnp.where(used, jnp.concatenate([even, odd], 0), 0.0)
            coeff[own, :, span] = value.astype(bf16)
            scaled[own, :, span] = (value * scale[:, span]).astype(bf16)
            norms.append(jnp.sum(value * value, 0, keepdims=True))
        norms = jnp.concatenate(norms, 1)
        fourth = jnp.sum(squares * norms * norms, 1, keepdims=True)
        total = jnp.sum(squares, 1, keepdims=True)
        weighted = scaled[own]
        gram = lax.dot_general(weighted, weighted, (((1,), (1,)), ((), ())), preferred_element_type=f32)
        sample = gram / total
        ident = jnp.where(used, eye, 0.0)
        level = total_of(sample * eye) / count.astype(f32)
        spread = total_of((sample - level * ident) ** 2)
        excess = (fourth / total - total_of(sample * sample)) / (2.0 * image_total)
        weight = excess / (excess + spread)
        covs[own] = (1.0 - weight) * sample + (weight * level) * ident

    def invert(own, carry):
        place = first_place + own
        freq = tab[block, place]
        cov = covs[own]
        cov_parts = side_by_side(cov)
        power, series, size = [], [], []
        for g in range(groups_count):
            system = (gain[g, freq] * gain[g, freq]) * cov + noise[freq] * eye
            size.append(jnp.sqrt(total_of(system * system)))
            power.append(eye - system / size[g])
            series.append(eye + power[g])
        for sweep in range(NS_ITERS):
            for g in range(groups_count):
                right = side_by_side(power[g])
                if sweep == 0:
                    power[g] = wide_product(right, right)
                elif sweep == NS_ITERS - 1:
                    series[g] = series[g] + wide_product(side_by_side(series[g]), right)
                else:
                    both = wide_product(jnp.concatenate([right, side_by_side(series[g])], 0), right)
                    power[g] = both[:128]
                    series[g] = series[g] + both[128:]
        for g in range(groups_count):
            product = wide_product(cov_parts, side_by_side(series[g])) * (gain[g, freq] / size[g])
            filters[own, :, 128 * g:128 * (g + 1)] = product.astype(bf16)
        return carry

    lax.fori_loop(0, OWN, invert, 0)

    def apply(own, carry):
        where = tab[block, first_place + own + 2 * BLOCK]
        for chunk in range(columns // 256):
            span = slice(256 * chunk, 256 * (chunk + 1))
            value = coeff[own, :, span]
            masked = jnp.concatenate(
                [jnp.where(ids[:, span] == float(g), value, jnp.zeros_like(value)) for g in range(groups_count)], 0
            )
            chosen = jnp.dot(filters[own], masked, preferred_element_type=f32)
            for m in range(2):
                even = chosen[:64, 128 * m:128 * (m + 1)]
                odd = chosen[64:, 128 * m:128 * (m + 1)]
                clean[4 * chunk + 2 * m, pl.ds(where, 64), :] = jnp.where(low, even, swap_halves(odd))
                clean[4 * chunk + 2 * m + 1, pl.ds(where, 64), :] = jnp.where(low, swap_halves(even), odd)
        return carry

    lax.fori_loop(0, OWN, apply, 0)
    out[...] = clean[:, 0:ROWS, :].astype(bf16)


def back_kernel(freqs, tab, returned, basis, inverse, out_any, rows, turned, back, images, sems):
    wide = 2 * freqs
    pitch = wide + PITCH_PAD
    local = images.shape[0]
    blocks = freqs // BLOCK
    per_chunk = local // IMAGE_CHUNKS
    low = low_half((64, 128))
    pair_row = lax.broadcasted_iota(jnp.int32, (64, 128), 0) * 2

    def unpack(block, carry):
        for dest in range(OWN):
            rows[dest, 0:ROWS, :] = returned[block * OWN + dest].astype(f32)
            for pair in range(2):
                place = dest * OWN + 2 * pair
                first = rows[dest, pl.ds(tab[block, place + 2 * BLOCK], 64), :]
                second = rows[dest, pl.ds(tab[block, place + 1 + 2 * BLOCK], 64), :]
                count = jnp.where(low, tab[block, place + BLOCK], tab[block, place + 1 + BLOCK])
                even = jnp.where(low, first, swap_halves(second))
                odd = jnp.where(low, swap_halves(first), second)
                slot = dest * 2 + pair
                turned[slot, pl.ds(0, 64, stride=2), :] = jnp.where(pair_row < count, even, 0.0)
                turned[slot, pl.ds(1, 64, stride=2), :] = jnp.where(pair_row + 1 < count, odd, 0.0)
                lhs = turned[slot].astype(bf16).T
                for which in range(2):
                    freq = tab[block, place + which]
                    value = jnp.dot(lhs[64 * which:64 * (which + 1)], basis[freq], preferred_element_type=f32)
                    value = value.astype(bf16).astype(f32)
                    back[pl.ds(freq, local, stride=pitch), :] = value[:local]
                    back[pl.ds(freq + freqs, local, stride=pitch), :] = value[local:]
        return carry

    lax.fori_loop(0, blocks, unpack, 0)

    def out_copy(chunk):
        span = pl.ds(chunk * per_chunk, per_chunk)
        return pltpu.make_async_copy(images.at[span], out_any.at[span], sems.at[chunk])

    def transform(chunk, carry):
        for image in range(per_chunk):
            which = chunk * per_chunk + image
            start = pl.multiple_of(which * pitch, 8)
            lhs = back[pl.ds(start, wide), :].astype(bf16)
            value = lax.dot_general(lhs, inverse[...], (((0,), (0,)), ((), ())), preferred_element_type=f32)
            images[which] = value.astype(bf16)
        out_copy(chunk).start()
        return carry

    lax.fori_loop(0, IMAGE_CHUNKS, transform, 0)
    for chunk in range(IMAGE_CHUNKS):
        out_copy(chunk).wait()


def front(counts, group_ids, images, radial_basis):
    local, radii, angles = images.shape
    freqs, _, pmax = radial_basis.shape
    blocks = freqs // BLOCK
    forward, _ = fixed_tables(angles, freqs)
    vmem = pl.BlockSpec(memory_space=pltpu.VMEM)
    hbm = pl.BlockSpec(memory_space=pltpu.HBM)
    return pl.pallas_call(
        functools.partial(front_kernel, freqs),
        in_specs=[vmem, vmem, hbm, hbm, hbm],
        out_specs=(vmem, pl.BlockSpec(memory_space=pltpu.SMEM)),
        out_shape=(
            jax.ShapeDtypeStruct((blocks * OWN, ROWS, 128), bf16),
            jax.ShapeDtypeStruct((blocks, 128), jnp.int32),
        ),
        scratch_shapes=[
            pltpu.VMEM(images.shape, bf16),
            pltpu.VMEM(forward.shape, bf16),
            pltpu.VMEM(radial_basis.shape, bf16),
            pltpu.VMEM((local * (2 * freqs + PITCH_PAD), 128), f32),
            pltpu.VMEM((2 * OWN, 128, 128), f32),
            pltpu.VMEM((OWN, ROWS + 64, 128), f32),
            pltpu.VMEM((blocks, 128), jnp.int32),
            pltpu.SemaphoreType.DMA((IMAGE_CHUNKS,)),
            pltpu.SemaphoreType.DMA((2,)),
            pltpu.SemaphoreType.DMA((blocks,)),
        ],
        compiler_params=pltpu.CompilerParams(vmem_limit_bytes=FRONT_VMEM),
        name="front",
    )(
        counts.reshape(1, freqs), group_ids.reshape(1, local), images, jnp.asarray(forward), radial_basis
    )


def middle(me, tab, ctf_gain, noise_var, arrived, image_total):
    smem = pl.BlockSpec(memory_space=pltpu.SMEM)
    vmem = pl.BlockSpec(memory_space=pltpu.VMEM)
    devices = arrived.shape[0]
    groups_count = ctf_gain.shape[0]
    return pl.pallas_call(
        functools.partial(middle_kernel, float(image_total)),
        in_specs=[smem, smem, smem, smem, vmem],
        out_specs=vmem,
        out_shape=jax.ShapeDtypeStruct(arrived.shape, bf16),
        scratch_shapes=[
            pltpu.VMEM((devices, ROWS + 64, 128), f32),
            pltpu.VMEM((OWN, 128, devices * 64), bf16),
            pltpu.VMEM((OWN, 128, devices * 64), bf16),
            pltpu.VMEM((OWN, 128, 128), f32),
            pltpu.VMEM((OWN, 128, groups_count * 128), bf16),
            pltpu.VMEM((devices, ROWS + 64, 128), f32),
        ],
        compiler_params=pltpu.CompilerParams(vmem_limit_bytes=VMEM_LIMIT),
        name="middle",
    )(me, tab, ctf_gain, noise_var, arrived)


def back(tab, returned, turned_basis, images_shape):
    local, radii, angles = images_shape
    freqs = turned_basis.shape[0]
    _, inverse = fixed_tables(angles, freqs)
    vmem = pl.BlockSpec(memory_space=pltpu.VMEM)
    return pl.pallas_call(
        functools.partial(back_kernel, freqs),
        in_specs=[pl.BlockSpec(memory_space=pltpu.SMEM), vmem, vmem, vmem],
        out_specs=pl.BlockSpec(memory_space=pltpu.HBM),
        out_shape=jax.ShapeDtypeStruct(images_shape, bf16),
        scratch_shapes=[
            pltpu.VMEM((OWN, ROWS + 64, 128), f32),
            pltpu.VMEM((2 * OWN, 128, 128), f32),
            pltpu.VMEM((local * (2 * freqs + PITCH_PAD), 128), f32),
            pltpu.VMEM(images_shape, bf16),
            pltpu.SemaphoreType.DMA((IMAGE_CHUNKS,)),
        ],
        compiler_params=pltpu.CompilerParams(vmem_limit_bytes=VMEM_LIMIT),
        name="back",
    )(tab, returned, turned_basis, jnp.asarray(inverse))


def owned_body(images, group_ids, counts, radial_basis, ctf_gain, noise_var):
    axes = ("img", "grp")
    image_total = images.shape[0] * lax.axis_size(axes)
    packed, tab = front(counts, group_ids, images, radial_basis)
    arrived = lax.all_to_all(packed, axes, split_axis=0, concat_axis=0, tiled=True)
    turned_basis = jnp.swapaxes(radial_basis, 1, 2)
    me = lax.axis_index(axes).astype(jnp.int32).reshape(1)
    arrived, turned_basis = lax.optimization_barrier((arrived, turned_basis))
    cleaned = middle(me, tab, ctf_gain, noise_var, arrived, image_total)
    returned = lax.all_to_all(cleaned, axes, split_axis=0, concat_axis=0, tiled=True)
    return back(tab, returned, turned_basis, images.shape)


def body(images, group_ids, counts, radial_basis, ctf_gain, noise_var):
    devices = lax.axis_size("img") * lax.axis_size("grp")
    freqs = radial_basis.shape[0]
    fits = (
        freqs == OWN * devices
        and lax.axis_size("grp") * OWN == BLOCK
        and images.shape[0] == 32
        and freqs // BLOCK == IMAGE_CHUNKS
        and radial_basis.shape[1:] == (128, 128)
        and freqs % 128 == 0
        and images.shape[2] % 128 == 0
        and ctf_gain.shape[0] % 2 == 0
    )
    chosen = owned_body if fits else general_body
    return chosen(images, group_ids, counts, radial_basis, ctf_gain, noise_var)


def solution(mesh):
    placed = (P(("img", "grp"), None, None), P(("img", "grp")), P(), P(), P(), P())
    return jax.shard_map(
        body, mesh=mesh, in_specs=placed, out_specs=P(("img", "grp"), None, None), check_vma=False
    )
```

```python
import functools
import math

import jax
import jax.numpy as jnp
import numpy as np
from jax import lax
from jax.experimental import pallas as pl
from jax.experimental.pallas import tpu as pltpu
from jax.sharding import PartitionSpec as P

NS_ITERS = 7


def dft_tables(angles, freqs):
    angle_index = jnp.arange(angles, dtype=jnp.int32)
    freq_index = jnp.arange(freqs, dtype=jnp.int32)
    turns = angle_index[:, None] * freq_index[None, :] % angles
    phases = turns.astype(jnp.float32) * (2.0 * math.pi / angles)
    factor = 1.0 / math.sqrt(angles)
    cosine = jnp.cos(phases) * factor
    sine = -jnp.sin(phases) * factor
    forward = jnp.concatenate([cosine, sine], 1).astype(jnp.bfloat16)
    doubling = jnp.where(freq_index == 0, 1.0, 2.0).astype(jnp.float32)
    inverse = jnp.concatenate([cosine * doubling[None, :], sine * doubling[None, :]], 1).T.astype(
        jnp.bfloat16
    )
    return (forward, inverse)


def shrink_cov(gram, fourth, total, used, image_total):
    sample = gram / total[:, None, None]
    ident = used[:, :, None] * jnp.eye(used.shape[1], dtype=jnp.float32)[None]
    level = jnp.trace(sample, axis1=1, axis2=2) / jnp.sum(used, 1)
    spread = jnp.sum((sample - level[:, None, None] * ident) ** 2, (1, 2))
    excess = (fourth / total - jnp.sum(sample * sample, (1, 2))) / (2.0 * image_total)
    weight = excess / (excess + spread)
    return (1.0 - weight)[:, None, None] * sample + (weight * level)[:, None, None] * ident


def wiener_filters(cov, gain, noise_level, steps_count):
    identity = jnp.eye(cov.shape[1], dtype=jnp.float32)[None]
    system = (gain * gain)[:, None, None] * cov + noise_level[:, None, None] * identity
    frobenius = jnp.sqrt(jnp.sum(system * system, (1, 2)))
    approx = identity / frobenius[:, None, None]
    for sweep in range(steps_count):
        middle = jnp.matmul(approx, system, precision=lax.Precision.HIGHEST)
        approx = 2.0 * approx - jnp.matmul(middle, approx, precision=lax.Precision.HIGHEST)
    product = jnp.matmul(cov, approx, precision=lax.Precision.HIGHEST)
    return (gain[:, None, None] * product).astype(jnp.bfloat16)


def general_body(images, group_ids, counts, radial_basis, ctf_gain, noise_var):
    local_images = images.shape[0]
    radii = images.shape[1]
    angles = images.shape[2]
    freqs = radial_basis.shape[0]
    pmax = radial_basis.shape[2]
    groups_count = ctf_gain.shape[0]
    owners = lax.axis_size("img")
    owned = freqs // owners
    forward, inverse = dft_tables(angles, freqs)
    used = (jnp.arange(pmax, dtype=jnp.int32)[None, :] < counts[:, None]).astype(jnp.float32)
    basis_used = (radial_basis.astype(jnp.float32) * used[:, None, :]).astype(jnp.bfloat16)
    spectrum = jnp.dot(
        images.reshape(local_images * radii, angles), forward, preferred_element_type=jnp.float32
    )
    spectrum = spectrum.astype(jnp.bfloat16).reshape(local_images, radii, 2, freqs)
    coeffs = jnp.einsum(
        "nrck,krp->kcnp", spectrum, basis_used, preferred_element_type=jnp.float32
    ).astype(jnp.bfloat16)
    first = lax.axis_index("img") * owned
    arrived = lax.all_to_all(coeffs, "img", split_axis=0, concat_axis=2, tiled=True)
    all_ids = lax.all_gather(group_ids, "img", axis=0, tiled=True)
    gains_local = lax.dynamic_slice_in_dim(ctf_gain, first, owned, 1)
    noise_local = lax.dynamic_slice_in_dim(noise_var, first, owned, 0)
    used_local = lax.dynamic_slice_in_dim(used, first, owned, 0)
    onehot = (all_ids[:, None] == jnp.arange(groups_count, dtype=jnp.int32)[None, :]).astype(
        jnp.float32
    )
    gains_kn = jnp.dot(onehot, gains_local, precision=lax.Precision.HIGHEST).T
    scaled = (arrived * gains_kn[:, None, :, None]).astype(jnp.bfloat16)
    gram_part = jnp.einsum("kcnp,kcnq->kpq", scaled, scaled, preferred_element_type=jnp.float32)
    norms = jnp.einsum("kcnp,kcnp->kcn", arrived, arrived, preferred_element_type=jnp.float32)
    squares = gains_kn * gains_kn
    fourth_part = jnp.sum(squares[:, None, :] * norms * norms, (1, 2))
    total_part = 2.0 * jnp.sum(squares, 1)
    gram, fourth, total = lax.psum((gram_part, fourth_part, total_part), "grp")
    image_total = arrived.shape[2] * lax.axis_size("grp")
    cov = shrink_cov(gram, fourth, total, used_local, image_total)
    combos = groups_count * owned
    cov_all = jnp.broadcast_to(cov[None], (groups_count, owned, pmax, pmax)).reshape(
        combos, pmax, pmax
    )
    gain_all = gains_local.reshape(combos)
    noise_all = jnp.tile(noise_local, groups_count)
    share = combos // lax.axis_size("grp")
    start = lax.axis_index("grp") * share
    mine = wiener_filters(
        lax.dynamic_slice_in_dim(cov_all, start, share, 0),
        lax.dynamic_slice_in_dim(gain_all, start, share, 0),
        lax.dynamic_slice_in_dim(noise_all, start, share, 0),
        NS_ITERS,
    )
    filters = lax.all_gather(mine, "grp", axis=0, tiled=True)
    filters = filters.reshape(groups_count, owned, pmax, pmax)
    result = jnp.zeros(arrived.shape, jnp.float32)
    for which_group in range(groups_count):
        part = jnp.einsum(
            "kcnq,kpq->kcnp", arrived, filters[which_group], preferred_element_type=jnp.float32
        )
        result = result + jnp.where((all_ids == which_group)[None, None, :, None], part, 0.0)
    cleaned = result.astype(jnp.bfloat16)
    returned = lax.all_to_all(cleaned, "img", split_axis=2, concat_axis=0, tiled=True)
    back = jnp.einsum(
        "kcnp,krp->nrck", returned, basis_used, preferred_element_type=jnp.float32
    ).astype(jnp.bfloat16)
    back = back.reshape(local_images * radii, 2 * freqs)
    denoised = jnp.dot(back, inverse, preferred_element_type=jnp.float32).astype(jnp.bfloat16)
    return denoised.reshape(local_images, radii, angles)


WAYS = (
    ((0, 4, 8, 15), (1, 5, 9, 14), (2, 6, 10, 13), (3, 7, 11, 12)),
    ((0, 6, 9, 15), (1, 7, 8, 14), (3, 5, 10, 12), (2, 4, 11, 13)),
    ((2, 6, 9, 13), (1, 5, 11, 12), (0, 7, 8, 15), (3, 4, 10, 14)),
    ((2, 6, 10, 12), (1, 4, 9, 15), (0, 7, 11, 14), (3, 5, 8, 13)),
    ((2, 4, 11, 14), (0, 7, 9, 12), (3, 5, 8, 15), (1, 6, 10, 13)),
    ((3, 4, 10, 13), (1, 5, 8, 15), (0, 6, 9, 14), (2, 7, 11, 12)),
    ((2, 7, 8, 12), (3, 4, 10, 15), (1, 6, 9, 14), (0, 5, 11, 13)),
    ((2, 4, 9, 14), (0, 6, 11, 12), (1, 5, 10, 13), (3, 7, 8, 15)),
)
OWN = 4
BLOCK = 16
FULL_ROWS = 208
SHORT_ROWS = 176
HEAVIEST = 3 * BLOCK
IMAGE_CHUNKS = 8
PITCH_PAD = 8
VMEM_LIMIT = 48 * 1024 * 1024
FRONT_VMEM = 121 * 512 * 1024

f32 = jnp.float32
bf16 = jnp.bfloat16


def fixed_tables(angles, freqs):
    turns = np.arange(angles)[:, None] * np.arange(freqs)[None, :] % angles
    phases = turns * (2.0 * math.pi / angles)
    cosine = np.cos(phases) / math.sqrt(angles)
    sine = -np.sin(phases) / math.sqrt(angles)
    forward = np.concatenate([cosine, sine], 1)
    doubling = np.where(np.arange(freqs) == 0, 1.0, 2.0)[None, :]
    inverse = np.concatenate([cosine * doubling, sine * doubling], 1).T
    return forward.T.astype(np.float32).astype(jnp.bfloat16), inverse.astype(np.float32).astype(jnp.bfloat16)


def owner_tables(row_of_counts, blocks):
    every = jnp.broadcast_to(row_of_counts, (blocks, row_of_counts.shape[1]))
    block = lax.broadcasted_iota(jnp.int32, every.shape, 0)
    counts = every
    for which in range(1, blocks):
        counts = jnp.where(block == which, pltpu.roll(every, every.shape[1] - BLOCK * which, 1), counts)
    counts = counts[:, :BLOCK]
    lane = lax.broadcasted_iota(jnp.int32, counts.shape, 1)
    rank = jnp.zeros(counts.shape, jnp.int32)
    for other in range(BLOCK):
        column = counts[:, other:other + 1]
        before = (column > counts) | ((column == counts) & (lane > other))
        rank = rank + before.astype(jnp.int32)
    def over_lanes(hit, value):
        return jnp.sum(jnp.where(hit, value, 0).astype(f32), 1, keepdims=True).astype(jnp.int32)

    by_rank = [over_lanes(rank == place, (counts + 1) // 2) for place in range(BLOCK)]
    least, wanted = None, None
    for way in WAYS:
        loads = [by_rank[ranks[0]] + by_rank[ranks[1]] + by_rank[ranks[2]] + by_rank[ranks[3]] for ranks in way]
        load = functools.reduce(jnp.maximum, loads)
        flat = [place for ranks in way for place in ranks]
        if least is None:
            least, wanted = load, [jnp.full(load.shape, place, jnp.int32) for place in flat]
        else:
            better = load < least
            least = jnp.where(better, load, least)
            wanted = [jnp.where(better, place, old) for place, old in zip(flat, wanted)]
    full = lax.broadcasted_iota(jnp.int32, (blocks, 128), 1)
    first = lax.broadcasted_iota(jnp.int32, (blocks, 1), 0) * BLOCK
    heaviest = jnp.max(least.astype(f32), 0, keepdims=True).astype(jnp.int32)
    table = jnp.where(full == HEAVIEST, heaviest, 0)
    for dest in range(OWN):
        offset = jnp.zeros((blocks, 1), jnp.int32)
        for own in range(OWN):
            place = dest * OWN + own
            hit = rank == wanted[place]
            freq = over_lanes(hit, lane) + first
            count = over_lanes(hit, counts)
            table = jnp.where(full == place, freq, table)
            table = jnp.where(full == place + BLOCK, count, table)
            table = jnp.where(full == place + 2 * BLOCK, offset, table)
            offset = offset + (count + 1) // 2
    return table


def low_half(shape):
    return lax.broadcasted_iota(jnp.int32, shape, 1) < 64


def swap_halves(value):
    return pltpu.roll(value, 64, 1)


def front_kernel(freqs, counts, ids, images_any, forward_any, basis_any, packed, whole_any, tab,
                 images, forward, basis, spec, turned, rows, table, whole, image_sems, sems, basis_sems):
    wide = 2 * freqs
    pitch = wide + PITCH_PAD
    local = images.shape[0]
    blocks = freqs // BLOCK
    per_chunk = local // IMAGE_CHUNKS

    def image_copy(chunk):
        span = pl.ds(chunk * per_chunk, per_chunk)
        return pltpu.make_async_copy(images_any.at[span], images.at[span], image_sems.at[chunk])

    def basis_copy(block):
        span = pl.ds(block * BLOCK, BLOCK)
        return pltpu.make_async_copy(basis_any.at[span], basis.at[span], basis_sems.at[block])

    forward_copy = pltpu.make_async_copy(forward_any, forward, sems.at[0])
    table_copy = pltpu.make_async_copy(table, tab, sems.at[1])
    forward_copy.start()
    for chunk in range(IMAGE_CHUNKS):
        image_copy(chunk).start()
    table[...] = owner_tables(counts[...], blocks)
    table_copy.start()
    id_row = jnp.concatenate([ids[...].astype(f32)] * (128 // local), 1)
    forward_copy.wait()

    def transform(chunk, carry):
        image_copy(chunk).wait()
        basis_copy(chunk).start()
        for pair in range(per_chunk // 2):
            first = chunk * per_chunk + 2 * pair
            both = images[pl.ds(first, 2)].reshape(256, images.shape[2])
            part = lax.dot_general(forward[...], both, (((1,), (1,)), ((), ())), preferred_element_type=f32)
            part = part.astype(bf16).astype(f32)
            for which in range(2):
                start = pl.multiple_of((first + which) * pitch, 8)
                spec[pl.ds(start, wide), :] = part[:, 128 * which:128 * (which + 1)]
        return carry

    lax.fori_loop(0, IMAGE_CHUNKS, transform, 0)
    table_copy.wait()
    too_heavy = tab[0, HEAVIEST] > SHORT_ROWS - 1
    low = low_half((64, 128))

    def pack(block, carry):
        basis_copy(block).wait()
        for dest in range(OWN):
            for pair in range(2):
                place = dest * OWN + 2 * pair
                parts = []
                for which in range(2):
                    freq = tab[block, place + which]
                    real = spec[pl.ds(freq, local, stride=pitch), :]
                    imag = spec[pl.ds(freq + freqs, local, stride=pitch), :]
                    lhs = jnp.concatenate([real, imag], 0).astype(bf16)
                    parts.append(jnp.dot(lhs, basis[freq], preferred_element_type=f32).astype(bf16))
                slot = dest * 2 + pair
                turned[slot] = jnp.concatenate(parts, 0).T.astype(f32)
                even = turned[slot, pl.ds(0, 64, stride=2), :]
                odd = turned[slot, pl.ds(1, 64, stride=2), :]
                rows[dest, pl.ds(tab[block, place + 2 * BLOCK], 64), :] = jnp.where(low, even, swap_halves(odd))
                rows[dest, pl.ds(tab[block, place + 1 + 2 * BLOCK], 64), :] = jnp.where(low, swap_halves(even), odd)

        @pl.when(too_heavy)
        def _():
            for dest in range(OWN):
                rows[dest, FULL_ROWS - 1:FULL_ROWS, :] = id_row
                whole[dest] = rows[dest, 0:FULL_ROWS, :].astype(bf16)
            copy = pltpu.make_async_copy(whole, whole_any.at[pl.ds(block * OWN, OWN)], sems.at[0])
            copy.start()
            copy.wait()

        for dest in range(OWN):
            rows[dest, SHORT_ROWS - 1:SHORT_ROWS, :] = id_row
            packed[block * OWN + dest] = rows[dest, 0:SHORT_ROWS, :].astype(bf16)
        return carry

    lax.fori_loop(0, blocks, pack, 0)


def split(value):
    high = value.astype(bf16)
    return high, (value - high.astype(f32)).astype(bf16)


def side_by_side(value):
    high, low = split(value)
    return jnp.concatenate([high, low], 1)


def wide_product(left, right):
    both = jnp.dot(left, jnp.concatenate([right, right], 0), preferred_element_type=f32)
    return both[:, :128] + both[:, 128:]


def total_of(value):
    return jnp.sum(jnp.sum(value, 1, keepdims=True), 0, keepdims=True)


def middle_kernel(image_total, me, tab, gain, noise, arrived, out, wide, coeff, scaled, covs, filters, clean):
    devices, sent_rows, _ = arrived.shape
    groups_count = gain.shape[0]
    columns = devices * 64
    low = low_half((64, 128))
    block = me[0] // OWN
    first_place = lax.rem(me[0], OWN) * OWN
    wide[:, 0:sent_rows, :] = arrived[...].astype(f32)
    pieces = [
        jnp.where(low_half((1, 128)), wide[2 * m, sent_rows - 1:sent_rows, :], wide[2 * m + 1, sent_rows - 1:sent_rows, :])
        for m in range(devices // 2)
    ]
    ids = jnp.concatenate(pieces, 1)
    row = lax.broadcasted_iota(jnp.int32, (128, 128), 0)
    column = lax.broadcasted_iota(jnp.int32, (128, 128), 1)
    slot_row = jnp.where(row < 64, 2 * row, 2 * row - 127)
    eye = (row == column).astype(f32)

    for own in range(OWN):
        place = first_place + own
        freq = tab[block, place]
        count = tab[block, place + BLOCK]
        where = tab[block, place + 2 * BLOCK]
        used = slot_row < count
        scale = jnp.zeros((1, columns), f32)
        for g in range(groups_count):
            scale = jnp.where(ids == float(g), gain[g, freq], scale)
        squares = scale * scale
        norms = []
        for m in range(devices // 2):
            span = slice(128 * m, 128 * (m + 1))
            first = wide[2 * m, pl.ds(where, 64), :]
            second = wide[2 * m + 1, pl.ds(where, 64), :]
            even = jnp.where(low, first, swap_halves(second))
            odd = jnp.where(low, swap_halves(first), second)
            value = jnp.where(used, jnp.concatenate([even, odd], 0), 0.0)
            coeff[own, :, span] = value.astype(bf16)
            scaled[own, :, span] = (value * scale[:, span]).astype(bf16)
            norms.append(jnp.sum(value * value, 0, keepdims=True))
        norms = jnp.concatenate(norms, 1)
        fourth = jnp.sum(squares * norms * norms, 1, keepdims=True)
        total = jnp.sum(squares, 1, keepdims=True)
        weighted = scaled[own]
        gram = lax.dot_general(weighted, weighted, (((1,), (1,)), ((), ())), preferred_element_type=f32)
        sample = gram / total
        ident = jnp.where(used, eye, 0.0)
        level = total_of(sample * eye) / count.astype(f32)
        spread = total_of((sample - level * ident) ** 2)
        excess = (fourth / total - total_of(sample * sample)) / (2.0 * image_total)
        weight = excess / (excess + spread)
        covs[own] = (1.0 - weight) * sample + (weight * level) * ident

    def invert(own, carry):
        place = first_place + own
        freq = tab[block, place]
        cov = covs[own]
        cov_parts = side_by_side(cov)
        power, series, size = [], [], []
        for g in range(groups_count):
            system = (gain[g, freq] * gain[g, freq]) * cov + noise[freq] * eye
            size.append(jnp.sqrt(total_of(system * system)))
            power.append(eye - system / size[g])
            series.append(eye + power[g])
        for sweep in range(NS_ITERS):
            for g in range(groups_count):
                right = side_by_side(power[g])
                if sweep == 0:
                    power[g] = wide_product(right, right)
                elif sweep == NS_ITERS - 1:
                    series[g] = series[g] + wide_product(side_by_side(series[g]), right)
                else:
                    both = wide_product(jnp.concatenate([right, side_by_side(series[g])], 0), right)
                    power[g] = both[:128]
                    series[g] = series[g] + both[128:]
        for g in range(groups_count):
            product = wide_product(cov_parts, side_by_side(series[g])) * (gain[g, freq] / size[g])
            filters[own, :, 128 * g:128 * (g + 1)] = product.astype(bf16)
        return carry

    lax.fori_loop(0, OWN, invert, 0)

    def apply(own, carry):
        where = tab[block, first_place + own + 2 * BLOCK]
        for chunk in range(columns // 256):
            span = slice(256 * chunk, 256 * (chunk + 1))
            value = coeff[own, :, span]
            masked = jnp.concatenate(
                [jnp.where(ids[:, span] == float(g), value, jnp.zeros_like(value)) for g in range(groups_count)], 0
            )
            chosen = jnp.dot(filters[own], masked, preferred_element_type=f32)
            for m in range(2):
                even = chosen[:64, 128 * m:128 * (m + 1)]
                odd = chosen[64:, 128 * m:128 * (m + 1)]
                clean[4 * chunk + 2 * m, pl.ds(where, 64), :] = jnp.where(low, even, swap_halves(odd))
                clean[4 * chunk + 2 * m + 1, pl.ds(where, 64), :] = jnp.where(low, swap_halves(even), odd)
        return carry

    lax.fori_loop(0, OWN, apply, 0)
    out[...] = clean[:, 0:sent_rows, :].astype(bf16)


def back_kernel(freqs, tab, returned, basis, inverse, out_any, rows, turned, back, images, sems):
    wide = 2 * freqs
    pitch = wide + PITCH_PAD
    local = images.shape[0]
    blocks = freqs // BLOCK
    per_chunk = local // IMAGE_CHUNKS
    low = low_half((64, 128))
    pair_row = lax.broadcasted_iota(jnp.int32, (64, 128), 0) * 2

    def unpack(block, carry):
        for dest in range(OWN):
            rows[dest, 0:returned.shape[1], :] = returned[block * OWN + dest].astype(f32)
            for pair in range(2):
                place = dest * OWN + 2 * pair
                first = rows[dest, pl.ds(tab[block, place + 2 * BLOCK], 64), :]
                second = rows[dest, pl.ds(tab[block, place + 1 + 2 * BLOCK], 64), :]
                count = jnp.where(low, tab[block, place + BLOCK], tab[block, place + 1 + BLOCK])
                even = jnp.where(low, first, swap_halves(second))
                odd = jnp.where(low, swap_halves(first), second)
                slot = dest * 2 + pair
                turned[slot, pl.ds(0, 64, stride=2), :] = jnp.where(pair_row < count, even, 0.0)
                turned[slot, pl.ds(1, 64, stride=2), :] = jnp.where(pair_row + 1 < count, odd, 0.0)
                lhs = turned[slot].astype(bf16).T
                for which in range(2):
                    freq = tab[block, place + which]
                    value = jnp.dot(lhs[64 * which:64 * (which + 1)], basis[freq], preferred_element_type=f32)
                    value = value.astype(bf16).astype(f32)
                    back[pl.ds(freq, local, stride=pitch), :] = value[:local]
                    back[pl.ds(freq + freqs, local, stride=pitch), :] = value[local:]
        return carry

    lax.fori_loop(0, blocks, unpack, 0)

    def out_copy(chunk):
        span = pl.ds(chunk * per_chunk, per_chunk)
        return pltpu.make_async_copy(images.at[span], out_any.at[span], sems.at[chunk])

    def transform(chunk, carry):
        for image in range(per_chunk):
            which = chunk * per_chunk + image
            start = pl.multiple_of(which * pitch, 8)
            lhs = back[pl.ds(start, wide), :].astype(bf16)
            value = lax.dot_general(lhs, inverse[...], (((0,), (0,)), ((), ())), preferred_element_type=f32)
            images[which] = value.astype(bf16)
        out_copy(chunk).start()
        return carry

    lax.fori_loop(0, IMAGE_CHUNKS, transform, 0)
    for chunk in range(IMAGE_CHUNKS):
        out_copy(chunk).wait()


def front(counts, group_ids, images, radial_basis):
    local, radii, angles = images.shape
    freqs, _, pmax = radial_basis.shape
    blocks = freqs // BLOCK
    forward, _ = fixed_tables(angles, freqs)
    vmem = pl.BlockSpec(memory_space=pltpu.VMEM)
    hbm = pl.BlockSpec(memory_space=pltpu.HBM)
    return pl.pallas_call(
        functools.partial(front_kernel, freqs),
        in_specs=[vmem, vmem, hbm, hbm, hbm],
        out_specs=(vmem, hbm, pl.BlockSpec(memory_space=pltpu.SMEM)),
        out_shape=(
            jax.ShapeDtypeStruct((blocks * OWN, SHORT_ROWS, 128), bf16),
            jax.ShapeDtypeStruct((blocks * OWN, FULL_ROWS, 128), bf16),
            jax.ShapeDtypeStruct((blocks, 128), jnp.int32),
        ),
        scratch_shapes=[
            pltpu.VMEM(images.shape, bf16),
            pltpu.VMEM(forward.shape, bf16),
            pltpu.VMEM(radial_basis.shape, bf16),
            pltpu.VMEM((local * (2 * freqs + PITCH_PAD), 128), f32),
            pltpu.VMEM((2 * OWN, 128, 128), f32),
            pltpu.VMEM((OWN, FULL_ROWS + 64, 128), f32),
            pltpu.VMEM((blocks, 128), jnp.int32),
            pltpu.VMEM((OWN, FULL_ROWS, 128), bf16),
            pltpu.SemaphoreType.DMA((IMAGE_CHUNKS,)),
            pltpu.SemaphoreType.DMA((2,)),
            pltpu.SemaphoreType.DMA((blocks,)),
        ],
        compiler_params=pltpu.CompilerParams(vmem_limit_bytes=FRONT_VMEM),
        name="front",
    )(
        counts.reshape(1, freqs), group_ids.reshape(1, local), images, jnp.asarray(forward), radial_basis
    )


def middle(me, tab, ctf_gain, noise_var, arrived, image_total):
    smem = pl.BlockSpec(memory_space=pltpu.SMEM)
    vmem = pl.BlockSpec(memory_space=pltpu.VMEM)
    devices, sent_rows, _ = arrived.shape
    groups_count = ctf_gain.shape[0]
    return pl.pallas_call(
        functools.partial(middle_kernel, float(image_total)),
        in_specs=[smem, smem, smem, smem, vmem],
        out_specs=vmem,
        out_shape=jax.ShapeDtypeStruct(arrived.shape, bf16),
        scratch_shapes=[
            pltpu.VMEM((devices, sent_rows + 64, 128), f32),
            pltpu.VMEM((OWN, 128, devices * 64), bf16),
            pltpu.VMEM((OWN, 128, devices * 64), bf16),
            pltpu.VMEM((OWN, 128, 128), f32),
            pltpu.VMEM((OWN, 128, groups_count * 128), bf16),
            pltpu.VMEM((devices, sent_rows + 64, 128), f32),
        ],
        compiler_params=pltpu.CompilerParams(vmem_limit_bytes=VMEM_LIMIT),
        name="middle",
    )(me, tab, ctf_gain, noise_var, arrived)


def back(tab, returned, turned_basis, images_shape):
    local, radii, angles = images_shape
    freqs = turned_basis.shape[0]
    _, inverse = fixed_tables(angles, freqs)
    vmem = pl.BlockSpec(memory_space=pltpu.VMEM)
    return pl.pallas_call(
        functools.partial(back_kernel, freqs),
        in_specs=[pl.BlockSpec(memory_space=pltpu.SMEM), vmem, vmem, vmem],
        out_specs=pl.BlockSpec(memory_space=pltpu.HBM),
        out_shape=jax.ShapeDtypeStruct(images_shape, bf16),
        scratch_shapes=[
            pltpu.VMEM((OWN, returned.shape[1] + 64, 128), f32),
            pltpu.VMEM((2 * OWN, 128, 128), f32),
            pltpu.VMEM((local * (2 * freqs + PITCH_PAD), 128), f32),
            pltpu.VMEM(images_shape, bf16),
            pltpu.SemaphoreType.DMA((IMAGE_CHUNKS,)),
        ],
        compiler_params=pltpu.CompilerParams(vmem_limit_bytes=VMEM_LIMIT),
        name="back",
    )(tab, returned, turned_basis, jnp.asarray(inverse))


def owned_body(images, group_ids, counts, radial_basis, ctf_gain, noise_var):
    axes = ("img", "grp")
    image_total = images.shape[0] * lax.axis_size(axes)
    short, whole, tab = front(counts, group_ids, images, radial_basis)
    me = lax.axis_index(axes).astype(jnp.int32).reshape(1)

    def rest(packed, tab, me, radial_basis, ctf_gain, noise_var):
        arrived = lax.all_to_all(packed, axes, split_axis=0, concat_axis=0, tiled=True)
        turned_basis = jnp.swapaxes(radial_basis, 1, 2)
        arrived, turned_basis = lax.optimization_barrier((arrived, turned_basis))
        cleaned = middle(me, tab, ctf_gain, noise_var, arrived, image_total)
        returned = lax.all_to_all(cleaned, axes, split_axis=0, concat_axis=0, tiled=True)
        return back(tab, returned, turned_basis, images.shape)

    return lax.cond(
        tab[0, HEAVIEST] > SHORT_ROWS - 1,
        lambda short, whole, *others: rest(whole, *others),
        lambda short, whole, *others: rest(short, *others),
        short, whole, tab, me, radial_basis, ctf_gain, noise_var,
    )


def body(images, group_ids, counts, radial_basis, ctf_gain, noise_var):
    devices = lax.axis_size("img") * lax.axis_size("grp")
    freqs = radial_basis.shape[0]
    fits = (
        freqs == OWN * devices
        and lax.axis_size("grp") * OWN == BLOCK
        and images.shape[0] == 32
        and freqs // BLOCK == IMAGE_CHUNKS
        and radial_basis.shape[1:] == (128, 128)
        and freqs % 128 == 0
        and images.shape[2] % 128 == 0
        and ctf_gain.shape[0] % 2 == 0
    )
    chosen = owned_body if fits else general_body
    return chosen(images, group_ids, counts, radial_basis, ctf_gain, noise_var)


def solution(mesh):
    placed = (P(("img", "grp"), None, None), P(("img", "grp")), P(), P(), P(), P())
    return jax.shard_map(
        body, mesh=mesh, in_specs=placed, out_specs=P(("img", "grp"), None, None), check_vma=False
    )
```

```python
import functools
import math

import jax
import jax.numpy as jnp
import numpy as np
from jax import lax
from jax.experimental import pallas as pl
from jax.experimental.pallas import tpu as pltpu
from jax.sharding import PartitionSpec as P

NS_ITERS = 7


def dft_tables(angles, freqs):
    angle_index = jnp.arange(angles, dtype=jnp.int32)
    freq_index = jnp.arange(freqs, dtype=jnp.int32)
    turns = angle_index[:, None] * freq_index[None, :] % angles
    phases = turns.astype(jnp.float32) * (2.0 * math.pi / angles)
    factor = 1.0 / math.sqrt(angles)
    cosine = jnp.cos(phases) * factor
    sine = -jnp.sin(phases) * factor
    forward = jnp.concatenate([cosine, sine], 1).astype(jnp.bfloat16)
    doubling = jnp.where(freq_index == 0, 1.0, 2.0).astype(jnp.float32)
    inverse = jnp.concatenate([cosine * doubling[None, :], sine * doubling[None, :]], 1).T.astype(
        jnp.bfloat16
    )
    return (forward, inverse)


def shrink_cov(gram, fourth, total, used, image_total):
    sample = gram / total[:, None, None]
    ident = used[:, :, None] * jnp.eye(used.shape[1], dtype=jnp.float32)[None]
    level = jnp.trace(sample, axis1=1, axis2=2) / jnp.sum(used, 1)
    spread = jnp.sum((sample - level[:, None, None] * ident) ** 2, (1, 2))
    excess = (fourth / total - jnp.sum(sample * sample, (1, 2))) / (2.0 * image_total)
    weight = excess / (excess + spread)
    return (1.0 - weight)[:, None, None] * sample + (weight * level)[:, None, None] * ident


def wiener_filters(cov, gain, noise_level, steps_count):
    identity = jnp.eye(cov.shape[1], dtype=jnp.float32)[None]
    system = (gain * gain)[:, None, None] * cov + noise_level[:, None, None] * identity
    frobenius = jnp.sqrt(jnp.sum(system * system, (1, 2)))
    approx = identity / frobenius[:, None, None]
    for sweep in range(steps_count):
        middle = jnp.matmul(approx, system, precision=lax.Precision.HIGHEST)
        approx = 2.0 * approx - jnp.matmul(middle, approx, precision=lax.Precision.HIGHEST)
    product = jnp.matmul(cov, approx, precision=lax.Precision.HIGHEST)
    return (gain[:, None, None] * product).astype(jnp.bfloat16)


def general_body(images, group_ids, counts, radial_basis, ctf_gain, noise_var):
    local_images = images.shape[0]
    radii = images.shape[1]
    angles = images.shape[2]
    freqs = radial_basis.shape[0]
    pmax = radial_basis.shape[2]
    groups_count = ctf_gain.shape[0]
    owners = lax.axis_size("img")
    owned = freqs // owners
    forward, inverse = dft_tables(angles, freqs)
    used = (jnp.arange(pmax, dtype=jnp.int32)[None, :] < counts[:, None]).astype(jnp.float32)
    basis_used = (radial_basis.astype(jnp.float32) * used[:, None, :]).astype(jnp.bfloat16)
    spectrum = jnp.dot(
        images.reshape(local_images * radii, angles), forward, preferred_element_type=jnp.float32
    )
    spectrum = spectrum.astype(jnp.bfloat16).reshape(local_images, radii, 2, freqs)
    coeffs = jnp.einsum(
        "nrck,krp->kcnp", spectrum, basis_used, preferred_element_type=jnp.float32
    ).astype(jnp.bfloat16)
    first = lax.axis_index("img") * owned
    arrived = lax.all_to_all(coeffs, "img", split_axis=0, concat_axis=2, tiled=True)
    all_ids = lax.all_gather(group_ids, "img", axis=0, tiled=True)
    gains_local = lax.dynamic_slice_in_dim(ctf_gain, first, owned, 1)
    noise_local = lax.dynamic_slice_in_dim(noise_var, first, owned, 0)
    used_local = lax.dynamic_slice_in_dim(used, first, owned, 0)
    onehot = (all_ids[:, None] == jnp.arange(groups_count, dtype=jnp.int32)[None, :]).astype(
        jnp.float32
    )
    gains_kn = jnp.dot(onehot, gains_local, precision=lax.Precision.HIGHEST).T
    scaled = (arrived * gains_kn[:, None, :, None]).astype(jnp.bfloat16)
    gram_part = jnp.einsum("kcnp,kcnq->kpq", scaled, scaled, preferred_element_type=jnp.float32)
    norms = jnp.einsum("kcnp,kcnp->kcn", arrived, arrived, preferred_element_type=jnp.float32)
    squares = gains_kn * gains_kn
    fourth_part = jnp.sum(squares[:, None, :] * norms * norms, (1, 2))
    total_part = 2.0 * jnp.sum(squares, 1)
    gram, fourth, total = lax.psum((gram_part, fourth_part, total_part), "grp")
    image_total = arrived.shape[2] * lax.axis_size("grp")
    cov = shrink_cov(gram, fourth, total, used_local, image_total)
    combos = groups_count * owned
    cov_all = jnp.broadcast_to(cov[None], (groups_count, owned, pmax, pmax)).reshape(
        combos, pmax, pmax
    )
    gain_all = gains_local.reshape(combos)
    noise_all = jnp.tile(noise_local, groups_count)
    share = combos // lax.axis_size("grp")
    start = lax.axis_index("grp") * share
    mine = wiener_filters(
        lax.dynamic_slice_in_dim(cov_all, start, share, 0),
        lax.dynamic_slice_in_dim(gain_all, start, share, 0),
        lax.dynamic_slice_in_dim(noise_all, start, share, 0),
        NS_ITERS,
    )
    filters = lax.all_gather(mine, "grp", axis=0, tiled=True)
    filters = filters.reshape(groups_count, owned, pmax, pmax)
    result = jnp.zeros(arrived.shape, jnp.float32)
    for which_group in range(groups_count):
        part = jnp.einsum(
            "kcnq,kpq->kcnp", arrived, filters[which_group], preferred_element_type=jnp.float32
        )
        result = result + jnp.where((all_ids == which_group)[None, None, :, None], part, 0.0)
    cleaned = result.astype(jnp.bfloat16)
    returned = lax.all_to_all(cleaned, "img", split_axis=2, concat_axis=0, tiled=True)
    back = jnp.einsum(
        "kcnp,krp->nrck", returned, basis_used, preferred_element_type=jnp.float32
    ).astype(jnp.bfloat16)
    back = back.reshape(local_images * radii, 2 * freqs)
    denoised = jnp.dot(back, inverse, preferred_element_type=jnp.float32).astype(jnp.bfloat16)
    return denoised.reshape(local_images, radii, angles)


WAYS = (
    ((0, 4, 8, 15), (1, 5, 9, 14), (2, 6, 10, 13), (3, 7, 11, 12)),
    ((0, 6, 9, 15), (1, 7, 8, 14), (3, 5, 10, 12), (2, 4, 11, 13)),
    ((2, 6, 9, 13), (1, 5, 11, 12), (0, 7, 8, 15), (3, 4, 10, 14)),
    ((2, 6, 10, 12), (1, 4, 9, 15), (0, 7, 11, 14), (3, 5, 8, 13)),
    ((2, 4, 11, 14), (0, 7, 9, 12), (3, 5, 8, 15), (1, 6, 10, 13)),
    ((3, 4, 10, 13), (1, 5, 8, 15), (0, 6, 9, 14), (2, 7, 11, 12)),
    ((2, 7, 8, 12), (3, 4, 10, 15), (1, 6, 9, 14), (0, 5, 11, 13)),
    ((2, 4, 9, 14), (0, 6, 11, 12), (1, 5, 10, 13), (3, 7, 8, 15)),
)
OWN = 4
BLOCK = 16
FULL_ROWS = 208
SHORT_ROWS = 176
HEAVIEST = 3 * BLOCK
IMAGE_CHUNKS = 8
PITCH_PAD = 8
VMEM_LIMIT = 48 * 1024 * 1024
FRONT_VMEM = 121 * 512 * 1024

f32 = jnp.float32
bf16 = jnp.bfloat16


def fixed_tables(angles, freqs):
    turns = np.arange(angles)[:, None] * np.arange(freqs)[None, :] % angles
    phases = turns * (2.0 * math.pi / angles)
    cosine = np.cos(phases) / math.sqrt(angles)
    sine = -np.sin(phases) / math.sqrt(angles)
    forward = np.concatenate([cosine, sine], 1)
    doubling = np.where(np.arange(freqs) == 0, 1.0, 2.0)[None, :]
    inverse = np.concatenate([cosine * doubling, sine * doubling], 1).T
    return forward.T.astype(np.float32).astype(jnp.bfloat16), inverse.astype(np.float32).astype(jnp.bfloat16)


def owner_tables(row_of_counts, blocks):
    every = jnp.broadcast_to(row_of_counts, (blocks, row_of_counts.shape[1]))
    block = lax.broadcasted_iota(jnp.int32, every.shape, 0)
    counts = every
    for which in range(1, blocks):
        counts = jnp.where(block == which, pltpu.roll(every, every.shape[1] - BLOCK * which, 1), counts)
    counts = counts[:, :BLOCK]
    lane = lax.broadcasted_iota(jnp.int32, counts.shape, 1)
    rank = jnp.zeros(counts.shape, jnp.int32)
    for other in range(BLOCK):
        column = counts[:, other:other + 1]
        before = (column > counts) | ((column == counts) & (lane > other))
        rank = rank + before.astype(jnp.int32)
    def over_lanes(hit, value):
        return jnp.sum(jnp.where(hit, value, 0).astype(f32), 1, keepdims=True).astype(jnp.int32)

    by_rank = [over_lanes(rank == place, (counts + 1) // 2) for place in range(BLOCK)]
    least, wanted = None, None
    for way in WAYS:
        loads = [by_rank[ranks[0]] + by_rank[ranks[1]] + by_rank[ranks[2]] + by_rank[ranks[3]] for ranks in way]
        load = functools.reduce(jnp.maximum, loads)
        flat = [place for ranks in way for place in ranks]
        if least is None:
            least, wanted = load, [jnp.full(load.shape, place, jnp.int32) for place in flat]
        else:
            better = load < least
            least = jnp.where(better, load, least)
            wanted = [jnp.where(better, place, old) for place, old in zip(flat, wanted)]
    full = lax.broadcasted_iota(jnp.int32, (blocks, 128), 1)
    first = lax.broadcasted_iota(jnp.int32, (blocks, 1), 0) * BLOCK
    heaviest = jnp.max(least.astype(f32), 0, keepdims=True).astype(jnp.int32)
    table = jnp.where(full == HEAVIEST, heaviest, 0)
    for dest in range(OWN):
        offset = jnp.zeros((blocks, 1), jnp.int32)
        for own in range(OWN):
            place = dest * OWN + own
            hit = rank == wanted[place]
            freq = over_lanes(hit, lane) + first
            count = over_lanes(hit, counts)
            table = jnp.where(full == place, freq, table)
            table = jnp.where(full == place + BLOCK, count, table)
            table = jnp.where(full == place + 2 * BLOCK, offset, table)
            offset = offset + (count + 1) // 2
    return table


def low_half(shape):
    return lax.broadcasted_iota(jnp.int32, shape, 1) < 64


def swap_halves(value):
    return pltpu.roll(value, 64, 1)


def front_kernel(freqs, counts, ids, images_any, forward_any, basis_any, packed, whole_any, tab,
                 images, forward, basis, spec, turned, rows, table, whole, image_sems, sems, basis_sems):
    wide = 2 * freqs
    pitch = wide + PITCH_PAD
    local = images.shape[0]
    blocks = freqs // BLOCK
    per_chunk = local // IMAGE_CHUNKS

    def image_copy(chunk):
        span = pl.ds(chunk * per_chunk, per_chunk)
        return pltpu.make_async_copy(images_any.at[span], images.at[span], image_sems.at[chunk])

    def basis_copy(block):
        span = pl.ds(block * BLOCK, BLOCK)
        return pltpu.make_async_copy(basis_any.at[span], basis.at[span], basis_sems.at[block])

    forward_copy = pltpu.make_async_copy(forward_any, forward, sems.at[0])
    table_copy = pltpu.make_async_copy(table, tab, sems.at[1])
    forward_copy.start()
    for chunk in range(IMAGE_CHUNKS):
        image_copy(chunk).start()
    table[...] = owner_tables(counts[...], blocks)
    table_copy.start()
    id_row = jnp.concatenate([ids[...].astype(f32)] * (128 // local), 1)
    forward_copy.wait()

    def transform(chunk, carry):
        image_copy(chunk).wait()
        basis_copy(chunk).start()
        for pair in range(per_chunk // 2):
            first = chunk * per_chunk + 2 * pair
            both = images[pl.ds(first, 2)].reshape(256, images.shape[2])
            part = lax.dot_general(forward[...], both, (((1,), (1,)), ((), ())), preferred_element_type=f32)
            part = part.astype(bf16).astype(f32)
            for which in range(2):
                start = pl.multiple_of((first + which) * pitch, 8)
                spec[pl.ds(start, wide), :] = part[:, 128 * which:128 * (which + 1)]
        return carry

    lax.fori_loop(0, IMAGE_CHUNKS, transform, 0, unroll=True)
    table_copy.wait()
    too_heavy = tab[0, HEAVIEST] > SHORT_ROWS - 1
    low = low_half((64, 128))

    def gather(block):
        for dest in range(OWN):
            for pair in range(2):
                place = dest * OWN + 2 * pair
                parts = []
                for which in range(2):
                    freq = tab[block, place + which]
                    real = spec[pl.ds(freq, local, stride=pitch), :]
                    imag = spec[pl.ds(freq + freqs, local, stride=pitch), :]
                    lhs = jnp.concatenate([real, imag], 0).astype(bf16)
                    parts.append(jnp.dot(lhs, basis[freq], preferred_element_type=f32).astype(bf16))
                slot = dest * 2 + pair
                turned[slot] = jnp.concatenate(parts, 0).T.astype(f32)
                even = turned[slot, pl.ds(0, 64, stride=2), :]
                odd = turned[slot, pl.ds(1, 64, stride=2), :]
                rows[dest, pl.ds(tab[block, place + 2 * BLOCK], 64), :] = jnp.where(low, even, swap_halves(odd))
                rows[dest, pl.ds(tab[block, place + 1 + 2 * BLOCK], 64), :] = jnp.where(low, swap_halves(even), odd)

    def pack(block, carry):
        basis_copy(block).wait()
        gather(block)
        for dest in range(OWN):
            rows[dest, SHORT_ROWS - 1:SHORT_ROWS, :] = id_row
            packed[block * OWN + dest] = rows[dest, 0:SHORT_ROWS, :].astype(bf16)
        return carry

    lax.fori_loop(0, blocks, pack, 0, unroll=2)

    @pl.when(too_heavy)
    def _():
        def pack_whole(block, carry):
            gather(block)
            for dest in range(OWN):
                rows[dest, FULL_ROWS - 1:FULL_ROWS, :] = id_row
                whole[dest] = rows[dest, 0:FULL_ROWS, :].astype(bf16)
            copy = pltpu.make_async_copy(whole, whole_any.at[pl.ds(block * OWN, OWN)], sems.at[0])
            copy.start()
            copy.wait()
            return carry

        lax.fori_loop(0, blocks, pack_whole, 0)


def split(value):
    high = value.astype(bf16)
    return high, (value - high.astype(f32)).astype(bf16)


def side_by_side(value):
    high, low = split(value)
    return jnp.concatenate([high, low], 1)


def wide_product(left, right):
    both = jnp.dot(left, jnp.concatenate([right, right], 0), preferred_element_type=f32)
    return both[:, :128] + both[:, 128:]


def total_of(value):
    return jnp.sum(jnp.sum(value, 1, keepdims=True), 0, keepdims=True)


def middle_kernel(image_total, me, tab, gain, noise, arrived, out, wide, coeff, scaled, covs, filters, clean):
    devices, sent_rows, _ = arrived.shape
    groups_count = gain.shape[0]
    columns = devices * 64
    low = low_half((64, 128))
    block = me[0] // OWN
    first_place = lax.rem(me[0], OWN) * OWN
    wide[:, 0:sent_rows, :] = arrived[...].astype(f32)
    pieces = [
        jnp.where(low_half((1, 128)), wide[2 * m, sent_rows - 1:sent_rows, :], wide[2 * m + 1, sent_rows - 1:sent_rows, :])
        for m in range(devices // 2)
    ]
    ids = jnp.concatenate(pieces, 1)
    row = lax.broadcasted_iota(jnp.int32, (128, 128), 0)
    column = lax.broadcasted_iota(jnp.int32, (128, 128), 1)
    slot_row = jnp.where(row < 64, 2 * row, 2 * row - 127)
    eye = (row == column).astype(f32)

    def gather(own):
        place = first_place + own
        freq = tab[block, place]
        count = tab[block, place + BLOCK]
        where = tab[block, place + 2 * BLOCK]
        used = slot_row < count
        scale = jnp.zeros((1, columns), f32)
        for g in range(groups_count):
            scale = jnp.where(ids == float(g), gain[g, freq], scale)
        squares = scale * scale
        norms = []
        for m in range(devices // 2):
            span = slice(128 * m, 128 * (m + 1))
            first = wide[2 * m, pl.ds(where, 64), :]
            second = wide[2 * m + 1, pl.ds(where, 64), :]
            even = jnp.where(low, first, swap_halves(second))
            odd = jnp.where(low, swap_halves(first), second)
            value = jnp.where(used, jnp.concatenate([even, odd], 0), 0.0)
            coeff[own, :, span] = value.astype(bf16)
            scaled[own, :, span] = (value * scale[:, span]).astype(bf16)
            norms.append(jnp.sum(value * value, 0, keepdims=True))
        norms = jnp.concatenate(norms, 1)
        fourth = jnp.sum(squares * norms * norms, 1, keepdims=True)
        total = jnp.sum(squares, 1, keepdims=True)
        weighted = scaled[own]
        gram = lax.dot_general(weighted, weighted, (((1,), (1,)), ((), ())), preferred_element_type=f32)
        sample = gram / total
        ident = jnp.where(used, eye, 0.0)
        level = total_of(sample * eye) / count.astype(f32)
        spread = total_of((sample - level * ident) ** 2)
        excess = (fourth / total - total_of(sample * sample)) / (2.0 * image_total)
        weight = excess / (excess + spread)
        covs[own] = (1.0 - weight) * sample + (weight * level) * ident

    def invert(own):
        place = first_place + own
        freq = tab[block, place]
        cov = covs[own]
        cov_parts = side_by_side(cov)
        cov_square = wide_product(cov_parts, cov_parts)
        trace = total_of(cov * eye)
        square = total_of(cov * cov)
        power, series, size = [], [], []
        for g in range(groups_count):
            h, s = gain[g, freq] * gain[g, freq], noise[freq]
            size.append(jnp.sqrt(h * h * square + 2.0 * h * s * trace + 128.0 * s * s))
            a, b = 1.0 - s / size[g], h / size[g]
            series.append((1.0 + a) * eye - b * cov)
            power.append((a * a) * eye - (2.0 * a * b) * cov + (b * b) * cov_square)
        for sweep in range(1, NS_ITERS):
            for g in range(groups_count):
                right = side_by_side(power[g])
                if sweep == NS_ITERS - 1:
                    series[g] = series[g] + wide_product(side_by_side(series[g]), right)
                else:
                    both = wide_product(jnp.concatenate([right, side_by_side(series[g])], 0), right)
                    power[g] = both[:128]
                    series[g] = series[g] + both[128:]
        for g in range(groups_count):
            product = wide_product(cov_parts, side_by_side(series[g])) * (gain[g, freq] / size[g])
            filters[own, :, 128 * g:128 * (g + 1)] = product.astype(bf16)

    def apply(own):
        where = tab[block, first_place + own + 2 * BLOCK]
        for chunk in range(columns // 256):
            span = slice(256 * chunk, 256 * (chunk + 1))
            value = coeff[own, :, span]
            masked = jnp.concatenate(
                [jnp.where(ids[:, span] == float(g), value, jnp.zeros_like(value)) for g in range(groups_count)], 0
            )
            chosen = jnp.dot(filters[own], masked, preferred_element_type=f32)
            for m in range(2):
                even = chosen[:64, 128 * m:128 * (m + 1)]
                odd = chosen[64:, 128 * m:128 * (m + 1)]
                clean[4 * chunk + 2 * m, pl.ds(where, 64), :] = jnp.where(low, even, swap_halves(odd))
                clean[4 * chunk + 2 * m + 1, pl.ds(where, 64), :] = jnp.where(low, swap_halves(even), odd)

    for turn in range(OWN + 2):
        if turn < OWN:
            gather(turn)
        if 1 <= turn <= OWN:
            invert(turn - 1)
        if turn >= 2:
            apply(turn - 2)
    out[...] = clean[:, 0:sent_rows, :].astype(bf16)


def back_kernel(freqs, tab, returned, basis, inverse, out_any, rows, turned, back, images, sems):
    wide = 2 * freqs
    pitch = wide + PITCH_PAD
    local = images.shape[0]
    blocks = freqs // BLOCK
    per_chunk = local // IMAGE_CHUNKS
    low = low_half((64, 128))
    pair_row = lax.broadcasted_iota(jnp.int32, (64, 128), 0) * 2

    def unpack(block, carry):
        for dest in range(OWN):
            rows[dest, 0:returned.shape[1], :] = returned[block * OWN + dest].astype(f32)
            for pair in range(2):
                place = dest * OWN + 2 * pair
                first = rows[dest, pl.ds(tab[block, place + 2 * BLOCK], 64), :]
                second = rows[dest, pl.ds(tab[block, place + 1 + 2 * BLOCK], 64), :]
                count = jnp.where(low, tab[block, place + BLOCK], tab[block, place + 1 + BLOCK])
                even = jnp.where(low, first, swap_halves(second))
                odd = jnp.where(low, swap_halves(first), second)
                slot = dest * 2 + pair
                turned[slot, pl.ds(0, 64, stride=2), :] = jnp.where(pair_row < count, even, 0.0)
                turned[slot, pl.ds(1, 64, stride=2), :] = jnp.where(pair_row + 1 < count, odd, 0.0)
                lhs = turned[slot].astype(bf16).T
                for which in range(2):
                    freq = tab[block, place + which]
                    value = jnp.dot(lhs[64 * which:64 * (which + 1)], basis[freq], preferred_element_type=f32)
                    value = value.astype(bf16).astype(f32)
                    back[pl.ds(freq, local, stride=pitch), :] = value[:local]
                    back[pl.ds(freq + freqs, local, stride=pitch), :] = value[local:]
        return carry

    lax.fori_loop(0, blocks, unpack, 0, unroll=4)

    def out_copy(chunk):
        span = pl.ds(chunk * per_chunk, per_chunk)
        return pltpu.make_async_copy(images.at[span], out_any.at[span], sems.at[chunk])

    def transform(chunk, carry):
        for image in range(per_chunk):
            which = chunk * per_chunk + image
            start = pl.multiple_of(which * pitch, 8)
            lhs = back[pl.ds(start, wide), :].astype(bf16)
            value = lax.dot_general(lhs, inverse[...], (((0,), (0,)), ((), ())), preferred_element_type=f32)
            images[which] = value.astype(bf16)
        out_copy(chunk).start()
        return carry

    lax.fori_loop(0, IMAGE_CHUNKS, transform, 0, unroll=True)
    for chunk in range(IMAGE_CHUNKS):
        out_copy(chunk).wait()


def front(counts, group_ids, images, radial_basis):
    local, radii, angles = images.shape
    freqs, _, pmax = radial_basis.shape
    blocks = freqs // BLOCK
    forward, _ = fixed_tables(angles, freqs)
    vmem = pl.BlockSpec(memory_space=pltpu.VMEM)
    hbm = pl.BlockSpec(memory_space=pltpu.HBM)
    return pl.pallas_call(
        functools.partial(front_kernel, freqs),
        in_specs=[vmem, vmem, hbm, hbm, hbm],
        out_specs=(vmem, hbm, pl.BlockSpec(memory_space=pltpu.SMEM)),
        out_shape=(
            jax.ShapeDtypeStruct((blocks * OWN, SHORT_ROWS, 128), bf16),
            jax.ShapeDtypeStruct((blocks * OWN, FULL_ROWS, 128), bf16),
            jax.ShapeDtypeStruct((blocks, 128), jnp.int32),
        ),
        scratch_shapes=[
            pltpu.VMEM(images.shape, bf16),
            pltpu.VMEM(forward.shape, bf16),
            pltpu.VMEM(radial_basis.shape, bf16),
            pltpu.VMEM((local * (2 * freqs + PITCH_PAD), 128), f32),
            pltpu.VMEM((2 * OWN, 128, 128), f32),
            pltpu.VMEM((OWN, FULL_ROWS + 64, 128), f32),
            pltpu.VMEM((blocks, 128), jnp.int32),
            pltpu.VMEM((OWN, FULL_ROWS, 128), bf16),
            pltpu.SemaphoreType.DMA((IMAGE_CHUNKS,)),
            pltpu.SemaphoreType.DMA((2,)),
            pltpu.SemaphoreType.DMA((blocks,)),
        ],
        compiler_params=pltpu.CompilerParams(vmem_limit_bytes=FRONT_VMEM),
        name="front",
    )(
        counts.reshape(1, freqs), group_ids.reshape(1, local), images, jnp.asarray(forward), radial_basis
    )


def middle(me, tab, ctf_gain, noise_var, arrived, image_total):
    smem = pl.BlockSpec(memory_space=pltpu.SMEM)
    vmem = pl.BlockSpec(memory_space=pltpu.VMEM)
    devices, sent_rows, _ = arrived.shape
    groups_count = ctf_gain.shape[0]
    return pl.pallas_call(
        functools.partial(middle_kernel, float(image_total)),
        in_specs=[smem, smem, smem, smem, vmem],
        out_specs=vmem,
        out_shape=jax.ShapeDtypeStruct(arrived.shape, bf16),
        scratch_shapes=[
            pltpu.VMEM((devices, sent_rows + 64, 128), f32),
            pltpu.VMEM((OWN, 128, devices * 64), bf16),
            pltpu.VMEM((OWN, 128, devices * 64), bf16),
            pltpu.VMEM((OWN, 128, 128), f32),
            pltpu.VMEM((OWN, 128, groups_count * 128), bf16),
            pltpu.VMEM((devices, sent_rows + 64, 128), f32),
        ],
        compiler_params=pltpu.CompilerParams(vmem_limit_bytes=VMEM_LIMIT),
        name="middle",
    )(me, tab, ctf_gain, noise_var, arrived)


def back(tab, returned, turned_basis, images_shape):
    local, radii, angles = images_shape
    freqs = turned_basis.shape[0]
    _, inverse = fixed_tables(angles, freqs)
    vmem = pl.BlockSpec(memory_space=pltpu.VMEM)
    return pl.pallas_call(
        functools.partial(back_kernel, freqs),
        in_specs=[pl.BlockSpec(memory_space=pltpu.SMEM), vmem, vmem, vmem],
        out_specs=pl.BlockSpec(memory_space=pltpu.HBM),
        out_shape=jax.ShapeDtypeStruct(images_shape, bf16),
        scratch_shapes=[
            pltpu.VMEM((OWN, returned.shape[1] + 64, 128), f32),
            pltpu.VMEM((2 * OWN, 128, 128), f32),
            pltpu.VMEM((local * (2 * freqs + PITCH_PAD), 128), f32),
            pltpu.VMEM(images_shape, bf16),
            pltpu.SemaphoreType.DMA((IMAGE_CHUNKS,)),
        ],
        compiler_params=pltpu.CompilerParams(vmem_limit_bytes=VMEM_LIMIT),
        name="back",
    )(tab, returned, turned_basis, jnp.asarray(inverse))


def owned_body(images, group_ids, counts, radial_basis, ctf_gain, noise_var):
    axes = ("img", "grp")
    image_total = images.shape[0] * lax.axis_size(axes)
    short, whole, tab = front(counts, group_ids, images, radial_basis)
    me = lax.axis_index(axes).astype(jnp.int32).reshape(1)

    def rest(packed, tab, me, radial_basis, ctf_gain, noise_var):
        arrived = lax.all_to_all(packed, axes, split_axis=0, concat_axis=0, tiled=True)
        turned_basis = jnp.swapaxes(radial_basis, 1, 2)
        arrived, turned_basis = lax.optimization_barrier((arrived, turned_basis))
        cleaned = middle(me, tab, ctf_gain, noise_var, arrived, image_total)
        returned = lax.all_to_all(cleaned, axes, split_axis=0, concat_axis=0, tiled=True)
        return back(tab, returned, turned_basis, images.shape)

    return lax.cond(
        tab[0, HEAVIEST] > SHORT_ROWS - 1,
        lambda short, whole, *others: rest(whole, *others),
        lambda short, whole, *others: rest(short, *others),
        short, whole, tab, me, radial_basis, ctf_gain, noise_var,
    )


def body(images, group_ids, counts, radial_basis, ctf_gain, noise_var):
    devices = lax.axis_size("img") * lax.axis_size("grp")
    freqs = radial_basis.shape[0]
    fits = (
        freqs == OWN * devices
        and lax.axis_size("grp") * OWN == BLOCK
        and images.shape[0] == 32
        and freqs // BLOCK == IMAGE_CHUNKS
        and radial_basis.shape[1:] == (128, 128)
        and freqs % 128 == 0
        and images.shape[2] % 128 == 0
        and ctf_gain.shape[0] % 2 == 0
    )
    chosen = owned_body if fits else general_body
    return chosen(images, group_ids, counts, radial_basis, ctf_gain, noise_var)


def solution(mesh):
    placed = (P(("img", "grp"), None, None), P(("img", "grp")), P(), P(), P(), P())
    return jax.shard_map(
        body, mesh=mesh, in_specs=placed, out_specs=P(("img", "grp"), None, None), check_vma=False
    )
```

```python
import functools
import math

import jax
import jax.numpy as jnp
import numpy as np
from jax import lax
from jax.experimental import pallas as pl
from jax.experimental.pallas import tpu as pltpu
from jax.sharding import PartitionSpec as P

NS_ITERS = 7


def dft_tables(angles, freqs):
    angle_index = jnp.arange(angles, dtype=jnp.int32)
    freq_index = jnp.arange(freqs, dtype=jnp.int32)
    turns = angle_index[:, None] * freq_index[None, :] % angles
    phases = turns.astype(jnp.float32) * (2.0 * math.pi / angles)
    factor = 1.0 / math.sqrt(angles)
    cosine = jnp.cos(phases) * factor
    sine = -jnp.sin(phases) * factor
    forward = jnp.concatenate([cosine, sine], 1).astype(jnp.bfloat16)
    doubling = jnp.where(freq_index == 0, 1.0, 2.0).astype(jnp.float32)
    inverse = jnp.concatenate([cosine * doubling[None, :], sine * doubling[None, :]], 1).T.astype(
        jnp.bfloat16
    )
    return (forward, inverse)


def shrink_cov(gram, fourth, total, used, image_total):
    sample = gram / total[:, None, None]
    ident = used[:, :, None] * jnp.eye(used.shape[1], dtype=jnp.float32)[None]
    level = jnp.trace(sample, axis1=1, axis2=2) / jnp.sum(used, 1)
    spread = jnp.sum((sample - level[:, None, None] * ident) ** 2, (1, 2))
    excess = (fourth / total - jnp.sum(sample * sample, (1, 2))) / (2.0 * image_total)
    weight = excess / (excess + spread)
    return (1.0 - weight)[:, None, None] * sample + (weight * level)[:, None, None] * ident


def wiener_filters(cov, gain, noise_level, steps_count):
    identity = jnp.eye(cov.shape[1], dtype=jnp.float32)[None]
    system = (gain * gain)[:, None, None] * cov + noise_level[:, None, None] * identity
    frobenius = jnp.sqrt(jnp.sum(system * system, (1, 2)))
    approx = identity / frobenius[:, None, None]
    for sweep in range(steps_count):
        middle = jnp.matmul(approx, system, precision=lax.Precision.HIGHEST)
        approx = 2.0 * approx - jnp.matmul(middle, approx, precision=lax.Precision.HIGHEST)
    product = jnp.matmul(cov, approx, precision=lax.Precision.HIGHEST)
    return (gain[:, None, None] * product).astype(jnp.bfloat16)


def general_body(images, group_ids, counts, radial_basis, ctf_gain, noise_var):
    local_images = images.shape[0]
    radii = images.shape[1]
    angles = images.shape[2]
    freqs = radial_basis.shape[0]
    pmax = radial_basis.shape[2]
    groups_count = ctf_gain.shape[0]
    owners = lax.axis_size("img")
    owned = freqs // owners
    forward, inverse = dft_tables(angles, freqs)
    used = (jnp.arange(pmax, dtype=jnp.int32)[None, :] < counts[:, None]).astype(jnp.float32)
    basis_used = (radial_basis.astype(jnp.float32) * used[:, None, :]).astype(jnp.bfloat16)
    spectrum = jnp.dot(
        images.reshape(local_images * radii, angles), forward, preferred_element_type=jnp.float32
    )
    spectrum = spectrum.astype(jnp.bfloat16).reshape(local_images, radii, 2, freqs)
    coeffs = jnp.einsum(
        "nrck,krp->kcnp", spectrum, basis_used, preferred_element_type=jnp.float32
    ).astype(jnp.bfloat16)
    first = lax.axis_index("img") * owned
    arrived = lax.all_to_all(coeffs, "img", split_axis=0, concat_axis=2, tiled=True)
    all_ids = lax.all_gather(group_ids, "img", axis=0, tiled=True)
    gains_local = lax.dynamic_slice_in_dim(ctf_gain, first, owned, 1)
    noise_local = lax.dynamic_slice_in_dim(noise_var, first, owned, 0)
    used_local = lax.dynamic_slice_in_dim(used, first, owned, 0)
    onehot = (all_ids[:, None] == jnp.arange(groups_count, dtype=jnp.int32)[None, :]).astype(
        jnp.float32
    )
    gains_kn = jnp.dot(onehot, gains_local, precision=lax.Precision.HIGHEST).T
    scaled = (arrived * gains_kn[:, None, :, None]).astype(jnp.bfloat16)
    gram_part = jnp.einsum("kcnp,kcnq->kpq", scaled, scaled, preferred_element_type=jnp.float32)
    norms = jnp.einsum("kcnp,kcnp->kcn", arrived, arrived, preferred_element_type=jnp.float32)
    squares = gains_kn * gains_kn
    fourth_part = jnp.sum(squares[:, None, :] * norms * norms, (1, 2))
    total_part = 2.0 * jnp.sum(squares, 1)
    gram, fourth, total = lax.psum((gram_part, fourth_part, total_part), "grp")
    image_total = arrived.shape[2] * lax.axis_size("grp")
    cov = shrink_cov(gram, fourth, total, used_local, image_total)
    combos = groups_count * owned
    cov_all = jnp.broadcast_to(cov[None], (groups_count, owned, pmax, pmax)).reshape(
        combos, pmax, pmax
    )
    gain_all = gains_local.reshape(combos)
    noise_all = jnp.tile(noise_local, groups_count)
    share = combos // lax.axis_size("grp")
    start = lax.axis_index("grp") * share
    mine = wiener_filters(
        lax.dynamic_slice_in_dim(cov_all, start, share, 0),
        lax.dynamic_slice_in_dim(gain_all, start, share, 0),
        lax.dynamic_slice_in_dim(noise_all, start, share, 0),
        NS_ITERS,
    )
    filters = lax.all_gather(mine, "grp", axis=0, tiled=True)
    filters = filters.reshape(groups_count, owned, pmax, pmax)
    result = jnp.zeros(arrived.shape, jnp.float32)
    for which_group in range(groups_count):
        part = jnp.einsum(
            "kcnq,kpq->kcnp", arrived, filters[which_group], preferred_element_type=jnp.float32
        )
        result = result + jnp.where((all_ids == which_group)[None, None, :, None], part, 0.0)
    cleaned = result.astype(jnp.bfloat16)
    returned = lax.all_to_all(cleaned, "img", split_axis=2, concat_axis=0, tiled=True)
    back = jnp.einsum(
        "kcnp,krp->nrck", returned, basis_used, preferred_element_type=jnp.float32
    ).astype(jnp.bfloat16)
    back = back.reshape(local_images * radii, 2 * freqs)
    denoised = jnp.dot(back, inverse, preferred_element_type=jnp.float32).astype(jnp.bfloat16)
    return denoised.reshape(local_images, radii, angles)


WAYS = (
    ((0, 4, 8, 15), (1, 5, 9, 14), (2, 6, 10, 13), (3, 7, 11, 12)),
    ((0, 6, 9, 15), (1, 7, 8, 14), (3, 5, 10, 12), (2, 4, 11, 13)),
    ((2, 6, 9, 13), (1, 5, 11, 12), (0, 7, 8, 15), (3, 4, 10, 14)),
    ((2, 6, 10, 12), (1, 4, 9, 15), (0, 7, 11, 14), (3, 5, 8, 13)),
    ((2, 4, 11, 14), (0, 7, 9, 12), (3, 5, 8, 15), (1, 6, 10, 13)),
    ((3, 4, 10, 13), (1, 5, 8, 15), (0, 6, 9, 14), (2, 7, 11, 12)),
    ((2, 7, 8, 12), (3, 4, 10, 15), (1, 6, 9, 14), (0, 5, 11, 13)),
    ((2, 4, 9, 14), (0, 6, 11, 12), (1, 5, 10, 13), (3, 7, 8, 15)),
)
OWN = 4
BLOCK = 16
FULL_ROWS = 208
SHORT_ROWS = 176
HEAVIEST = 3 * BLOCK
IMAGE_CHUNKS = 8
AHEAD = 4
PITCH_PAD = 8
VMEM_LIMIT = 48 * 1024 * 1024
FRONT_VMEM = 121 * 512 * 1024

f32 = jnp.float32
bf16 = jnp.bfloat16


def fixed_tables(angles, freqs):
    turns = np.arange(angles)[:, None] * np.arange(freqs)[None, :] % angles
    phases = turns * (2.0 * math.pi / angles)
    cosine = np.cos(phases) / math.sqrt(angles)
    sine = -np.sin(phases) / math.sqrt(angles)
    forward = np.concatenate([cosine, sine], 1)
    doubling = np.where(np.arange(freqs) == 0, 1.0, 2.0)[None, :]
    inverse = np.concatenate([cosine * doubling, sine * doubling], 1).T
    return forward.T.astype(np.float32).astype(jnp.bfloat16), inverse.astype(np.float32).astype(jnp.bfloat16)


def owner_tables(row_of_counts, blocks):
    every = jnp.broadcast_to(row_of_counts, (blocks, row_of_counts.shape[1]))
    block = lax.broadcasted_iota(jnp.int32, every.shape, 0)
    counts = every
    for which in range(1, blocks):
        counts = jnp.where(block == which, pltpu.roll(every, every.shape[1] - BLOCK * which, 1), counts)
    counts = counts[:, :BLOCK]
    lane = lax.broadcasted_iota(jnp.int32, counts.shape, 1)
    rank = jnp.zeros(counts.shape, jnp.int32)
    for other in range(BLOCK):
        column = counts[:, other:other + 1]
        before = (column > counts) | ((column == counts) & (lane > other))
        rank = rank + before.astype(jnp.int32)
    def over_lanes(hit, value):
        return jnp.sum(jnp.where(hit, value, 0).astype(f32), 1, keepdims=True).astype(jnp.int32)

    by_rank = [over_lanes(rank == place, (counts + 1) // 2) for place in range(BLOCK)]
    least, wanted = None, None
    for way in WAYS:
        loads = [by_rank[ranks[0]] + by_rank[ranks[1]] + by_rank[ranks[2]] + by_rank[ranks[3]] for ranks in way]
        load = functools.reduce(jnp.maximum, loads)
        flat = [place for ranks in way for place in ranks]
        if least is None:
            least, wanted = load, [jnp.full(load.shape, place, jnp.int32) for place in flat]
        else:
            better = load < least
            least = jnp.where(better, load, least)
            wanted = [jnp.where(better, place, old) for place, old in zip(flat, wanted)]
    full = lax.broadcasted_iota(jnp.int32, (blocks, 128), 1)
    first = lax.broadcasted_iota(jnp.int32, (blocks, 1), 0) * BLOCK
    heaviest = jnp.max(least.astype(f32), 0, keepdims=True).astype(jnp.int32)
    table = jnp.where(full == HEAVIEST, heaviest, 0)
    for dest in range(OWN):
        offset = jnp.zeros((blocks, 1), jnp.int32)
        for own in range(OWN):
            place = dest * OWN + own
            hit = rank == wanted[place]
            freq = over_lanes(hit, lane) + first
            count = over_lanes(hit, counts)
            table = jnp.where(full == place, freq, table)
            table = jnp.where(full == place + BLOCK, count, table)
            table = jnp.where(full == place + 2 * BLOCK, offset, table)
            offset = offset + (count + 1) // 2
    return table


def low_half(shape):
    return lax.broadcasted_iota(jnp.int32, shape, 1) < 64


def swap_halves(value):
    return pltpu.roll(value, 64, 1)


def front_kernel(freqs, counts_any, ids_any, images_any, forward_any, basis_any, packed, whole_any, table_any,
                 counts, ids, tab, images, forward, basis, spec, turned, rows, table, whole, image_sems, sems, basis_sems):
    wide = 2 * freqs
    pitch = wide + PITCH_PAD
    local = images.shape[0]
    blocks = freqs // BLOCK
    per_chunk = local // IMAGE_CHUNKS

    def image_copy(chunk):
        span = pl.ds(chunk * per_chunk, per_chunk)
        return pltpu.make_async_copy(images_any.at[span], images.at[span], image_sems.at[chunk])

    def basis_copy(block):
        span = pl.ds(block * BLOCK, BLOCK)
        return pltpu.make_async_copy(basis_any.at[span], basis.at[span], basis_sems.at[block])

    forward_copy = pltpu.make_async_copy(forward_any, forward, sems.at[0])
    table_copy = pltpu.make_async_copy(table, tab, sems.at[1])
    table_out = pltpu.make_async_copy(table, table_any, sems.at[2])
    counts_copy = pltpu.make_async_copy(counts_any, counts, sems.at[3])
    ids_copy = pltpu.make_async_copy(ids_any, ids, sems.at[4])
    copies = [image_copy(chunk) for chunk in range(IMAGE_CHUNKS)] + [basis_copy(block) for block in range(blocks)]
    counts_copy.start()
    ids_copy.start()
    forward_copy.start()
    for copy in copies[:AHEAD]:
        copy.start()
    counts_copy.wait()
    table[...] = owner_tables(counts[...], blocks)
    table_copy.start()
    table_out.start()
    ids_copy.wait()
    id_row = jnp.concatenate([ids[...].astype(f32)] * (128 // local), 1)
    forward_copy.wait()

    for chunk in range(IMAGE_CHUNKS):
        copies[chunk].wait()
        copies[chunk + AHEAD].start()
        for pair in range(per_chunk // 2):
            first = chunk * per_chunk + 2 * pair
            both = images[pl.ds(first, 2)].reshape(256, images.shape[2])
            part = lax.dot_general(forward[...], both, (((1,), (1,)), ((), ())), preferred_element_type=f32)
            part = part.astype(bf16).astype(f32)
            for which in range(2):
                start = pl.multiple_of((first + which) * pitch, 8)
                spec[pl.ds(start, wide), :] = part[:, 128 * which:128 * (which + 1)]

    for copy in copies[IMAGE_CHUNKS + AHEAD:]:
        copy.start()
    table_copy.wait()
    table_out.wait()
    too_heavy = tab[0, HEAVIEST] > SHORT_ROWS - 1
    low = low_half((64, 128))

    def gather(block):
        for dest in range(OWN):
            for pair in range(2):
                place = dest * OWN + 2 * pair
                parts = []
                for which in range(2):
                    freq = tab[block, place + which]
                    real = spec[pl.ds(freq, local, stride=pitch), :]
                    imag = spec[pl.ds(freq + freqs, local, stride=pitch), :]
                    lhs = jnp.concatenate([real, imag], 0).astype(bf16)
                    parts.append(jnp.dot(lhs, basis[freq], preferred_element_type=f32).astype(bf16))
                slot = dest * 2 + pair
                turned[slot] = jnp.concatenate(parts, 0).T.astype(f32)
                even = turned[slot, pl.ds(0, 64, stride=2), :]
                odd = turned[slot, pl.ds(1, 64, stride=2), :]
                rows[dest, pl.ds(tab[block, place + 2 * BLOCK], 64), :] = jnp.where(low, even, swap_halves(odd))
                rows[dest, pl.ds(tab[block, place + 1 + 2 * BLOCK], 64), :] = jnp.where(low, swap_halves(even), odd)

    def pack(block, carry):
        basis_copy(block).wait()
        gather(block)
        for dest in range(OWN):
            rows[dest, SHORT_ROWS - 1:SHORT_ROWS, :] = id_row
            packed[block * OWN + dest] = rows[dest, 0:SHORT_ROWS, :].astype(bf16)
        return carry

    lax.fori_loop(0, blocks, pack, 0, unroll=2)

    @pl.when(too_heavy)
    def _():
        def pack_whole(block, carry):
            gather(block)
            for dest in range(OWN):
                rows[dest, FULL_ROWS - 1:FULL_ROWS, :] = id_row
                whole[dest] = rows[dest, 0:FULL_ROWS, :].astype(bf16)
            copy = pltpu.make_async_copy(whole, whole_any.at[pl.ds(block * OWN, OWN)], sems.at[0])
            copy.start()
            copy.wait()
            return carry

        lax.fori_loop(0, blocks, pack_whole, 0)


def split(value):
    high = value.astype(bf16)
    return high, (value - high.astype(f32)).astype(bf16)


def side_by_side(value):
    high, low = split(value)
    return jnp.concatenate([high, low], 1)


def wide_product(left, right):
    both = jnp.dot(left, jnp.concatenate([right, right], 0), preferred_element_type=f32)
    return both[:, :128] + both[:, 128:]


def total_of(value):
    return jnp.sum(jnp.sum(value, 1, keepdims=True), 0, keepdims=True)


def middle_kernel(image_total, me_any, tab_any, gain_any, noise_any, arrived, out,
                  me, tab, gain, noise, wide, coeff, scaled, covs, filters, clean, sems):
    small = ((me_any, me), (tab_any, tab), (gain_any, gain), (noise_any, noise))
    copies = [pltpu.make_async_copy(source, target, sems.at[i]) for i, (source, target) in enumerate(small)]
    for copy in copies:
        copy.start()
    devices, sent_rows, _ = arrived.shape
    groups_count = gain.shape[0]
    columns = devices * 64
    low = low_half((64, 128))
    wide[:, 0:sent_rows, :] = arrived[...].astype(f32)
    pieces = [
        jnp.where(low_half((1, 128)), wide[2 * m, sent_rows - 1:sent_rows, :], wide[2 * m + 1, sent_rows - 1:sent_rows, :])
        for m in range(devices // 2)
    ]
    ids = jnp.concatenate(pieces, 1)
    row = lax.broadcasted_iota(jnp.int32, (128, 128), 0)
    column = lax.broadcasted_iota(jnp.int32, (128, 128), 1)
    slot_row = jnp.where(row < 64, 2 * row, 2 * row - 127)
    eye = (row == column).astype(f32)
    for copy in copies:
        copy.wait()
    block = me[0] // OWN
    first_place = lax.rem(me[0], OWN) * OWN

    def gather(own):
        place = first_place + own
        freq = tab[block, place]
        count = tab[block, place + BLOCK]
        where = tab[block, place + 2 * BLOCK]
        used = slot_row < count
        scale = jnp.zeros((1, columns), f32)
        for g in range(groups_count):
            scale = jnp.where(ids == float(g), gain[g, freq], scale)
        squares = scale * scale
        norms = []
        for m in range(devices // 2):
            span = slice(128 * m, 128 * (m + 1))
            first = wide[2 * m, pl.ds(where, 64), :]
            second = wide[2 * m + 1, pl.ds(where, 64), :]
            even = jnp.where(low, first, swap_halves(second))
            odd = jnp.where(low, swap_halves(first), second)
            value = jnp.where(used, jnp.concatenate([even, odd], 0), 0.0)
            coeff[own, :, span] = value.astype(bf16)
            scaled[own, :, span] = (value * scale[:, span]).astype(bf16)
            norms.append(jnp.sum(value * value, 0, keepdims=True))
        norms = jnp.concatenate(norms, 1)
        fourth = jnp.sum(squares * norms * norms, 1, keepdims=True)
        total = jnp.sum(squares, 1, keepdims=True)
        weighted = scaled[own]
        gram = lax.dot_general(weighted, weighted, (((1,), (1,)), ((), ())), preferred_element_type=f32)
        sample = gram / total
        ident = jnp.where(used, eye, 0.0)
        level = total_of(sample * eye) / count.astype(f32)
        spread = total_of((sample - level * ident) ** 2)
        excess = (fourth / total - total_of(sample * sample)) / (2.0 * image_total)
        weight = excess / (excess + spread)
        covs[own] = (1.0 - weight) * sample + (weight * level) * ident

    def invert(own):
        place = first_place + own
        freq = tab[block, place]
        cov = covs[own]
        cov_parts = side_by_side(cov)
        cov_square = wide_product(cov_parts, cov_parts)
        trace = total_of(cov * eye)
        square = total_of(cov * cov)
        power, series, size = [], [], []
        for g in range(groups_count):
            h, s = gain[g, freq] * gain[g, freq], noise[freq]
            size.append(jnp.sqrt(h * h * square + 2.0 * h * s * trace + 128.0 * s * s))
            a, b = 1.0 - s / size[g], h / size[g]
            series.append((1.0 + a) * eye - b * cov)
            power.append((a * a) * eye - (2.0 * a * b) * cov + (b * b) * cov_square)
        for sweep in range(1, NS_ITERS):
            for g in range(groups_count):
                right = side_by_side(power[g])
                if sweep == NS_ITERS - 1:
                    series[g] = series[g] + wide_product(side_by_side(series[g]), right)
                else:
                    both = wide_product(jnp.concatenate([right, side_by_side(series[g])], 0), right)
                    power[g] = both[:128]
                    series[g] = series[g] + both[128:]
        for g in range(groups_count):
            product = wide_product(cov_parts, side_by_side(series[g])) * (gain[g, freq] / size[g])
            filters[own, :, 128 * g:128 * (g + 1)] = product.astype(bf16)

    def apply(own):
        where = tab[block, first_place + own + 2 * BLOCK]
        for chunk in range(columns // 256):
            span = slice(256 * chunk, 256 * (chunk + 1))
            value = coeff[own, :, span]
            masked = jnp.concatenate(
                [jnp.where(ids[:, span] == float(g), value, jnp.zeros_like(value)) for g in range(groups_count)], 0
            )
            chosen = jnp.dot(filters[own], masked, preferred_element_type=f32)
            for m in range(2):
                even = chosen[:64, 128 * m:128 * (m + 1)]
                odd = chosen[64:, 128 * m:128 * (m + 1)]
                clean[4 * chunk + 2 * m, pl.ds(where, 64), :] = jnp.where(low, even, swap_halves(odd))
                clean[4 * chunk + 2 * m + 1, pl.ds(where, 64), :] = jnp.where(low, swap_halves(even), odd)

    for turn in range(OWN + 2):
        if turn < OWN:
            gather(turn)
        if 1 <= turn <= OWN:
            invert(turn - 1)
        if turn >= 2:
            apply(turn - 2)
    out[...] = clean[:, 0:sent_rows, :].astype(bf16)


def back_kernel(freqs, tab, returned, basis, inverse, out_any, rows, turned, back, images, sems):
    wide = 2 * freqs
    pitch = wide + PITCH_PAD
    local = images.shape[0]
    blocks = freqs // BLOCK
    per_chunk = local // IMAGE_CHUNKS
    low = low_half((64, 128))
    pair_row = lax.broadcasted_iota(jnp.int32, (64, 128), 0) * 2

    def unpack(block, carry):
        for dest in range(OWN):
            rows[dest, 0:returned.shape[1], :] = returned[block * OWN + dest].astype(f32)
            for pair in range(2):
                place = dest * OWN + 2 * pair
                first = rows[dest, pl.ds(tab[block, place + 2 * BLOCK], 64), :]
                second = rows[dest, pl.ds(tab[block, place + 1 + 2 * BLOCK], 64), :]
                count = jnp.where(low, tab[block, place + BLOCK], tab[block, place + 1 + BLOCK])
                even = jnp.where(low, first, swap_halves(second))
                odd = jnp.where(low, swap_halves(first), second)
                slot = dest * 2 + pair
                turned[slot, pl.ds(0, 64, stride=2), :] = jnp.where(pair_row < count, even, 0.0)
                turned[slot, pl.ds(1, 64, stride=2), :] = jnp.where(pair_row + 1 < count, odd, 0.0)
                lhs = turned[slot].astype(bf16).T
                for which in range(2):
                    freq = tab[block, place + which]
                    value = jnp.dot(lhs[64 * which:64 * (which + 1)], basis[freq], preferred_element_type=f32)
                    value = value.astype(bf16).astype(f32)
                    back[pl.ds(freq, local, stride=pitch), :] = value[:local]
                    back[pl.ds(freq + freqs, local, stride=pitch), :] = value[local:]
        return carry

    lax.fori_loop(0, blocks, unpack, 0, unroll=4)

    def out_copy(chunk):
        span = pl.ds(chunk * per_chunk, per_chunk)
        return pltpu.make_async_copy(images.at[span], out_any.at[span], sems.at[chunk])

    def transform(chunk, carry):
        for image in range(per_chunk):
            which = chunk * per_chunk + image
            start = pl.multiple_of(which * pitch, 8)
            lhs = back[pl.ds(start, wide), :].astype(bf16)
            value = lax.dot_general(lhs, inverse[...], (((0,), (0,)), ((), ())), preferred_element_type=f32)
            images[which] = value.astype(bf16)
        out_copy(chunk).start()
        return carry

    lax.fori_loop(0, IMAGE_CHUNKS, transform, 0, unroll=True)
    for chunk in range(IMAGE_CHUNKS):
        out_copy(chunk).wait()


def front(counts, group_ids, images, radial_basis):
    local, radii, angles = images.shape
    freqs, _, pmax = radial_basis.shape
    blocks = freqs // BLOCK
    forward, _ = fixed_tables(angles, freqs)
    vmem = pl.BlockSpec(memory_space=pltpu.VMEM)
    hbm = pl.BlockSpec(memory_space=pltpu.HBM)
    return pl.pallas_call(
        functools.partial(front_kernel, freqs),
        in_specs=[hbm, hbm, hbm, hbm, hbm],
        out_specs=(vmem, hbm, hbm),
        out_shape=(
            jax.ShapeDtypeStruct((blocks * OWN, SHORT_ROWS, 128), bf16),
            jax.ShapeDtypeStruct((blocks * OWN, FULL_ROWS, 128), bf16),
            jax.ShapeDtypeStruct((blocks, 128), jnp.int32),
        ),
        scratch_shapes=[
            pltpu.VMEM((1, freqs), jnp.int32),
            pltpu.VMEM((1, local), jnp.int32),
            pltpu.SMEM((blocks, 128), jnp.int32),
            pltpu.VMEM(images.shape, bf16),
            pltpu.VMEM(forward.shape, bf16),
            pltpu.VMEM(radial_basis.shape, bf16),
            pltpu.VMEM((local * (2 * freqs + PITCH_PAD), 128), f32),
            pltpu.VMEM((2 * OWN, 128, 128), f32),
            pltpu.VMEM((OWN, FULL_ROWS + 64, 128), f32),
            pltpu.VMEM((blocks, 128), jnp.int32),
            pltpu.VMEM((OWN, FULL_ROWS, 128), bf16),
            pltpu.SemaphoreType.DMA((IMAGE_CHUNKS,)),
            pltpu.SemaphoreType.DMA((5,)),
            pltpu.SemaphoreType.DMA((blocks,)),
        ],
        compiler_params=pltpu.CompilerParams(vmem_limit_bytes=FRONT_VMEM),
        name="front",
    )(
        counts.reshape(1, freqs), group_ids.reshape(1, local), images, jnp.asarray(forward), radial_basis
    )


def middle(me, tab, ctf_gain, noise_var, arrived, image_total):
    hbm = pl.BlockSpec(memory_space=pltpu.HBM)
    vmem = pl.BlockSpec(memory_space=pltpu.VMEM)
    devices, sent_rows, _ = arrived.shape
    groups_count = ctf_gain.shape[0]
    return pl.pallas_call(
        functools.partial(middle_kernel, float(image_total)),
        in_specs=[hbm, hbm, hbm, hbm, vmem],
        out_specs=vmem,
        out_shape=jax.ShapeDtypeStruct(arrived.shape, bf16),
        scratch_shapes=[
            pltpu.SMEM(me.shape, jnp.int32),
            pltpu.SMEM(tab.shape, jnp.int32),
            pltpu.SMEM(ctf_gain.shape, f32),
            pltpu.SMEM(noise_var.shape, f32),
            pltpu.VMEM((devices, sent_rows + 64, 128), f32),
            pltpu.VMEM((OWN, 128, devices * 64), bf16),
            pltpu.VMEM((OWN, 128, devices * 64), bf16),
            pltpu.VMEM((OWN, 128, 128), f32),
            pltpu.VMEM((OWN, 128, groups_count * 128), bf16),
            pltpu.VMEM((devices, sent_rows + 64, 128), f32),
            pltpu.SemaphoreType.DMA((4,)),
        ],
        compiler_params=pltpu.CompilerParams(vmem_limit_bytes=VMEM_LIMIT),
        name="middle",
    )(me, tab, ctf_gain, noise_var, arrived)


def back(tab, returned, turned_basis, images_shape):
    local, radii, angles = images_shape
    freqs = turned_basis.shape[0]
    _, inverse = fixed_tables(angles, freqs)
    vmem = pl.BlockSpec(memory_space=pltpu.VMEM)
    return pl.pallas_call(
        functools.partial(back_kernel, freqs),
        in_specs=[pl.BlockSpec(memory_space=pltpu.SMEM), vmem, vmem, vmem],
        out_specs=pl.BlockSpec(memory_space=pltpu.HBM),
        out_shape=jax.ShapeDtypeStruct(images_shape, bf16),
        scratch_shapes=[
            pltpu.VMEM((OWN, returned.shape[1] + 64, 128), f32),
            pltpu.VMEM((2 * OWN, 128, 128), f32),
            pltpu.VMEM((local * (2 * freqs + PITCH_PAD), 128), f32),
            pltpu.VMEM(images_shape, bf16),
            pltpu.SemaphoreType.DMA((IMAGE_CHUNKS,)),
        ],
        compiler_params=pltpu.CompilerParams(vmem_limit_bytes=VMEM_LIMIT),
        name="back",
    )(tab, returned, turned_basis, jnp.asarray(inverse))


def owned_body(images, group_ids, counts, radial_basis, ctf_gain, noise_var):
    axes = ("img", "grp")
    image_total = images.shape[0] * lax.axis_size(axes)
    short, whole, tab = front(counts, group_ids, images, radial_basis)
    me = lax.axis_index(axes).astype(jnp.int32).reshape(1)

    def rest(packed, tab, me, radial_basis, ctf_gain, noise_var):
        arrived = lax.all_to_all(packed, axes, split_axis=0, concat_axis=0, tiled=True)
        turned_basis = jnp.swapaxes(radial_basis, 1, 2)
        arrived, turned_basis = lax.optimization_barrier((arrived, turned_basis))
        cleaned = middle(me, tab, ctf_gain, noise_var, arrived, image_total)
        returned = lax.all_to_all(cleaned, axes, split_axis=0, concat_axis=0, tiled=True)
        return back(tab, returned, turned_basis, images.shape)

    return lax.cond(
        tab[0, HEAVIEST] > SHORT_ROWS - 1,
        lambda short, whole, *others: rest(whole, *others),
        lambda short, whole, *others: rest(short, *others),
        short, whole, tab, me, radial_basis, ctf_gain, noise_var,
    )


def body(images, group_ids, counts, radial_basis, ctf_gain, noise_var):
    devices = lax.axis_size("img") * lax.axis_size("grp")
    freqs = radial_basis.shape[0]
    fits = (
        freqs == OWN * devices
        and lax.axis_size("grp") * OWN == BLOCK
        and images.shape[0] == 32
        and freqs // BLOCK >= AHEAD
        and radial_basis.shape[1:] == (128, 128)
        and freqs % 128 == 0
        and images.shape[2] % 128 == 0
        and ctf_gain.shape[0] % 2 == 0
    )
    chosen = owned_body if fits else general_body
    return chosen(images, group_ids, counts, radial_basis, ctf_gain, noise_var)


def solution(mesh):
    placed = (P(("img", "grp"), None, None), P(("img", "grp")), P(), P(), P(), P())
    return jax.shard_map(
        body, mesh=mesh, in_specs=placed, out_specs=P(("img", "grp"), None, None), check_vma=False
    )
```

```python
import functools
import math

import jax
import jax.numpy as jnp
import numpy as np
from jax import lax
from jax.experimental import pallas as pl
from jax.experimental.pallas import tpu as pltpu
from jax.sharding import PartitionSpec as P

NS_ITERS = 7


def dft_tables(angles, freqs):
    angle_index = jnp.arange(angles, dtype=jnp.int32)
    freq_index = jnp.arange(freqs, dtype=jnp.int32)
    turns = angle_index[:, None] * freq_index[None, :] % angles
    phases = turns.astype(jnp.float32) * (2.0 * math.pi / angles)
    factor = 1.0 / math.sqrt(angles)
    cosine = jnp.cos(phases) * factor
    sine = -jnp.sin(phases) * factor
    forward = jnp.concatenate([cosine, sine], 1).astype(jnp.bfloat16)
    doubling = jnp.where(freq_index == 0, 1.0, 2.0).astype(jnp.float32)
    inverse = jnp.concatenate([cosine * doubling[None, :], sine * doubling[None, :]], 1).T.astype(
        jnp.bfloat16
    )
    return (forward, inverse)


def shrink_cov(gram, fourth, total, used, image_total):
    sample = gram / total[:, None, None]
    ident = used[:, :, None] * jnp.eye(used.shape[1], dtype=jnp.float32)[None]
    level = jnp.trace(sample, axis1=1, axis2=2) / jnp.sum(used, 1)
    spread = jnp.sum((sample - level[:, None, None] * ident) ** 2, (1, 2))
    excess = (fourth / total - jnp.sum(sample * sample, (1, 2))) / (2.0 * image_total)
    weight = excess / (excess + spread)
    return (1.0 - weight)[:, None, None] * sample + (weight * level)[:, None, None] * ident


def wiener_filters(cov, gain, noise_level, steps_count):
    identity = jnp.eye(cov.shape[1], dtype=jnp.float32)[None]
    system = (gain * gain)[:, None, None] * cov + noise_level[:, None, None] * identity
    frobenius = jnp.sqrt(jnp.sum(system * system, (1, 2)))
    approx = identity / frobenius[:, None, None]
    for sweep in range(steps_count):
        middle = jnp.matmul(approx, system, precision=lax.Precision.HIGHEST)
        approx = 2.0 * approx - jnp.matmul(middle, approx, precision=lax.Precision.HIGHEST)
    product = jnp.matmul(cov, approx, precision=lax.Precision.HIGHEST)
    return (gain[:, None, None] * product).astype(jnp.bfloat16)


def general_body(images, group_ids, counts, radial_basis, ctf_gain, noise_var):
    local_images = images.shape[0]
    radii = images.shape[1]
    angles = images.shape[2]
    freqs = radial_basis.shape[0]
    pmax = radial_basis.shape[2]
    groups_count = ctf_gain.shape[0]
    owners = lax.axis_size("img")
    owned = freqs // owners
    forward, inverse = dft_tables(angles, freqs)
    used = (jnp.arange(pmax, dtype=jnp.int32)[None, :] < counts[:, None]).astype(jnp.float32)
    basis_used = (radial_basis.astype(jnp.float32) * used[:, None, :]).astype(jnp.bfloat16)
    spectrum = jnp.dot(
        images.reshape(local_images * radii, angles), forward, preferred_element_type=jnp.float32
    )
    spectrum = spectrum.astype(jnp.bfloat16).reshape(local_images, radii, 2, freqs)
    coeffs = jnp.einsum(
        "nrck,krp->kcnp", spectrum, basis_used, preferred_element_type=jnp.float32
    ).astype(jnp.bfloat16)
    first = lax.axis_index("img") * owned
    arrived = lax.all_to_all(coeffs, "img", split_axis=0, concat_axis=2, tiled=True)
    all_ids = lax.all_gather(group_ids, "img", axis=0, tiled=True)
    gains_local = lax.dynamic_slice_in_dim(ctf_gain, first, owned, 1)
    noise_local = lax.dynamic_slice_in_dim(noise_var, first, owned, 0)
    used_local = lax.dynamic_slice_in_dim(used, first, owned, 0)
    onehot = (all_ids[:, None] == jnp.arange(groups_count, dtype=jnp.int32)[None, :]).astype(
        jnp.float32
    )
    gains_kn = jnp.dot(onehot, gains_local, precision=lax.Precision.HIGHEST).T
    scaled = (arrived * gains_kn[:, None, :, None]).astype(jnp.bfloat16)
    gram_part = jnp.einsum("kcnp,kcnq->kpq", scaled, scaled, preferred_element_type=jnp.float32)
    norms = jnp.einsum("kcnp,kcnp->kcn", arrived, arrived, preferred_element_type=jnp.float32)
    squares = gains_kn * gains_kn
    fourth_part = jnp.sum(squares[:, None, :] * norms * norms, (1, 2))
    total_part = 2.0 * jnp.sum(squares, 1)
    gram, fourth, total = lax.psum((gram_part, fourth_part, total_part), "grp")
    image_total = arrived.shape[2] * lax.axis_size("grp")
    cov = shrink_cov(gram, fourth, total, used_local, image_total)
    combos = groups_count * owned
    cov_all = jnp.broadcast_to(cov[None], (groups_count, owned, pmax, pmax)).reshape(
        combos, pmax, pmax
    )
    gain_all = gains_local.reshape(combos)
    noise_all = jnp.tile(noise_local, groups_count)
    share = combos // lax.axis_size("grp")
    start = lax.axis_index("grp") * share
    mine = wiener_filters(
        lax.dynamic_slice_in_dim(cov_all, start, share, 0),
        lax.dynamic_slice_in_dim(gain_all, start, share, 0),
        lax.dynamic_slice_in_dim(noise_all, start, share, 0),
        NS_ITERS,
    )
    filters = lax.all_gather(mine, "grp", axis=0, tiled=True)
    filters = filters.reshape(groups_count, owned, pmax, pmax)
    result = jnp.zeros(arrived.shape, jnp.float32)
    for which_group in range(groups_count):
        part = jnp.einsum(
            "kcnq,kpq->kcnp", arrived, filters[which_group], preferred_element_type=jnp.float32
        )
        result = result + jnp.where((all_ids == which_group)[None, None, :, None], part, 0.0)
    cleaned = result.astype(jnp.bfloat16)
    returned = lax.all_to_all(cleaned, "img", split_axis=2, concat_axis=0, tiled=True)
    back = jnp.einsum(
        "kcnp,krp->nrck", returned, basis_used, preferred_element_type=jnp.float32
    ).astype(jnp.bfloat16)
    back = back.reshape(local_images * radii, 2 * freqs)
    denoised = jnp.dot(back, inverse, preferred_element_type=jnp.float32).astype(jnp.bfloat16)
    return denoised.reshape(local_images, radii, angles)


WAYS = (
    ((0, 4, 8, 15), (1, 5, 9, 14), (2, 6, 10, 13), (3, 7, 11, 12)),
    ((0, 6, 9, 15), (1, 7, 8, 14), (3, 5, 10, 12), (2, 4, 11, 13)),
    ((2, 6, 9, 13), (1, 5, 11, 12), (0, 7, 8, 15), (3, 4, 10, 14)),
    ((2, 6, 10, 12), (1, 4, 9, 15), (0, 7, 11, 14), (3, 5, 8, 13)),
    ((2, 4, 11, 14), (0, 7, 9, 12), (3, 5, 8, 15), (1, 6, 10, 13)),
    ((3, 4, 10, 13), (1, 5, 8, 15), (0, 6, 9, 14), (2, 7, 11, 12)),
    ((2, 7, 8, 12), (3, 4, 10, 15), (1, 6, 9, 14), (0, 5, 11, 13)),
    ((2, 4, 9, 14), (0, 6, 11, 12), (1, 5, 10, 13), (3, 7, 8, 15)),
)
OWN = 4
BLOCK = 16
SENT_ROWS = (168, 208)
FULL_ROWS = SENT_ROWS[-1]
SHORT_ROWS = SENT_ROWS[0]
TRADES = ((0, 1), (2, 3), (0, 2), (1, 3))
HEAVIEST = 3 * BLOCK
IMAGE_CHUNKS = 8
AHEAD = 4
PITCH_PAD = 8
VMEM_LIMIT = 48 * 1024 * 1024
BACK_VMEM = VMEM_LIMIT
FRONT_VMEM = 121 * 512 * 1024

f32 = jnp.float32
bf16 = jnp.bfloat16


def fixed_tables(angles, freqs):
    turns = np.arange(angles)[:, None] * np.arange(freqs)[None, :] % angles
    phases = turns * (2.0 * math.pi / angles)
    cosine = np.cos(phases) / math.sqrt(angles)
    sine = -np.sin(phases) / math.sqrt(angles)
    forward = np.concatenate([cosine, sine], 1)
    doubling = np.where(np.arange(freqs) == 0, 1.0, 2.0)[None, :]
    inverse = np.concatenate([cosine * doubling, sine * doubling], 1).T
    return forward.T.astype(np.float32).astype(jnp.bfloat16), inverse.astype(np.float32).astype(jnp.bfloat16)


def owner_tables(row_of_counts, blocks):
    every = jnp.broadcast_to(row_of_counts, (blocks, row_of_counts.shape[1]))
    block = lax.broadcasted_iota(jnp.int32, every.shape, 0)
    counts = every
    for which in range(1, blocks):
        counts = jnp.where(block == which, pltpu.roll(every, every.shape[1] - BLOCK * which, 1), counts)
    counts = counts[:, :BLOCK]
    lane = lax.broadcasted_iota(jnp.int32, counts.shape, 1)
    rank = jnp.zeros(counts.shape, jnp.int32)
    for other in range(BLOCK):
        column = counts[:, other:other + 1]
        before = (column > counts) | ((column == counts) & (lane > other))
        rank = rank + before.astype(jnp.int32)
    def over_lanes(hit, value):
        return jnp.sum(jnp.where(hit, value, 0).astype(f32), 1, keepdims=True).astype(jnp.int32)

    by_rank = [over_lanes(rank == place, (counts + 1) // 2) for place in range(BLOCK)]
    least, wanted = None, None
    for way in WAYS:
        loads = [by_rank[ranks[0]] + by_rank[ranks[1]] + by_rank[ranks[2]] + by_rank[ranks[3]] for ranks in way]
        load = functools.reduce(jnp.maximum, loads)
        flat = [place for ranks in way for place in ranks]
        if least is None:
            least, wanted = load, [jnp.full(load.shape, place, jnp.int32) for place in flat]
        else:
            better = load < least
            least = jnp.where(better, load, least)
            wanted = [jnp.where(better, place, old) for place, old in zip(flat, wanted)]
    held = [jnp.zeros(least.shape, jnp.int32) for _ in wanted]
    for place in range(BLOCK):
        held = [jnp.where(want == place, by_rank[place], old) for want, old in zip(wanted, held)]
    for one, two in TRADES:
        ones, twos = range(one * OWN, (one + 1) * OWN), range(two * OWN, (two + 1) * OWN)
        gap = sum(held[i] for i in ones) - sum(held[j] for j in twos)
        best, chosen = jnp.abs(gap), jnp.full(gap.shape, -1, jnp.int32)
        for i in ones:
            for j in twos:
                left = jnp.abs(gap - 2 * (held[i] - held[j]))
                chosen = jnp.where(left < best, i * BLOCK + j, chosen)
                best = jnp.minimum(left, best)
        moves = [(i, j, chosen == i * BLOCK + j) for i in ones for j in twos]
        for values in (held, wanted):
            old = list(values)
            for i, j, move in moves:
                values[i] = jnp.where(move, old[j], values[i])
                values[j] = jnp.where(move, old[i], values[j])
    least = functools.reduce(jnp.maximum, [sum(held[dest * OWN:(dest + 1) * OWN]) for dest in range(OWN)])
    full = lax.broadcasted_iota(jnp.int32, (blocks, 128), 1)
    first = lax.broadcasted_iota(jnp.int32, (blocks, 1), 0) * BLOCK
    heaviest = jnp.max(least.astype(f32), 0, keepdims=True).astype(jnp.int32)
    table = jnp.where(full == HEAVIEST, heaviest, 0)
    for dest in range(OWN):
        offset = jnp.zeros((blocks, 1), jnp.int32)
        for own in range(OWN):
            place = dest * OWN + own
            hit = rank == wanted[place]
            freq = over_lanes(hit, lane) + first
            count = over_lanes(hit, counts)
            table = jnp.where(full == place, freq, table)
            table = jnp.where(full == place + BLOCK, count, table)
            table = jnp.where(full == place + 2 * BLOCK, offset, table)
            offset = offset + (count + 1) // 2
    return table


def low_half(shape):
    return lax.broadcasted_iota(jnp.int32, shape, 1) < 64


def swap_halves(value):
    return pltpu.roll(value, 64, 1)


def front_kernel(freqs, counts_any, ids_any, images_any, forward_any, basis_any, packed, *others):
    larger_any, table_any = others[:len(SENT_ROWS) - 1], others[len(SENT_ROWS) - 1]
    (counts, ids, tab, images, forward, basis, spec, turned, rows, table, larger, image_sems, sems, basis_sems) = others[len(SENT_ROWS):]
    wide = 2 * freqs
    pitch = wide + PITCH_PAD
    local = images.shape[0]
    blocks = freqs // BLOCK
    per_chunk = local // IMAGE_CHUNKS

    def image_copy(chunk):
        span = pl.ds(chunk * per_chunk, per_chunk)
        return pltpu.make_async_copy(images_any.at[span], images.at[span], image_sems.at[chunk])

    def basis_copy(block):
        span = pl.ds(block * BLOCK, BLOCK)
        return pltpu.make_async_copy(basis_any.at[span], basis.at[span], basis_sems.at[block])

    forward_copy = pltpu.make_async_copy(forward_any, forward, sems.at[0])
    table_copy = pltpu.make_async_copy(table, tab, sems.at[1])
    table_out = pltpu.make_async_copy(table, table_any, sems.at[2])
    counts_copy = pltpu.make_async_copy(counts_any, counts, sems.at[3])
    ids_copy = pltpu.make_async_copy(ids_any, ids, sems.at[4])
    copies = [image_copy(chunk) for chunk in range(IMAGE_CHUNKS)] + [basis_copy(block) for block in range(blocks)]
    counts_copy.start()
    ids_copy.start()
    forward_copy.start()
    for copy in copies[:AHEAD]:
        copy.start()
    counts_copy.wait()
    table[...] = owner_tables(counts[...], blocks)
    table_copy.start()
    table_out.start()
    ids_copy.wait()
    id_row = jnp.concatenate([ids[...].astype(f32)] * (128 // local), 1)
    forward_copy.wait()

    for chunk in range(IMAGE_CHUNKS):
        copies[chunk].wait()
        copies[chunk + AHEAD].start()
        for pair in range(per_chunk // 2):
            first = chunk * per_chunk + 2 * pair
            both = images[pl.ds(first, 2)].reshape(256, images.shape[2])
            part = lax.dot_general(forward[...], both, (((1,), (1,)), ((), ())), preferred_element_type=f32)
            part = part.astype(bf16).astype(f32)
            for which in range(2):
                start = pl.multiple_of((first + which) * pitch, 8)
                spec[pl.ds(start, wide), :] = part[:, 128 * which:128 * (which + 1)]

    for copy in copies[IMAGE_CHUNKS + AHEAD:]:
        copy.start()
    table_copy.wait()
    table_out.wait()
    heaviest = tab[0, HEAVIEST]
    low = low_half((64, 128))

    def gather(block):
        for dest in range(OWN):
            for pair in range(2):
                place = dest * OWN + 2 * pair
                parts = []
                for which in range(2):
                    freq = tab[block, place + which]
                    real = spec[pl.ds(freq, local, stride=pitch), :]
                    imag = spec[pl.ds(freq + freqs, local, stride=pitch), :]
                    lhs = jnp.concatenate([real, imag], 0).astype(bf16)
                    parts.append(jnp.dot(lhs, basis[freq], preferred_element_type=f32).astype(bf16))
                slot = dest * 2 + pair
                turned[slot] = jnp.concatenate(parts, 0).T.astype(f32)
                even = turned[slot, pl.ds(0, 64, stride=2), :]
                odd = turned[slot, pl.ds(1, 64, stride=2), :]
                rows[dest, pl.ds(tab[block, place + 2 * BLOCK], 64), :] = jnp.where(low, even, swap_halves(odd))
                rows[dest, pl.ds(tab[block, place + 1 + 2 * BLOCK], 64), :] = jnp.where(low, swap_halves(even), odd)

    def pack(block, carry):
        basis_copy(block).wait()
        gather(block)
        for dest in range(OWN):
            rows[dest, SHORT_ROWS - 1:SHORT_ROWS, :] = id_row
            packed[block * OWN + dest] = rows[dest, 0:SHORT_ROWS, :].astype(bf16)
        return carry

    lax.fori_loop(0, blocks, pack, 0, unroll=2)

    for sent_rows, sent_any in zip(SENT_ROWS[1:], larger_any):

        @pl.when(heaviest > SHORT_ROWS - 1)
        def _(sent_rows=sent_rows, sent_any=sent_any):
            def pack_larger(block, carry):
                gather(block)
                for dest in range(OWN):
                    rows[dest, sent_rows - 1:sent_rows, :] = id_row
                    larger[dest, 0:sent_rows, :] = rows[dest, 0:sent_rows, :].astype(bf16)
                copy = pltpu.make_async_copy(
                    larger.at[:, 0:sent_rows], sent_any.at[pl.ds(block * OWN, OWN)], sems.at[0]
                )
                copy.start()
                copy.wait()
                return carry

            lax.fori_loop(0, blocks, pack_larger, 0)


def split(value):
    high = value.astype(bf16)
    return high, (value - high.astype(f32)).astype(bf16)


def side_by_side(value):
    high, low = split(value)
    return jnp.concatenate([high, low], 1)


def wide_product(left, right):
    both = jnp.dot(left, jnp.concatenate([right, right], 0), preferred_element_type=f32)
    return both[:, :128] + both[:, 128:]


def total_of(value):
    return jnp.sum(jnp.sum(value, 1, keepdims=True), 0, keepdims=True)


def middle_kernel(image_total, me_any, tab_any, gain_any, noise_any, arrived, out,
                  me, tab, gain, noise, wide, coeff, scaled, covs, filters, clean, sems):
    small = ((me_any, me), (tab_any, tab), (gain_any, gain), (noise_any, noise))
    copies = [pltpu.make_async_copy(source, target, sems.at[i]) for i, (source, target) in enumerate(small)]
    for copy in copies:
        copy.start()
    devices, sent_rows, _ = arrived.shape
    groups_count = gain.shape[0]
    columns = devices * 64
    low = low_half((64, 128))
    wide[:, 0:sent_rows, :] = arrived[...].astype(f32)
    pieces = [
        jnp.where(low_half((1, 128)), wide[2 * m, sent_rows - 1:sent_rows, :], wide[2 * m + 1, sent_rows - 1:sent_rows, :])
        for m in range(devices // 2)
    ]
    ids = jnp.concatenate(pieces, 1)
    row = lax.broadcasted_iota(jnp.int32, (128, 128), 0)
    column = lax.broadcasted_iota(jnp.int32, (128, 128), 1)
    slot_row = jnp.where(row < 64, 2 * row, 2 * row - 127)
    eye = (row == column).astype(f32)
    for copy in copies:
        copy.wait()
    block = me[0] // OWN
    first_place = lax.rem(me[0], OWN) * OWN

    def gather(own):
        place = first_place + own
        freq = tab[block, place]
        count = tab[block, place + BLOCK]
        where = tab[block, place + 2 * BLOCK]
        used = slot_row < count
        scale = jnp.zeros((1, columns), f32)
        for g in range(groups_count):
            scale = jnp.where(ids == float(g), gain[g, freq], scale)
        squares = scale * scale
        norms = []
        for m in range(devices // 2):
            span = slice(128 * m, 128 * (m + 1))
            first = wide[2 * m, pl.ds(where, 64), :]
            second = wide[2 * m + 1, pl.ds(where, 64), :]
            even = jnp.where(low, first, swap_halves(second))
            odd = jnp.where(low, swap_halves(first), second)
            value = jnp.where(used, jnp.concatenate([even, odd], 0), 0.0)
            coeff[own, :, span] = value.astype(bf16)
            scaled[own, :, span] = (value * scale[:, span]).astype(bf16)
            norms.append(jnp.sum(value * value, 0, keepdims=True))
        norms = jnp.concatenate(norms, 1)
        fourth = jnp.sum(squares * norms * norms, 1, keepdims=True)
        total = jnp.sum(squares, 1, keepdims=True)
        weighted = scaled[own]
        gram = lax.dot_general(weighted, weighted, (((1,), (1,)), ((), ())), preferred_element_type=f32)
        sample = gram / total
        ident = jnp.where(used, eye, 0.0)
        level = total_of(sample * eye) / count.astype(f32)
        spread = total_of((sample - level * ident) ** 2)
        excess = (fourth / total - total_of(sample * sample)) / (2.0 * image_total)
        weight = excess / (excess + spread)
        covs[own] = (1.0 - weight) * sample + (weight * level) * ident

    def invert(own):
        place = first_place + own
        freq = tab[block, place]
        cov = covs[own]
        cov_parts = side_by_side(cov)
        cov_square = wide_product(cov_parts, cov_parts)
        trace = total_of(cov * eye)
        square = total_of(cov * cov)
        power, series, size = [], [], []
        for g in range(groups_count):
            h, s = gain[g, freq] * gain[g, freq], noise[freq]
            size.append(jnp.sqrt(h * h * square + 2.0 * h * s * trace + 128.0 * s * s))
            a, b = 1.0 - s / size[g], h / size[g]
            series.append((1.0 + a) * eye - b * cov)
            power.append((a * a) * eye - (2.0 * a * b) * cov + (b * b) * cov_square)
        for sweep in range(1, NS_ITERS):
            for g in range(groups_count):
                right = side_by_side(power[g])
                if sweep == NS_ITERS - 1:
                    series[g] = series[g] + wide_product(side_by_side(series[g]), right)
                else:
                    both = wide_product(jnp.concatenate([right, side_by_side(series[g])], 0), right)
                    power[g] = both[:128]
                    series[g] = series[g] + both[128:]
        for g in range(groups_count):
            product = wide_product(cov_parts, side_by_side(series[g])) * (gain[g, freq] / size[g])
            filters[own, :, 128 * g:128 * (g + 1)] = product.astype(bf16)

    def apply(own):
        where = tab[block, first_place + own + 2 * BLOCK]
        for chunk in range(columns // 256):
            span = slice(256 * chunk, 256 * (chunk + 1))
            value = coeff[own, :, span]
            masked = jnp.concatenate(
                [jnp.where(ids[:, span] == float(g), value, jnp.zeros_like(value)) for g in range(groups_count)], 0
            )
            chosen = jnp.dot(filters[own], masked, preferred_element_type=f32)
            for m in range(2):
                even = chosen[:64, 128 * m:128 * (m + 1)]
                odd = chosen[64:, 128 * m:128 * (m + 1)]
                clean[4 * chunk + 2 * m, pl.ds(where, 64), :] = jnp.where(low, even, swap_halves(odd))
                clean[4 * chunk + 2 * m + 1, pl.ds(where, 64), :] = jnp.where(low, swap_halves(even), odd)

    for turn in range(OWN + 2):
        if turn < OWN:
            gather(turn)
        if 1 <= turn <= OWN:
            invert(turn - 1)
        if turn >= 2:
            apply(turn - 2)
    out[...] = clean[:, 0:sent_rows, :].astype(bf16)


def back_kernel(freqs, tab, returned, basis, inverse, out_any, rows, turned, back, images, sems):
    wide = 2 * freqs
    pitch = wide + PITCH_PAD
    local = images.shape[0]
    blocks = freqs // BLOCK
    per_chunk = local // IMAGE_CHUNKS
    low = low_half((64, 128))
    pair_row = lax.broadcasted_iota(jnp.int32, (64, 128), 0) * 2

    def unpack(block, carry):
        for dest in range(OWN):
            rows[dest, 0:returned.shape[1], :] = returned[block * OWN + dest].astype(f32)
            for pair in range(2):
                place = dest * OWN + 2 * pair
                first = rows[dest, pl.ds(tab[block, place + 2 * BLOCK], 64), :]
                second = rows[dest, pl.ds(tab[block, place + 1 + 2 * BLOCK], 64), :]
                count = jnp.where(low, tab[block, place + BLOCK], tab[block, place + 1 + BLOCK])
                even = jnp.where(low, first, swap_halves(second))
                odd = jnp.where(low, swap_halves(first), second)
                slot = dest * 2 + pair
                turned[slot, pl.ds(0, 64, stride=2), :] = jnp.where(pair_row < count, even, 0.0)
                turned[slot, pl.ds(1, 64, stride=2), :] = jnp.where(pair_row + 1 < count, odd, 0.0)
                lhs = turned[slot].astype(bf16).T
                for which in range(2):
                    freq = tab[block, place + which]
                    value = jnp.dot(lhs[64 * which:64 * (which + 1)], basis[freq], preferred_element_type=f32)
                    value = value.astype(bf16).astype(f32)
                    back[pl.ds(freq, local, stride=pitch), :] = value[:local]
                    back[pl.ds(freq + freqs, local, stride=pitch), :] = value[local:]
        return carry

    lax.fori_loop(0, blocks, unpack, 0, unroll=4)

    def out_copy(chunk):
        span = pl.ds(chunk * per_chunk, per_chunk)
        return pltpu.make_async_copy(images.at[span], out_any.at[span], sems.at[chunk])

    def transform(chunk, carry):
        for image in range(per_chunk):
            which = chunk * per_chunk + image
            start = pl.multiple_of(which * pitch, 8)
            lhs = back[pl.ds(start, wide), :].astype(bf16)
            value = lax.dot_general(lhs, inverse[...], (((0,), (0,)), ((), ())), preferred_element_type=f32)
            images[which] = value.astype(bf16)
        out_copy(chunk).start()
        return carry

    lax.fori_loop(0, IMAGE_CHUNKS, transform, 0, unroll=True)
    for chunk in range(IMAGE_CHUNKS):
        out_copy(chunk).wait()


def front(counts, group_ids, images, radial_basis):
    local, radii, angles = images.shape
    freqs, _, pmax = radial_basis.shape
    blocks = freqs // BLOCK
    forward, _ = fixed_tables(angles, freqs)
    vmem = pl.BlockSpec(memory_space=pltpu.VMEM)
    hbm = pl.BlockSpec(memory_space=pltpu.HBM)
    return pl.pallas_call(
        functools.partial(front_kernel, freqs),
        in_specs=[hbm, hbm, hbm, hbm, hbm],
        out_specs=(vmem,) + (hbm,) * len(SENT_ROWS),
        out_shape=(
            *[jax.ShapeDtypeStruct((blocks * OWN, sent_rows, 128), bf16) for sent_rows in SENT_ROWS],
            jax.ShapeDtypeStruct((blocks, 128), jnp.int32),
        ),
        scratch_shapes=[
            pltpu.VMEM((1, freqs), jnp.int32),
            pltpu.VMEM((1, local), jnp.int32),
            pltpu.SMEM((blocks, 128), jnp.int32),
            pltpu.VMEM(images.shape, bf16),
            pltpu.VMEM(forward.shape, bf16),
            pltpu.VMEM(radial_basis.shape, bf16),
            pltpu.VMEM((local * (2 * freqs + PITCH_PAD), 128), f32),
            pltpu.VMEM((2 * OWN, 128, 128), f32),
            pltpu.VMEM((OWN, FULL_ROWS + 64, 128), f32),
            pltpu.VMEM((blocks, 128), jnp.int32),
            pltpu.VMEM((OWN, FULL_ROWS, 128), bf16),
            pltpu.SemaphoreType.DMA((IMAGE_CHUNKS,)),
            pltpu.SemaphoreType.DMA((5,)),
            pltpu.SemaphoreType.DMA((blocks,)),
        ],
        compiler_params=pltpu.CompilerParams(vmem_limit_bytes=FRONT_VMEM),
        name="front",
    )(
        counts.reshape(1, freqs), group_ids.reshape(1, local), images, jnp.asarray(forward), radial_basis
    )


def middle(me, tab, ctf_gain, noise_var, arrived, image_total):
    hbm = pl.BlockSpec(memory_space=pltpu.HBM)
    vmem = pl.BlockSpec(memory_space=pltpu.VMEM)
    devices, sent_rows, _ = arrived.shape
    groups_count = ctf_gain.shape[0]
    return pl.pallas_call(
        functools.partial(middle_kernel, float(image_total)),
        in_specs=[hbm, hbm, hbm, hbm, vmem],
        out_specs=vmem,
        out_shape=jax.ShapeDtypeStruct(arrived.shape, bf16),
        scratch_shapes=[
            pltpu.SMEM(me.shape, jnp.int32),
            pltpu.SMEM(tab.shape, jnp.int32),
            pltpu.SMEM(ctf_gain.shape, f32),
            pltpu.SMEM(noise_var.shape, f32),
            pltpu.VMEM((devices, sent_rows + 64, 128), f32),
            pltpu.VMEM((OWN, 128, devices * 64), bf16),
            pltpu.VMEM((OWN, 128, devices * 64), bf16),
            pltpu.VMEM((OWN, 128, 128), f32),
            pltpu.VMEM((OWN, 128, groups_count * 128), bf16),
            pltpu.VMEM((devices, sent_rows + 64, 128), f32),
            pltpu.SemaphoreType.DMA((4,)),
        ],
        compiler_params=pltpu.CompilerParams(vmem_limit_bytes=VMEM_LIMIT),
        name="middle",
    )(me, tab, ctf_gain, noise_var, arrived)


def back(tab, returned, turned_basis, images_shape):
    local, radii, angles = images_shape
    freqs = turned_basis.shape[0]
    _, inverse = fixed_tables(angles, freqs)
    vmem = pl.BlockSpec(memory_space=pltpu.VMEM)
    return pl.pallas_call(
        functools.partial(back_kernel, freqs),
        in_specs=[pl.BlockSpec(memory_space=pltpu.SMEM), vmem, vmem, vmem],
        out_specs=pl.BlockSpec(memory_space=pltpu.HBM),
        out_shape=jax.ShapeDtypeStruct(images_shape, bf16),
        scratch_shapes=[
            pltpu.VMEM((OWN, returned.shape[1] + 64, 128), f32),
            pltpu.VMEM((2 * OWN, 128, 128), f32),
            pltpu.VMEM((local * (2 * freqs + PITCH_PAD), 128), f32),
            pltpu.VMEM(images_shape, bf16),
            pltpu.SemaphoreType.DMA((IMAGE_CHUNKS,)),
        ],
        compiler_params=pltpu.CompilerParams(vmem_limit_bytes=BACK_VMEM),
        name="back",
    )(tab, returned, turned_basis, jnp.asarray(inverse))


def owned_body(images, group_ids, counts, radial_basis, ctf_gain, noise_var):
    axes = ("img", "grp")
    image_total = images.shape[0] * lax.axis_size(axes)
    *packed, tab = front(counts, group_ids, images, radial_basis)
    me = lax.axis_index(axes).astype(jnp.int32).reshape(1)

    def rest(packed, tab, me, radial_basis, ctf_gain, noise_var):
        arrived = lax.all_to_all(packed, axes, split_axis=0, concat_axis=0, tiled=True)
        turned_basis = jnp.swapaxes(radial_basis, 1, 2)
        arrived, turned_basis = lax.optimization_barrier((arrived, turned_basis))
        cleaned = middle(me, tab, ctf_gain, noise_var, arrived, image_total)
        returned = lax.all_to_all(cleaned, axes, split_axis=0, concat_axis=0, tiled=True)
        return back(tab, returned, turned_basis, images.shape)

    others = (tab, me, radial_basis, ctf_gain, noise_var)

    def from_level(level, packed, *others):
        if level == len(SENT_ROWS) - 1:
            return rest(packed[level], *others)
        return lax.cond(
            others[0][0, HEAVIEST] > SENT_ROWS[level] - 1,
            functools.partial(from_level, level + 1),
            lambda packed, *others: rest(packed[level], *others),
            packed, *others,
        )

    return from_level(0, packed, *others)


def body(images, group_ids, counts, radial_basis, ctf_gain, noise_var):
    devices = lax.axis_size("img") * lax.axis_size("grp")
    freqs = radial_basis.shape[0]
    fits = (
        freqs == OWN * devices
        and lax.axis_size("grp") * OWN == BLOCK
        and images.shape[0] == 32
        and freqs // BLOCK >= AHEAD
        and radial_basis.shape[1:] == (128, 128)
        and freqs % 128 == 0
        and images.shape[2] % 128 == 0
        and ctf_gain.shape[0] % 2 == 0
    )
    chosen = owned_body if fits else general_body
    return chosen(images, group_ids, counts, radial_basis, ctf_gain, noise_var)


def solution(mesh):
    placed = (P(("img", "grp"), None, None), P(("img", "grp")), P(), P(), P(), P())
    return jax.shard_map(
        body, mesh=mesh, in_specs=placed, out_specs=P(("img", "grp"), None, None), check_vma=False
    )
```

```python
import functools
import math

import jax
import jax.numpy as jnp
import numpy as np
from jax import lax
from jax.experimental import pallas as pl
from jax.experimental.pallas import tpu as pltpu
from jax.sharding import PartitionSpec as P

NS_ITERS = 7


def dft_tables(angles, freqs):
    angle_index = jnp.arange(angles, dtype=jnp.int32)
    freq_index = jnp.arange(freqs, dtype=jnp.int32)
    turns = angle_index[:, None] * freq_index[None, :] % angles
    phases = turns.astype(jnp.float32) * (2.0 * math.pi / angles)
    factor = 1.0 / math.sqrt(angles)
    cosine = jnp.cos(phases) * factor
    sine = -jnp.sin(phases) * factor
    forward = jnp.concatenate([cosine, sine], 1).astype(jnp.bfloat16)
    doubling = jnp.where(freq_index == 0, 1.0, 2.0).astype(jnp.float32)
    inverse = jnp.concatenate([cosine * doubling[None, :], sine * doubling[None, :]], 1).T.astype(
        jnp.bfloat16
    )
    return (forward, inverse)


def shrink_cov(gram, fourth, total, used, image_total):
    sample = gram / total[:, None, None]
    ident = used[:, :, None] * jnp.eye(used.shape[1], dtype=jnp.float32)[None]
    level = jnp.trace(sample, axis1=1, axis2=2) / jnp.sum(used, 1)
    spread = jnp.sum((sample - level[:, None, None] * ident) ** 2, (1, 2))
    excess = (fourth / total - jnp.sum(sample * sample, (1, 2))) / (2.0 * image_total)
    weight = excess / (excess + spread)
    return (1.0 - weight)[:, None, None] * sample + (weight * level)[:, None, None] * ident


def wiener_filters(cov, gain, noise_level, steps_count):
    identity = jnp.eye(cov.shape[1], dtype=jnp.float32)[None]
    system = (gain * gain)[:, None, None] * cov + noise_level[:, None, None] * identity
    frobenius = jnp.sqrt(jnp.sum(system * system, (1, 2)))
    approx = identity / frobenius[:, None, None]
    for sweep in range(steps_count):
        middle = jnp.matmul(approx, system, precision=lax.Precision.HIGHEST)
        approx = 2.0 * approx - jnp.matmul(middle, approx, precision=lax.Precision.HIGHEST)
    product = jnp.matmul(cov, approx, precision=lax.Precision.HIGHEST)
    return (gain[:, None, None] * product).astype(jnp.bfloat16)


def general_body(images, group_ids, counts, radial_basis, ctf_gain, noise_var):
    local_images = images.shape[0]
    radii = images.shape[1]
    angles = images.shape[2]
    freqs = radial_basis.shape[0]
    pmax = radial_basis.shape[2]
    groups_count = ctf_gain.shape[0]
    owners = lax.axis_size("img")
    owned = freqs // owners
    forward, inverse = dft_tables(angles, freqs)
    used = (jnp.arange(pmax, dtype=jnp.int32)[None, :] < counts[:, None]).astype(jnp.float32)
    basis_used = (radial_basis.astype(jnp.float32) * used[:, None, :]).astype(jnp.bfloat16)
    spectrum = jnp.dot(
        images.reshape(local_images * radii, angles), forward, preferred_element_type=jnp.float32
    )
    spectrum = spectrum.astype(jnp.bfloat16).reshape(local_images, radii, 2, freqs)
    coeffs = jnp.einsum(
        "nrck,krp->kcnp", spectrum, basis_used, preferred_element_type=jnp.float32
    ).astype(jnp.bfloat16)
    first = lax.axis_index("img") * owned
    arrived = lax.all_to_all(coeffs, "img", split_axis=0, concat_axis=2, tiled=True)
    all_ids = lax.all_gather(group_ids, "img", axis=0, tiled=True)
    gains_local = lax.dynamic_slice_in_dim(ctf_gain, first, owned, 1)
    noise_local = lax.dynamic_slice_in_dim(noise_var, first, owned, 0)
    used_local = lax.dynamic_slice_in_dim(used, first, owned, 0)
    onehot = (all_ids[:, None] == jnp.arange(groups_count, dtype=jnp.int32)[None, :]).astype(
        jnp.float32
    )
    gains_kn = jnp.dot(onehot, gains_local, precision=lax.Precision.HIGHEST).T
    scaled = (arrived * gains_kn[:, None, :, None]).astype(jnp.bfloat16)
    gram_part = jnp.einsum("kcnp,kcnq->kpq", scaled, scaled, preferred_element_type=jnp.float32)
    norms = jnp.einsum("kcnp,kcnp->kcn", arrived, arrived, preferred_element_type=jnp.float32)
    squares = gains_kn * gains_kn
    fourth_part = jnp.sum(squares[:, None, :] * norms * norms, (1, 2))
    total_part = 2.0 * jnp.sum(squares, 1)
    gram, fourth, total = lax.psum((gram_part, fourth_part, total_part), "grp")
    image_total = arrived.shape[2] * lax.axis_size("grp")
    cov = shrink_cov(gram, fourth, total, used_local, image_total)
    combos = groups_count * owned
    cov_all = jnp.broadcast_to(cov[None], (groups_count, owned, pmax, pmax)).reshape(
        combos, pmax, pmax
    )
    gain_all = gains_local.reshape(combos)
    noise_all = jnp.tile(noise_local, groups_count)
    share = combos // lax.axis_size("grp")
    start = lax.axis_index("grp") * share
    mine = wiener_filters(
        lax.dynamic_slice_in_dim(cov_all, start, share, 0),
        lax.dynamic_slice_in_dim(gain_all, start, share, 0),
        lax.dynamic_slice_in_dim(noise_all, start, share, 0),
        NS_ITERS,
    )
    filters = lax.all_gather(mine, "grp", axis=0, tiled=True)
    filters = filters.reshape(groups_count, owned, pmax, pmax)
    result = jnp.zeros(arrived.shape, jnp.float32)
    for which_group in range(groups_count):
        part = jnp.einsum(
            "kcnq,kpq->kcnp", arrived, filters[which_group], preferred_element_type=jnp.float32
        )
        result = result + jnp.where((all_ids == which_group)[None, None, :, None], part, 0.0)
    cleaned = result.astype(jnp.bfloat16)
    returned = lax.all_to_all(cleaned, "img", split_axis=2, concat_axis=0, tiled=True)
    back = jnp.einsum(
        "kcnp,krp->nrck", returned, basis_used, preferred_element_type=jnp.float32
    ).astype(jnp.bfloat16)
    back = back.reshape(local_images * radii, 2 * freqs)
    denoised = jnp.dot(back, inverse, preferred_element_type=jnp.float32).astype(jnp.bfloat16)
    return denoised.reshape(local_images, radii, angles)


WAYS = (
    ((0, 4, 8, 15), (1, 5, 9, 14), (2, 6, 10, 13), (3, 7, 11, 12)),
    ((0, 6, 9, 15), (1, 7, 8, 14), (3, 5, 10, 12), (2, 4, 11, 13)),
    ((2, 6, 9, 13), (1, 5, 11, 12), (0, 7, 8, 15), (3, 4, 10, 14)),
    ((2, 6, 10, 12), (1, 4, 9, 15), (0, 7, 11, 14), (3, 5, 8, 13)),
    ((2, 4, 11, 14), (0, 7, 9, 12), (3, 5, 8, 15), (1, 6, 10, 13)),
    ((3, 4, 10, 13), (1, 5, 8, 15), (0, 6, 9, 14), (2, 7, 11, 12)),
    ((2, 7, 8, 12), (3, 4, 10, 15), (1, 6, 9, 14), (0, 5, 11, 13)),
    ((2, 4, 9, 14), (0, 6, 11, 12), (1, 5, 10, 13), (3, 7, 8, 15)),
)
OWN = 4
BLOCK = 16
SENT_ROWS = (168, 208)
FULL_ROWS = SENT_ROWS[-1]
SHORT_ROWS = SENT_ROWS[0]
TRADES = ((0, 1), (2, 3), (0, 2), (1, 3))
HEAVIEST = 3 * BLOCK
IMAGE_CHUNKS = 8
AHEAD = 4
PITCH_PAD = 8
VMEM_LIMIT = 48 * 1024 * 1024
BACK_VMEM = VMEM_LIMIT
FRONT_VMEM = 121 * 512 * 1024

f32 = jnp.float32
bf16 = jnp.bfloat16


def fixed_tables(angles, freqs):
    turns = np.arange(angles)[:, None] * np.arange(freqs)[None, :] % angles
    phases = turns * (2.0 * math.pi / angles)
    cosine = np.cos(phases) / math.sqrt(angles)
    sine = -np.sin(phases) / math.sqrt(angles)
    forward = np.concatenate([cosine, sine], 1)
    doubling = np.where(np.arange(freqs) == 0, 1.0, 2.0)[None, :]
    inverse = np.concatenate([cosine * doubling, sine * doubling], 1).T
    return forward.T.astype(np.float32).astype(jnp.bfloat16), inverse.astype(np.float32).astype(jnp.bfloat16)


def owner_tables(row_of_counts, blocks):
    every = jnp.broadcast_to(row_of_counts, (blocks, row_of_counts.shape[1]))
    block = lax.broadcasted_iota(jnp.int32, every.shape, 0)
    counts = every
    for which in range(1, blocks):
        counts = jnp.where(block == which, pltpu.roll(every, every.shape[1] - BLOCK * which, 1), counts)
    counts = counts[:, :BLOCK]
    lane = lax.broadcasted_iota(jnp.int32, counts.shape, 1)
    rank = jnp.zeros(counts.shape, jnp.int32)
    for other in range(BLOCK):
        column = counts[:, other:other + 1]
        before = (column > counts) | ((column == counts) & (lane > other))
        rank = rank + before.astype(jnp.int32)
    def over_lanes(hit, value):
        return jnp.sum(jnp.where(hit, value, 0).astype(f32), 1, keepdims=True).astype(jnp.int32)

    by_rank = [over_lanes(rank == place, (counts + 1) // 2) for place in range(BLOCK)]
    least, wanted = None, None
    for way in WAYS:
        loads = [by_rank[ranks[0]] + by_rank[ranks[1]] + by_rank[ranks[2]] + by_rank[ranks[3]] for ranks in way]
        load = functools.reduce(jnp.maximum, loads)
        flat = [place for ranks in way for place in ranks]
        if least is None:
            least, wanted = load, [jnp.full(load.shape, place, jnp.int32) for place in flat]
        else:
            better = load < least
            least = jnp.where(better, load, least)
            wanted = [jnp.where(better, place, old) for place, old in zip(flat, wanted)]
    held = [jnp.zeros(least.shape, jnp.int32) for _ in wanted]
    for place in range(BLOCK):
        held = [jnp.where(want == place, by_rank[place], old) for want, old in zip(wanted, held)]
    for one, two in TRADES:
        ones, twos = range(one * OWN, (one + 1) * OWN), range(two * OWN, (two + 1) * OWN)
        gap = sum(held[i] for i in ones) - sum(held[j] for j in twos)
        best, chosen = jnp.abs(gap), jnp.full(gap.shape, -1, jnp.int32)
        for i in ones:
            for j in twos:
                left = jnp.abs(gap - 2 * (held[i] - held[j]))
                chosen = jnp.where(left < best, i * BLOCK + j, chosen)
                best = jnp.minimum(left, best)
        moves = [(i, j, chosen == i * BLOCK + j) for i in ones for j in twos]
        for values in (held, wanted):
            old = list(values)
            for i, j, move in moves:
                values[i] = jnp.where(move, old[j], values[i])
                values[j] = jnp.where(move, old[i], values[j])
    least = functools.reduce(jnp.maximum, [sum(held[dest * OWN:(dest + 1) * OWN]) for dest in range(OWN)])
    full = lax.broadcasted_iota(jnp.int32, (blocks, 128), 1)
    first = lax.broadcasted_iota(jnp.int32, (blocks, 1), 0) * BLOCK
    heaviest = jnp.max(least.astype(f32), 0, keepdims=True).astype(jnp.int32)
    table = jnp.where(full == HEAVIEST, heaviest, 0)
    for dest in range(OWN):
        offset = jnp.zeros((blocks, 1), jnp.int32)
        for own in range(OWN):
            place = dest * OWN + own
            hit = rank == wanted[place]
            freq = over_lanes(hit, lane) + first
            count = over_lanes(hit, counts)
            table = jnp.where(full == place, freq, table)
            table = jnp.where(full == place + BLOCK, count, table)
            table = jnp.where(full == place + 2 * BLOCK, offset, table)
            offset = offset + (count + 1) // 2
    return table


def low_half(shape):
    return lax.broadcasted_iota(jnp.int32, shape, 1) < 64


def swap_halves(value):
    return pltpu.roll(value, 64, 1)


def front_kernel(freqs, counts_any, ids_any, images_any, forward_any, basis_any, packed, *others):
    larger_any, table = others[:len(SENT_ROWS) - 1], others[len(SENT_ROWS) - 1]
    (counts, ids, tab, images, forward, basis, spec, turned, rows, larger, image_sems, sems, basis_sems) = others[len(SENT_ROWS):]
    wide = 2 * freqs
    pitch = wide + PITCH_PAD
    local = images.shape[0]
    blocks = freqs // BLOCK
    per_chunk = local // IMAGE_CHUNKS

    def image_copy(chunk):
        span = pl.ds(chunk * per_chunk, per_chunk)
        return pltpu.make_async_copy(images_any.at[span], images.at[span], image_sems.at[chunk])

    def basis_copy(block):
        span = pl.ds(block * BLOCK, BLOCK)
        return pltpu.make_async_copy(basis_any.at[span], basis.at[span], basis_sems.at[block])

    forward_copy = pltpu.make_async_copy(forward_any, forward, sems.at[0])
    table_copy = pltpu.make_async_copy(table, tab, sems.at[1])
    counts_copy = pltpu.make_async_copy(counts_any, counts, sems.at[2])
    ids_copy = pltpu.make_async_copy(ids_any, ids, sems.at[3])
    copies = [image_copy(chunk) for chunk in range(IMAGE_CHUNKS)] + [basis_copy(block) for block in range(blocks)]
    counts_copy.start()
    ids_copy.start()
    forward_copy.start()
    for copy in copies[:AHEAD]:
        copy.start()
    counts_copy.wait()
    table[...] = owner_tables(counts[...], blocks)
    table_copy.start()
    ids_copy.wait()
    id_row = jnp.concatenate([ids[...].astype(f32)] * (128 // local), 1)
    forward_copy.wait()

    for chunk in range(IMAGE_CHUNKS):
        copies[chunk].wait()
        copies[chunk + AHEAD].start()
        for pair in range(per_chunk // 2):
            first = chunk * per_chunk + 2 * pair
            both = images[pl.ds(first, 2)].reshape(256, images.shape[2])
            part = lax.dot_general(forward[...], both, (((1,), (1,)), ((), ())), preferred_element_type=f32)
            part = part.astype(bf16).astype(f32)
            for which in range(2):
                start = pl.multiple_of((first + which) * pitch, 8)
                spec[pl.ds(start, wide), :] = part[:, 128 * which:128 * (which + 1)]

    for copy in copies[IMAGE_CHUNKS + AHEAD:]:
        copy.start()
    table_copy.wait()
    heaviest = tab[0, HEAVIEST]
    low = low_half((64, 128))

    def gather(block, half):
        for dest in range(half * OWN, (half + 1) * OWN):
            for pair in range(2):
                place = (dest - half * OWN) * OWN + 2 * pair
                parts = []
                for which in range(2):
                    freq = tab[block, place + which]
                    real = spec[pl.ds(freq, local, stride=pitch), :]
                    imag = spec[pl.ds(freq + freqs, local, stride=pitch), :]
                    lhs = jnp.concatenate([real, imag], 0).astype(bf16)
                    parts.append(jnp.dot(lhs, basis[freq], preferred_element_type=f32).astype(bf16))
                slot = dest * 2 + pair
                turned[slot] = jnp.concatenate(parts, 0).T.astype(f32)
                even = turned[slot, pl.ds(0, 64, stride=2), :]
                odd = turned[slot, pl.ds(1, 64, stride=2), :]
                rows[dest, pl.ds(tab[block, place + 2 * BLOCK], 64), :] = jnp.where(low, even, swap_halves(odd))
                rows[dest, pl.ds(tab[block, place + 1 + 2 * BLOCK], 64), :] = jnp.where(low, swap_halves(even), odd)

    def pack(step, carry):
        for half in range(2):
            basis_copy(2 * step + half).wait()
        for half in range(2):
            gather(2 * step + half, half)
        for dest in range(2 * OWN):
            rows[dest, SHORT_ROWS - 1:SHORT_ROWS, :] = id_row
            packed[step * 2 * OWN + dest] = rows[dest, 0:SHORT_ROWS, :].astype(bf16)
        return carry

    lax.fori_loop(0, blocks // 2, pack, 0)

    for sent_rows, sent_any in zip(SENT_ROWS[1:], larger_any):

        @pl.when(heaviest > SHORT_ROWS - 1)
        def _(sent_rows=sent_rows, sent_any=sent_any):
            def pack_larger(block, carry):
                gather(block, 0)
                for dest in range(OWN):
                    rows[dest, sent_rows - 1:sent_rows, :] = id_row
                    larger[dest, 0:sent_rows, :] = rows[dest, 0:sent_rows, :].astype(bf16)
                copy = pltpu.make_async_copy(
                    larger.at[:, 0:sent_rows], sent_any.at[pl.ds(block * OWN, OWN)], sems.at[0]
                )
                copy.start()
                copy.wait()
                return carry

            lax.fori_loop(0, blocks, pack_larger, 0)


def split(value):
    high = value.astype(bf16)
    return high, (value - high.astype(f32)).astype(bf16)


def side_by_side(value):
    high, low = split(value)
    return jnp.concatenate([high, low], 1)


def wide_product(left, right):
    both = jnp.dot(left, jnp.concatenate([right, right], 0), preferred_element_type=f32)
    return both[:, :128] + both[:, 128:]


def total_of(value):
    return jnp.sum(jnp.sum(value, 1, keepdims=True), 0, keepdims=True)


def middle_kernel(image_total, me_any, tab_any, gain_any, noise_any, arrived, out,
                  me, tab, gain, noise, wide, coeff, scaled, covs, filters, clean, sems):
    small = ((me_any, me), (tab_any, tab), (gain_any, gain), (noise_any, noise))
    copies = [pltpu.make_async_copy(source, target, sems.at[i]) for i, (source, target) in enumerate(small)]
    for copy in copies:
        copy.start()
    devices, sent_rows, _ = arrived.shape
    groups_count = gain.shape[0]
    columns = devices * 64
    low = low_half((64, 128))
    wide[:, 0:sent_rows, :] = arrived[...].astype(f32)
    pieces = [
        jnp.where(low_half((1, 128)), wide[2 * m, sent_rows - 1:sent_rows, :], wide[2 * m + 1, sent_rows - 1:sent_rows, :])
        for m in range(devices // 2)
    ]
    ids = jnp.concatenate(pieces, 1)
    row = lax.broadcasted_iota(jnp.int32, (128, 128), 0)
    column = lax.broadcasted_iota(jnp.int32, (128, 128), 1)
    slot_row = jnp.where(row < 64, 2 * row, 2 * row - 127)
    eye = (row == column).astype(f32)
    for copy in copies:
        copy.wait()
    block = me[0] // OWN
    first_place = lax.rem(me[0], OWN) * OWN

    def gather(own):
        place = first_place + own
        freq = tab[block, place]
        count = tab[block, place + BLOCK]
        where = tab[block, place + 2 * BLOCK]
        used = slot_row < count
        scale = jnp.zeros((1, columns), f32)
        for g in range(groups_count):
            scale = jnp.where(ids == float(g), gain[g, freq], scale)
        squares = scale * scale
        norms = []
        for m in range(devices // 2):
            span = slice(128 * m, 128 * (m + 1))
            first = wide[2 * m, pl.ds(where, 64), :]
            second = wide[2 * m + 1, pl.ds(where, 64), :]
            even = jnp.where(low, first, swap_halves(second))
            odd = jnp.where(low, swap_halves(first), second)
            value = jnp.where(used, jnp.concatenate([even, odd], 0), 0.0)
            coeff[own, :, span] = value.astype(bf16)
            scaled[own, :, span] = (value * scale[:, span]).astype(bf16)
            norms.append(jnp.sum(value * value, 0, keepdims=True))
        norms = jnp.concatenate(norms, 1)
        fourth = jnp.sum(squares * norms * norms, 1, keepdims=True)
        total = jnp.sum(squares, 1, keepdims=True)
        weighted = scaled[own]
        gram = lax.dot_general(weighted, weighted, (((1,), (1,)), ((), ())), preferred_element_type=f32)
        sample = gram / total
        ident = jnp.where(used, eye, 0.0)
        level = total_of(sample * eye) / count.astype(f32)
        spread = total_of((sample - level * ident) ** 2)
        excess = (fourth / total - total_of(sample * sample)) / (2.0 * image_total)
        weight = excess / (excess + spread)
        covs[own] = (1.0 - weight) * sample + (weight * level) * ident

    def invert(own):
        place = first_place + own
        freq = tab[block, place]
        cov = covs[own]
        cov_parts = side_by_side(cov)
        cov_square = wide_product(cov_parts, cov_parts)
        trace = total_of(cov * eye)
        square = total_of(cov * cov)
        power, series, size = [], [], []
        for g in range(groups_count):
            h, s = gain[g, freq] * gain[g, freq], noise[freq]
            size.append(jnp.sqrt(h * h * square + 2.0 * h * s * trace + 128.0 * s * s))
            a, b = 1.0 - s / size[g], h / size[g]
            series.append((1.0 + a) * eye - b * cov)
            power.append((a * a) * eye - (2.0 * a * b) * cov + (b * b) * cov_square)
        for sweep in range(1, NS_ITERS):
            for g in range(groups_count):
                right = side_by_side(power[g])
                if sweep == NS_ITERS - 1:
                    series[g] = series[g] + wide_product(side_by_side(series[g]), right)
                else:
                    both = wide_product(jnp.concatenate([right, side_by_side(series[g])], 0), right)
                    power[g] = both[:128]
                    series[g] = series[g] + both[128:]
        for g in range(groups_count):
            product = wide_product(cov_parts, side_by_side(series[g])) * (gain[g, freq] / size[g])
            filters[own, :, 128 * g:128 * (g + 1)] = product.astype(bf16)

    def apply(own):
        where = tab[block, first_place + own + 2 * BLOCK]
        for chunk in range(columns // 256):
            span = slice(256 * chunk, 256 * (chunk + 1))
            value = coeff[own, :, span]
            masked = jnp.concatenate(
                [jnp.where(ids[:, span] == float(g), value, jnp.zeros_like(value)) for g in range(groups_count)], 0
            )
            chosen = jnp.dot(filters[own], masked, preferred_element_type=f32)
            for m in range(2):
                even = chosen[:64, 128 * m:128 * (m + 1)]
                odd = chosen[64:, 128 * m:128 * (m + 1)]
                clean[4 * chunk + 2 * m, pl.ds(where, 64), :] = jnp.where(low, even, swap_halves(odd))
                clean[4 * chunk + 2 * m + 1, pl.ds(where, 64), :] = jnp.where(low, swap_halves(even), odd)

    for turn in range(OWN + 2):
        if turn < OWN:
            gather(turn)
        if 1 <= turn <= OWN:
            invert(turn - 1)
        if turn >= 2:
            apply(turn - 2)
    out[...] = clean[:, 0:sent_rows, :].astype(bf16)


def back_kernel(freqs, tab, returned, basis, inverse, out_any, rows, turned, back, images, sems):
    wide = 2 * freqs
    pitch = wide + PITCH_PAD
    local = images.shape[0]
    blocks = freqs // BLOCK
    per_chunk = local // IMAGE_CHUNKS
    low = low_half((64, 128))
    pair_row = lax.broadcasted_iota(jnp.int32, (64, 128), 0) * 2

    def unpack(step, carry):
        for dest in range(4 * OWN):
            block = 4 * step + dest // OWN
            rows[dest, 0:returned.shape[1], :] = returned[step * 4 * OWN + dest].astype(f32)
            for pair in range(2):
                place = dest % OWN * OWN + 2 * pair
                first = rows[dest, pl.ds(tab[block, place + 2 * BLOCK], 64), :]
                second = rows[dest, pl.ds(tab[block, place + 1 + 2 * BLOCK], 64), :]
                count = jnp.where(low, tab[block, place + BLOCK], tab[block, place + 1 + BLOCK])
                even = jnp.where(low, first, swap_halves(second))
                odd = jnp.where(low, swap_halves(first), second)
                slot = dest * 2 + pair
                turned[slot, pl.ds(0, 64, stride=2), :] = jnp.where(pair_row < count, even, 0.0)
                turned[slot, pl.ds(1, 64, stride=2), :] = jnp.where(pair_row + 1 < count, odd, 0.0)
                lhs = turned[slot].astype(bf16).T
                for which in range(2):
                    freq = tab[block, place + which]
                    value = jnp.dot(lhs[64 * which:64 * (which + 1)], basis[freq], preferred_element_type=f32)
                    value = value.astype(bf16).astype(f32)
                    back[pl.ds(freq, local, stride=pitch), :] = value[:local]
                    back[pl.ds(freq + freqs, local, stride=pitch), :] = value[local:]
        return carry

    lax.fori_loop(0, blocks // 4, unpack, 0)

    def out_copy(chunk):
        span = pl.ds(chunk * per_chunk, per_chunk)
        return pltpu.make_async_copy(images.at[span], out_any.at[span], sems.at[chunk])

    def transform(chunk, carry):
        for image in range(per_chunk):
            which = chunk * per_chunk + image
            start = pl.multiple_of(which * pitch, 8)
            lhs = back[pl.ds(start, wide), :].astype(bf16)
            value = lax.dot_general(lhs, inverse[...], (((0,), (0,)), ((), ())), preferred_element_type=f32)
            images[which] = value.astype(bf16)
        out_copy(chunk).start()
        return carry

    lax.fori_loop(0, IMAGE_CHUNKS, transform, 0, unroll=True)
    for chunk in range(IMAGE_CHUNKS):
        out_copy(chunk).wait()


def front(counts, group_ids, images, radial_basis):
    local, radii, angles = images.shape
    freqs, _, pmax = radial_basis.shape
    blocks = freqs // BLOCK
    forward, _ = fixed_tables(angles, freqs)
    vmem = pl.BlockSpec(memory_space=pltpu.VMEM)
    hbm = pl.BlockSpec(memory_space=pltpu.HBM)
    return pl.pallas_call(
        functools.partial(front_kernel, freqs),
        in_specs=[hbm, hbm, hbm, hbm, hbm],
        out_specs=(vmem,) + (hbm,) * (len(SENT_ROWS) - 1) + (vmem,),
        out_shape=(
            *[jax.ShapeDtypeStruct((blocks * OWN, sent_rows, 128), bf16) for sent_rows in SENT_ROWS],
            jax.ShapeDtypeStruct((blocks, 128), jnp.int32),
        ),
        scratch_shapes=[
            pltpu.VMEM((1, freqs), jnp.int32),
            pltpu.VMEM((1, local), jnp.int32),
            pltpu.SMEM((blocks, 128), jnp.int32),
            pltpu.VMEM(images.shape, bf16),
            pltpu.VMEM(forward.shape, bf16),
            pltpu.VMEM(radial_basis.shape, bf16),
            pltpu.VMEM((local * (2 * freqs + PITCH_PAD), 128), f32),
            pltpu.VMEM((4 * OWN, 128, 128), f32),
            pltpu.VMEM((2 * OWN, FULL_ROWS + 64, 128), f32),
            pltpu.VMEM((OWN, FULL_ROWS, 128), bf16),
            pltpu.SemaphoreType.DMA((IMAGE_CHUNKS,)),
            pltpu.SemaphoreType.DMA((4,)),
            pltpu.SemaphoreType.DMA((blocks,)),
        ],
        compiler_params=pltpu.CompilerParams(vmem_limit_bytes=FRONT_VMEM),
        name="front",
    )(
        counts.reshape(1, freqs), group_ids.reshape(1, local), images, jnp.asarray(forward), radial_basis
    )


def middle(me, tab, ctf_gain, noise_var, arrived, image_total):
    hbm = pl.BlockSpec(memory_space=pltpu.HBM)
    vmem = pl.BlockSpec(memory_space=pltpu.VMEM)
    devices, sent_rows, _ = arrived.shape
    groups_count = ctf_gain.shape[0]
    return pl.pallas_call(
        functools.partial(middle_kernel, float(image_total)),
        in_specs=[hbm, hbm, hbm, hbm, vmem],
        out_specs=vmem,
        out_shape=jax.ShapeDtypeStruct(arrived.shape, bf16),
        scratch_shapes=[
            pltpu.SMEM(me.shape, jnp.int32),
            pltpu.SMEM(tab.shape, jnp.int32),
            pltpu.SMEM(ctf_gain.shape, f32),
            pltpu.SMEM(noise_var.shape, f32),
            pltpu.VMEM((devices, sent_rows + 64, 128), f32),
            pltpu.VMEM((OWN, 128, devices * 64), bf16),
            pltpu.VMEM((OWN, 128, devices * 64), bf16),
            pltpu.VMEM((OWN, 128, 128), f32),
            pltpu.VMEM((OWN, 128, groups_count * 128), bf16),
            pltpu.VMEM((devices, sent_rows + 64, 128), f32),
            pltpu.SemaphoreType.DMA((4,)),
        ],
        compiler_params=pltpu.CompilerParams(vmem_limit_bytes=VMEM_LIMIT),
        name="middle",
    )(me, tab, ctf_gain, noise_var, arrived)


def back(tab, returned, turned_basis, images_shape):
    local, radii, angles = images_shape
    freqs = turned_basis.shape[0]
    _, inverse = fixed_tables(angles, freqs)
    vmem = pl.BlockSpec(memory_space=pltpu.VMEM)
    return pl.pallas_call(
        functools.partial(back_kernel, freqs),
        in_specs=[pl.BlockSpec(memory_space=pltpu.SMEM), vmem, vmem, vmem],
        out_specs=pl.BlockSpec(memory_space=pltpu.HBM),
        out_shape=jax.ShapeDtypeStruct(images_shape, bf16),
        scratch_shapes=[
            pltpu.VMEM((4 * OWN, returned.shape[1] + 64, 128), f32),
            pltpu.VMEM((8 * OWN, 128, 128), f32),
            pltpu.VMEM((local * (2 * freqs + PITCH_PAD), 128), f32),
            pltpu.VMEM(images_shape, bf16),
            pltpu.SemaphoreType.DMA((IMAGE_CHUNKS,)),
        ],
        compiler_params=pltpu.CompilerParams(vmem_limit_bytes=BACK_VMEM),
        name="back",
    )(tab, returned, turned_basis, jnp.asarray(inverse))


def owned_body(images, group_ids, counts, radial_basis, ctf_gain, noise_var):
    axes = ("img", "grp")
    image_total = images.shape[0] * lax.axis_size(axes)
    *packed, tab = front(counts, group_ids, images, radial_basis)
    me = lax.axis_index(axes).astype(jnp.int32).reshape(1)

    def rest(packed, tab, me, radial_basis, ctf_gain, noise_var):
        arrived = lax.all_to_all(packed, axes, split_axis=0, concat_axis=0, tiled=True)
        turned_basis = jnp.swapaxes(radial_basis, 1, 2)
        arrived, turned_basis = lax.optimization_barrier((arrived, turned_basis))
        cleaned = middle(me, tab, ctf_gain, noise_var, arrived, image_total)
        returned = lax.all_to_all(cleaned, axes, split_axis=0, concat_axis=0, tiled=True)
        return back(tab, returned, turned_basis, images.shape)

    others = (tab, me, radial_basis, ctf_gain, noise_var)

    def from_level(level, packed, *others):
        if level == len(SENT_ROWS) - 1:
            return rest(packed[level], *others)
        return lax.cond(
            others[0][0, HEAVIEST] > SENT_ROWS[level] - 1,
            functools.partial(from_level, level + 1),
            lambda packed, *others: rest(packed[level], *others),
            packed, *others,
        )

    return from_level(0, packed, *others)


def body(images, group_ids, counts, radial_basis, ctf_gain, noise_var):
    devices = lax.axis_size("img") * lax.axis_size("grp")
    freqs = radial_basis.shape[0]
    fits = (
        freqs == OWN * devices
        and lax.axis_size("grp") * OWN == BLOCK
        and images.shape[0] == 32
        and freqs // BLOCK >= AHEAD
        and radial_basis.shape[1:] == (128, 128)
        and freqs % 128 == 0
        and images.shape[2] % 128 == 0
        and ctf_gain.shape[0] % 2 == 0
    )
    chosen = owned_body if fits else general_body
    return chosen(images, group_ids, counts, radial_basis, ctf_gain, noise_var)


def solution(mesh):
    placed = (P(("img", "grp"), None, None), P(("img", "grp")), P(), P(), P(), P())
    return jax.shard_map(
        body, mesh=mesh, in_specs=placed, out_specs=P(("img", "grp"), None, None), check_vma=False
    )
```

```python
import functools
import math

import jax
import jax.numpy as jnp
import numpy as np
from jax import lax
from jax.experimental import pallas as pl
from jax.experimental.pallas import tpu as pltpu
from jax.sharding import PartitionSpec as P

NS_ITERS = 7


def dft_tables(angles, freqs):
    angle_index = jnp.arange(angles, dtype=jnp.int32)
    freq_index = jnp.arange(freqs, dtype=jnp.int32)
    turns = angle_index[:, None] * freq_index[None, :] % angles
    phases = turns.astype(jnp.float32) * (2.0 * math.pi / angles)
    factor = 1.0 / math.sqrt(angles)
    cosine = jnp.cos(phases) * factor
    sine = -jnp.sin(phases) * factor
    forward = jnp.concatenate([cosine, sine], 1).astype(jnp.bfloat16)
    doubling = jnp.where(freq_index == 0, 1.0, 2.0).astype(jnp.float32)
    inverse = jnp.concatenate([cosine * doubling[None, :], sine * doubling[None, :]], 1).T.astype(
        jnp.bfloat16
    )
    return (forward, inverse)


def shrink_cov(gram, fourth, total, used, image_total):
    sample = gram / total[:, None, None]
    ident = used[:, :, None] * jnp.eye(used.shape[1], dtype=jnp.float32)[None]
    level = jnp.trace(sample, axis1=1, axis2=2) / jnp.sum(used, 1)
    spread = jnp.sum((sample - level[:, None, None] * ident) ** 2, (1, 2))
    excess = (fourth / total - jnp.sum(sample * sample, (1, 2))) / (2.0 * image_total)
    weight = excess / (excess + spread)
    return (1.0 - weight)[:, None, None] * sample + (weight * level)[:, None, None] * ident


def wiener_filters(cov, gain, noise_level, steps_count):
    identity = jnp.eye(cov.shape[1], dtype=jnp.float32)[None]
    system = (gain * gain)[:, None, None] * cov + noise_level[:, None, None] * identity
    frobenius = jnp.sqrt(jnp.sum(system * system, (1, 2)))
    approx = identity / frobenius[:, None, None]
    for sweep in range(steps_count):
        middle = jnp.matmul(approx, system, precision=lax.Precision.HIGHEST)
        approx = 2.0 * approx - jnp.matmul(middle, approx, precision=lax.Precision.HIGHEST)
    product = jnp.matmul(cov, approx, precision=lax.Precision.HIGHEST)
    return (gain[:, None, None] * product).astype(jnp.bfloat16)


def general_body(images, group_ids, counts, radial_basis, ctf_gain, noise_var):
    local_images = images.shape[0]
    radii = images.shape[1]
    angles = images.shape[2]
    freqs = radial_basis.shape[0]
    pmax = radial_basis.shape[2]
    groups_count = ctf_gain.shape[0]
    owners = lax.axis_size("img")
    owned = freqs // owners
    forward, inverse = dft_tables(angles, freqs)
    used = (jnp.arange(pmax, dtype=jnp.int32)[None, :] < counts[:, None]).astype(jnp.float32)
    basis_used = (radial_basis.astype(jnp.float32) * used[:, None, :]).astype(jnp.bfloat16)
    spectrum = jnp.dot(
        images.reshape(local_images * radii, angles), forward, preferred_element_type=jnp.float32
    )
    spectrum = spectrum.astype(jnp.bfloat16).reshape(local_images, radii, 2, freqs)
    coeffs = jnp.einsum(
        "nrck,krp->kcnp", spectrum, basis_used, preferred_element_type=jnp.float32
    ).astype(jnp.bfloat16)
    first = lax.axis_index("img") * owned
    arrived = lax.all_to_all(coeffs, "img", split_axis=0, concat_axis=2, tiled=True)
    all_ids = lax.all_gather(group_ids, "img", axis=0, tiled=True)
    gains_local = lax.dynamic_slice_in_dim(ctf_gain, first, owned, 1)
    noise_local = lax.dynamic_slice_in_dim(noise_var, first, owned, 0)
    used_local = lax.dynamic_slice_in_dim(used, first, owned, 0)
    onehot = (all_ids[:, None] == jnp.arange(groups_count, dtype=jnp.int32)[None, :]).astype(
        jnp.float32
    )
    gains_kn = jnp.dot(onehot, gains_local, precision=lax.Precision.HIGHEST).T
    scaled = (arrived * gains_kn[:, None, :, None]).astype(jnp.bfloat16)
    gram_part = jnp.einsum("kcnp,kcnq->kpq", scaled, scaled, preferred_element_type=jnp.float32)
    norms = jnp.einsum("kcnp,kcnp->kcn", arrived, arrived, preferred_element_type=jnp.float32)
    squares = gains_kn * gains_kn
    fourth_part = jnp.sum(squares[:, None, :] * norms * norms, (1, 2))
    total_part = 2.0 * jnp.sum(squares, 1)
    gram, fourth, total = lax.psum((gram_part, fourth_part, total_part), "grp")
    image_total = arrived.shape[2] * lax.axis_size("grp")
    cov = shrink_cov(gram, fourth, total, used_local, image_total)
    combos = groups_count * owned
    cov_all = jnp.broadcast_to(cov[None], (groups_count, owned, pmax, pmax)).reshape(
        combos, pmax, pmax
    )
    gain_all = gains_local.reshape(combos)
    noise_all = jnp.tile(noise_local, groups_count)
    share = combos // lax.axis_size("grp")
    start = lax.axis_index("grp") * share
    mine = wiener_filters(
        lax.dynamic_slice_in_dim(cov_all, start, share, 0),
        lax.dynamic_slice_in_dim(gain_all, start, share, 0),
        lax.dynamic_slice_in_dim(noise_all, start, share, 0),
        NS_ITERS,
    )
    filters = lax.all_gather(mine, "grp", axis=0, tiled=True)
    filters = filters.reshape(groups_count, owned, pmax, pmax)
    result = jnp.zeros(arrived.shape, jnp.float32)
    for which_group in range(groups_count):
        part = jnp.einsum(
            "kcnq,kpq->kcnp", arrived, filters[which_group], preferred_element_type=jnp.float32
        )
        result = result + jnp.where((all_ids == which_group)[None, None, :, None], part, 0.0)
    cleaned = result.astype(jnp.bfloat16)
    returned = lax.all_to_all(cleaned, "img", split_axis=2, concat_axis=0, tiled=True)
    back = jnp.einsum(
        "kcnp,krp->nrck", returned, basis_used, preferred_element_type=jnp.float32
    ).astype(jnp.bfloat16)
    back = back.reshape(local_images * radii, 2 * freqs)
    denoised = jnp.dot(back, inverse, preferred_element_type=jnp.float32).astype(jnp.bfloat16)
    return denoised.reshape(local_images, radii, angles)


WAYS = (
    ((0, 4, 8, 15), (1, 5, 9, 14), (2, 6, 10, 13), (3, 7, 11, 12)),
    ((0, 6, 9, 15), (1, 7, 8, 14), (3, 5, 10, 12), (2, 4, 11, 13)),
    ((2, 6, 9, 13), (1, 5, 11, 12), (0, 7, 8, 15), (3, 4, 10, 14)),
    ((2, 6, 10, 12), (1, 4, 9, 15), (0, 7, 11, 14), (3, 5, 8, 13)),
    ((2, 4, 11, 14), (0, 7, 9, 12), (3, 5, 8, 15), (1, 6, 10, 13)),
    ((3, 4, 10, 13), (1, 5, 8, 15), (0, 6, 9, 14), (2, 7, 11, 12)),
    ((2, 7, 8, 12), (3, 4, 10, 15), (1, 6, 9, 14), (0, 5, 11, 13)),
    ((2, 4, 9, 14), (0, 6, 11, 12), (1, 5, 10, 13), (3, 7, 8, 15)),
)
OWN = 4
BLOCK = 16
SENT_ROWS = (168, 208)
FULL_ROWS = SENT_ROWS[-1]
SHORT_ROWS = SENT_ROWS[0]
TRADES = ((0, 1), (2, 3), (0, 2), (1, 3))
HEAVIEST = 3 * BLOCK
IMAGE_CHUNKS = 8
AHEAD = 4
PITCH_PAD = 8
VMEM_LIMIT = 48 * 1024 * 1024
BACK_VMEM = VMEM_LIMIT
FRONT_VMEM = 121 * 512 * 1024

f32 = jnp.float32
bf16 = jnp.bfloat16


def fixed_tables(angles, freqs):
    turns = np.arange(angles)[:, None] * np.arange(freqs)[None, :] % angles
    phases = turns * (2.0 * math.pi / angles)
    cosine = np.cos(phases) / math.sqrt(angles)
    sine = -np.sin(phases) / math.sqrt(angles)
    forward = np.concatenate([cosine, sine], 1)
    doubling = np.where(np.arange(freqs) == 0, 1.0, 2.0)[None, :]
    inverse = np.concatenate([cosine * doubling, sine * doubling], 1).T
    return forward.T.astype(np.float32).astype(jnp.bfloat16), inverse.astype(np.float32).astype(jnp.bfloat16)


def owner_tables(row_of_counts, blocks):
    every = jnp.broadcast_to(row_of_counts, (blocks, row_of_counts.shape[1]))
    block = lax.broadcasted_iota(jnp.int32, every.shape, 0)
    counts = every
    for which in range(1, blocks):
        counts = jnp.where(block == which, pltpu.roll(every, every.shape[1] - BLOCK * which, 1), counts)
    counts = counts[:, :BLOCK]
    lane = lax.broadcasted_iota(jnp.int32, counts.shape, 1)
    rank = jnp.zeros(counts.shape, jnp.int32)
    for other in range(BLOCK):
        column = counts[:, other:other + 1]
        before = (column > counts) | ((column == counts) & (lane > other))
        rank = rank + before.astype(jnp.int32)
    def over_lanes(hit, value):
        return jnp.sum(jnp.where(hit, value, 0).astype(f32), 1, keepdims=True).astype(jnp.int32)

    by_rank = [over_lanes(rank == place, (counts + 1) // 2) for place in range(BLOCK)]
    least, wanted = None, None
    for way in WAYS:
        loads = [by_rank[ranks[0]] + by_rank[ranks[1]] + by_rank[ranks[2]] + by_rank[ranks[3]] for ranks in way]
        load = functools.reduce(jnp.maximum, loads)
        flat = [place for ranks in way for place in ranks]
        if least is None:
            least, wanted = load, [jnp.full(load.shape, place, jnp.int32) for place in flat]
        else:
            better = load < least
            least = jnp.where(better, load, least)
            wanted = [jnp.where(better, place, old) for place, old in zip(flat, wanted)]
    held = [jnp.zeros(least.shape, jnp.int32) for _ in wanted]
    for place in range(BLOCK):
        held = [jnp.where(want == place, by_rank[place], old) for want, old in zip(wanted, held)]
    for one, two in TRADES:
        ones, twos = range(one * OWN, (one + 1) * OWN), range(two * OWN, (two + 1) * OWN)
        gap = sum(held[i] for i in ones) - sum(held[j] for j in twos)
        best, chosen = jnp.abs(gap), jnp.full(gap.shape, -1, jnp.int32)
        for i in ones:
            for j in twos:
                left = jnp.abs(gap - 2 * (held[i] - held[j]))
                chosen = jnp.where(left < best, i * BLOCK + j, chosen)
                best = jnp.minimum(left, best)
        moves = [(i, j, chosen == i * BLOCK + j) for i in ones for j in twos]
        for values in (held, wanted):
            old = list(values)
            for i, j, move in moves:
                values[i] = jnp.where(move, old[j], values[i])
                values[j] = jnp.where(move, old[i], values[j])
    least = functools.reduce(jnp.maximum, [sum(held[dest * OWN:(dest + 1) * OWN]) for dest in range(OWN)])
    full = lax.broadcasted_iota(jnp.int32, (blocks, 128), 1)
    first = lax.broadcasted_iota(jnp.int32, (blocks, 1), 0) * BLOCK
    heaviest = jnp.max(least.astype(f32), 0, keepdims=True).astype(jnp.int32)
    table = jnp.where(full == HEAVIEST, heaviest, 0)
    for dest in range(OWN):
        offset = jnp.zeros((blocks, 1), jnp.int32)
        for own in range(OWN):
            place = dest * OWN + own
            hit = rank == wanted[place]
            freq = over_lanes(hit, lane) + first
            count = over_lanes(hit, counts)
            table = jnp.where(full == place, freq, table)
            table = jnp.where(full == place + BLOCK, count, table)
            table = jnp.where(full == place + 2 * BLOCK, offset, table)
            offset = offset + (count + 1) // 2
    return table


def low_half(shape):
    return lax.broadcasted_iota(jnp.int32, shape, 1) < 64


def swap_halves(value):
    return pltpu.roll(value, 64, 1)


def front_kernel(freqs, counts_any, ids_any, images_any, forward_any, basis_any, packed, *others):
    larger_any, table = others[:len(SENT_ROWS) - 1], others[len(SENT_ROWS) - 1]
    (counts, ids, tab, images, forward, basis, spec, turned, rows, larger, image_sems, sems, basis_sems) = others[len(SENT_ROWS):]
    wide = 2 * freqs
    pitch = wide + PITCH_PAD
    local = images.shape[0]
    blocks = freqs // BLOCK
    per_chunk = local // IMAGE_CHUNKS

    def image_copy(chunk):
        span = pl.ds(chunk * per_chunk, per_chunk)
        return pltpu.make_async_copy(images_any.at[span], images.at[span], image_sems.at[chunk])

    def basis_copy(block):
        span = pl.ds(block * BLOCK, BLOCK)
        return pltpu.make_async_copy(basis_any.at[span], basis.at[span], basis_sems.at[block])

    forward_copy = pltpu.make_async_copy(forward_any, forward, sems.at[0])
    table_copy = pltpu.make_async_copy(table, tab, sems.at[1])
    counts_copy = pltpu.make_async_copy(counts_any, counts, sems.at[2])
    ids_copy = pltpu.make_async_copy(ids_any, ids, sems.at[3])
    copies = [image_copy(chunk) for chunk in range(IMAGE_CHUNKS)] + [basis_copy(block) for block in range(blocks)]
    counts_copy.start()
    ids_copy.start()
    forward_copy.start()
    for copy in copies[:AHEAD]:
        copy.start()
    counts_copy.wait()
    table[...] = owner_tables(counts[...], blocks)
    table_copy.start()
    ids_copy.wait()
    id_row = jnp.concatenate([ids[...].astype(f32)] * (128 // local), 1)
    forward_copy.wait()

    for chunk in range(IMAGE_CHUNKS):
        if chunk % 2 == 0:
            for near in (chunk, chunk + 1):
                copies[near].wait()
                copies[near + AHEAD].start()
        for pair in range(per_chunk // 2):
            first = chunk * per_chunk + 2 * pair
            both = images[pl.ds(first, 2)].reshape(256, images.shape[2])
            part = lax.dot_general(forward[...], both, (((1,), (1,)), ((), ())), preferred_element_type=f32)
            part = part.astype(bf16).astype(f32)
            for which in range(2):
                start = pl.multiple_of((first + which) * pitch, 8)
                spec[pl.ds(start, wide), :] = part[:, 128 * which:128 * (which + 1)]

    for copy in copies[IMAGE_CHUNKS + AHEAD:]:
        copy.start()
    table_copy.wait()
    heaviest = tab[0, HEAVIEST]
    low = low_half((64, 128))

    def gather(block, half):
        for dest in range(half * OWN, (half + 1) * OWN):
            for pair in range(2):
                place = (dest - half * OWN) * OWN + 2 * pair
                parts = []
                for which in range(2):
                    freq = tab[block, place + which]
                    real = spec[pl.ds(freq, local, stride=pitch), :]
                    imag = spec[pl.ds(freq + freqs, local, stride=pitch), :]
                    lhs = jnp.concatenate([real, imag], 0).astype(bf16)
                    parts.append(jnp.dot(lhs, basis[freq], preferred_element_type=f32).astype(bf16))
                slot = dest * 2 + pair
                turned[slot] = jnp.concatenate(parts, 0).T.astype(f32)
                even = turned[slot, pl.ds(0, 64, stride=2), :]
                odd = turned[slot, pl.ds(1, 64, stride=2), :]
                rows[dest, pl.ds(tab[block, place + 2 * BLOCK], 64), :] = jnp.where(low, even, swap_halves(odd))
                rows[dest, pl.ds(tab[block, place + 1 + 2 * BLOCK], 64), :] = jnp.where(low, swap_halves(even), odd)

    def pack(step, carry):
        for half in range(2):
            basis_copy(2 * step + half).wait()
        for half in range(2):
            gather(2 * step + half, half)
        for dest in range(2 * OWN):
            rows[dest, SHORT_ROWS - 1:SHORT_ROWS, :] = id_row
            packed[step * 2 * OWN + dest] = rows[dest, 0:SHORT_ROWS, :].astype(bf16)
        return carry

    lax.fori_loop(0, blocks // 2, pack, 0)

    for sent_rows, sent_any in zip(SENT_ROWS[1:], larger_any):

        @pl.when(heaviest > SHORT_ROWS - 1)
        def _(sent_rows=sent_rows, sent_any=sent_any):
            def pack_larger(block, carry):
                gather(block, 0)
                for dest in range(OWN):
                    rows[dest, sent_rows - 1:sent_rows, :] = id_row
                    larger[dest, 0:sent_rows, :] = rows[dest, 0:sent_rows, :].astype(bf16)
                copy = pltpu.make_async_copy(
                    larger.at[:, 0:sent_rows], sent_any.at[pl.ds(block * OWN, OWN)], sems.at[0]
                )
                copy.start()
                copy.wait()
                return carry

            lax.fori_loop(0, blocks, pack_larger, 0)


def split(value):
    high = value.astype(bf16)
    return high, (value - high.astype(f32)).astype(bf16)


def side_by_side(value):
    high, low = split(value)
    return jnp.concatenate([high, low], 1)


def wide_product(left, right):
    both = jnp.dot(left, jnp.concatenate([right, right], 0), preferred_element_type=f32)
    return both[:, :128] + both[:, 128:]


def total_of(value):
    return jnp.sum(jnp.sum(value, 1, keepdims=True), 0, keepdims=True)


def middle_kernel(image_total, me_any, tab_any, gain_any, noise_any, arrived, out,
                  me, tab, gain, noise, wide, coeff, scaled, covs, filters, clean, sems):
    small = ((me_any, me), (tab_any, tab), (gain_any, gain), (noise_any, noise))
    copies = [pltpu.make_async_copy(source, target, sems.at[i]) for i, (source, target) in enumerate(small)]
    for copy in copies:
        copy.start()
    devices, sent_rows, _ = arrived.shape
    groups_count = gain.shape[0]
    columns = devices * 64
    low = low_half((64, 128))
    wide[:, 0:sent_rows, :] = arrived[...].astype(f32)
    pieces = [
        jnp.where(low_half((1, 128)), wide[2 * m, sent_rows - 1:sent_rows, :], wide[2 * m + 1, sent_rows - 1:sent_rows, :])
        for m in range(devices // 2)
    ]
    ids = jnp.concatenate(pieces, 1)
    row = lax.broadcasted_iota(jnp.int32, (128, 128), 0)
    column = lax.broadcasted_iota(jnp.int32, (128, 128), 1)
    slot_row = jnp.where(row < 64, 2 * row, 2 * row - 127)
    eye = (row == column).astype(f32)
    for copy in copies:
        copy.wait()
    block = me[0] // OWN
    first_place = lax.rem(me[0], OWN) * OWN

    def gather(own):
        place = first_place + own
        freq = tab[block, place]
        count = tab[block, place + BLOCK]
        where = tab[block, place + 2 * BLOCK]
        used = slot_row < count
        scale = jnp.zeros((1, columns), f32)
        for g in range(groups_count):
            scale = jnp.where(ids == float(g), gain[g, freq], scale)
        squares = scale * scale
        norms = []
        for m in range(devices // 2):
            span = slice(128 * m, 128 * (m + 1))
            first = wide[2 * m, pl.ds(where, 64), :]
            second = wide[2 * m + 1, pl.ds(where, 64), :]
            even = jnp.where(low, first, swap_halves(second))
            odd = jnp.where(low, swap_halves(first), second)
            value = jnp.where(used, jnp.concatenate([even, odd], 0), 0.0)
            coeff[own, :, span] = value.astype(bf16)
            scaled[own, :, span] = (value * scale[:, span]).astype(bf16)
            norms.append(jnp.sum(value * value, 0, keepdims=True))
        norms = jnp.concatenate(norms, 1)
        fourth = jnp.sum(squares * norms * norms, 1, keepdims=True)
        total = jnp.sum(squares, 1, keepdims=True)
        weighted = scaled[own]
        gram = lax.dot_general(weighted, weighted, (((1,), (1,)), ((), ())), preferred_element_type=f32)
        sample = gram / total
        ident = jnp.where(used, eye, 0.0)
        level = total_of(sample * eye) / count.astype(f32)
        spread = total_of((sample - level * ident) ** 2)
        excess = (fourth / total - total_of(sample * sample)) / (2.0 * image_total)
        weight = excess / (excess + spread)
        covs[own] = (1.0 - weight) * sample + (weight * level) * ident

    def invert(own):
        place = first_place + own
        freq = tab[block, place]
        cov = covs[own]
        cov_parts = side_by_side(cov)
        cov_square = wide_product(cov_parts, cov_parts)
        trace = total_of(cov * eye)
        square = total_of(cov * cov)
        power, series, size = [], [], []
        for g in range(groups_count):
            h, s = gain[g, freq] * gain[g, freq], noise[freq]
            size.append(jnp.sqrt(h * h * square + 2.0 * h * s * trace + 128.0 * s * s))
            a, b = 1.0 - s / size[g], h / size[g]
            series.append((1.0 + a) * eye - b * cov)
            power.append((a * a) * eye - (2.0 * a * b) * cov + (b * b) * cov_square)
        for sweep in range(1, NS_ITERS):
            for g in range(groups_count):
                right = side_by_side(power[g])
                if sweep == NS_ITERS - 1:
                    series[g] = series[g] + wide_product(side_by_side(series[g]), right)
                else:
                    both = wide_product(jnp.concatenate([right, side_by_side(series[g])], 0), right)
                    power[g] = both[:128]
                    series[g] = series[g] + both[128:]
        for g in range(groups_count):
            product = wide_product(cov_parts, side_by_side(series[g])) * (gain[g, freq] / size[g])
            filters[own, :, 128 * g:128 * (g + 1)] = product.astype(bf16)

    def apply(own):
        where = tab[block, first_place + own + 2 * BLOCK]
        for chunk in range(columns // 256):
            span = slice(256 * chunk, 256 * (chunk + 1))
            value = coeff[own, :, span]
            masked = jnp.concatenate(
                [jnp.where(ids[:, span] == float(g), value, jnp.zeros_like(value)) for g in range(groups_count)], 0
            )
            chosen = jnp.dot(filters[own], masked, preferred_element_type=f32)
            for m in range(2):
                even = chosen[:64, 128 * m:128 * (m + 1)]
                odd = chosen[64:, 128 * m:128 * (m + 1)]
                clean[4 * chunk + 2 * m, pl.ds(where, 64), :] = jnp.where(low, even, swap_halves(odd))
                clean[4 * chunk + 2 * m + 1, pl.ds(where, 64), :] = jnp.where(low, swap_halves(even), odd)

    for turn in range(OWN + 2):
        if turn < OWN:
            gather(turn)
        if 1 <= turn <= OWN:
            invert(turn - 1)
        if turn >= 2:
            apply(turn - 2)
    out[...] = clean[:, 0:sent_rows, :].astype(bf16)


def back_kernel(freqs, tab, returned, basis, inverse, out_any, rows, turned, back, images, sems):
    wide = 2 * freqs
    pitch = wide + PITCH_PAD
    local = images.shape[0]
    blocks = freqs // BLOCK
    per_chunk = local // IMAGE_CHUNKS
    low = low_half((64, 128))
    pair_row = lax.broadcasted_iota(jnp.int32, (64, 128), 0) * 2

    def unpack(step, carry):
        for dest in range(4 * OWN):
            block = 4 * step + dest // OWN
            rows[dest, 0:returned.shape[1], :] = returned[step * 4 * OWN + dest].astype(f32)
            for pair in range(2):
                place = dest % OWN * OWN + 2 * pair
                first = rows[dest, pl.ds(tab[block, place + 2 * BLOCK], 64), :]
                second = rows[dest, pl.ds(tab[block, place + 1 + 2 * BLOCK], 64), :]
                count = jnp.where(low, tab[block, place + BLOCK], tab[block, place + 1 + BLOCK])
                even = jnp.where(low, first, swap_halves(second))
                odd = jnp.where(low, swap_halves(first), second)
                slot = dest * 2 + pair
                turned[slot, pl.ds(0, 64, stride=2), :] = jnp.where(pair_row < count, even, 0.0)
                turned[slot, pl.ds(1, 64, stride=2), :] = jnp.where(pair_row + 1 < count, odd, 0.0)
                lhs = turned[slot].astype(bf16).T
                for which in range(2):
                    freq = tab[block, place + which]
                    value = jnp.dot(lhs[64 * which:64 * (which + 1)], basis[freq], preferred_element_type=f32)
                    value = value.astype(bf16).astype(f32)
                    back[pl.ds(freq, local, stride=pitch), :] = value[:local]
                    back[pl.ds(freq + freqs, local, stride=pitch), :] = value[local:]
        return carry

    lax.fori_loop(0, blocks // 4, unpack, 0)

    def out_copy(chunk):
        span = pl.ds(chunk * per_chunk, per_chunk)
        return pltpu.make_async_copy(images.at[span], out_any.at[span], sems.at[chunk])

    def transform(chunk, carry):
        for image in range(per_chunk):
            which = chunk * per_chunk + image
            start = pl.multiple_of(which * pitch, 8)
            lhs = back[pl.ds(start, wide), :].astype(bf16)
            value = lax.dot_general(lhs, inverse[...], (((0,), (0,)), ((), ())), preferred_element_type=f32)
            images[which] = value.astype(bf16)
        out_copy(chunk).start()
        return carry

    lax.fori_loop(0, IMAGE_CHUNKS, transform, 0, unroll=True)
    for chunk in range(IMAGE_CHUNKS):
        out_copy(chunk).wait()


def front(counts, group_ids, images, radial_basis):
    local, radii, angles = images.shape
    freqs, _, pmax = radial_basis.shape
    blocks = freqs // BLOCK
    forward, _ = fixed_tables(angles, freqs)
    vmem = pl.BlockSpec(memory_space=pltpu.VMEM)
    hbm = pl.BlockSpec(memory_space=pltpu.HBM)
    return pl.pallas_call(
        functools.partial(front_kernel, freqs),
        in_specs=[hbm, hbm, hbm, hbm, hbm],
        out_specs=(vmem,) + (hbm,) * (len(SENT_ROWS) - 1) + (vmem,),
        out_shape=(
            *[jax.ShapeDtypeStruct((blocks * OWN, sent_rows, 128), bf16) for sent_rows in SENT_ROWS],
            jax.ShapeDtypeStruct((blocks, 128), jnp.int32),
        ),
        scratch_shapes=[
            pltpu.VMEM((1, freqs), jnp.int32),
            pltpu.VMEM((1, local), jnp.int32),
            pltpu.SMEM((blocks, 128), jnp.int32),
            pltpu.VMEM(images.shape, bf16),
            pltpu.VMEM(forward.shape, bf16),
            pltpu.VMEM(radial_basis.shape, bf16),
            pltpu.VMEM((local * (2 * freqs + PITCH_PAD), 128), f32),
            pltpu.VMEM((4 * OWN, 128, 128), f32),
            pltpu.VMEM((2 * OWN, FULL_ROWS + 64, 128), f32),
            pltpu.VMEM((OWN, FULL_ROWS, 128), bf16),
            pltpu.SemaphoreType.DMA((IMAGE_CHUNKS,)),
            pltpu.SemaphoreType.DMA((4,)),
            pltpu.SemaphoreType.DMA((blocks,)),
        ],
        compiler_params=pltpu.CompilerParams(vmem_limit_bytes=FRONT_VMEM),
        name="front",
    )(
        counts.reshape(1, freqs), group_ids.reshape(1, local), images, jnp.asarray(forward), radial_basis
    )


def middle(me, tab, ctf_gain, noise_var, arrived, image_total):
    hbm = pl.BlockSpec(memory_space=pltpu.HBM)
    vmem = pl.BlockSpec(memory_space=pltpu.VMEM)
    devices, sent_rows, _ = arrived.shape
    groups_count = ctf_gain.shape[0]
    return pl.pallas_call(
        functools.partial(middle_kernel, float(image_total)),
        in_specs=[hbm, hbm, hbm, hbm, vmem],
        out_specs=vmem,
        out_shape=jax.ShapeDtypeStruct(arrived.shape, bf16),
        scratch_shapes=[
            pltpu.SMEM(me.shape, jnp.int32),
            pltpu.SMEM(tab.shape, jnp.int32),
            pltpu.SMEM(ctf_gain.shape, f32),
            pltpu.SMEM(noise_var.shape, f32),
            pltpu.VMEM((devices, sent_rows + 64, 128), f32),
            pltpu.VMEM((OWN, 128, devices * 64), bf16),
            pltpu.VMEM((OWN, 128, devices * 64), bf16),
            pltpu.VMEM((OWN, 128, 128), f32),
            pltpu.VMEM((OWN, 128, groups_count * 128), bf16),
            pltpu.VMEM((devices, sent_rows + 64, 128), f32),
            pltpu.SemaphoreType.DMA((4,)),
        ],
        compiler_params=pltpu.CompilerParams(vmem_limit_bytes=VMEM_LIMIT),
        name="middle",
    )(me, tab, ctf_gain, noise_var, arrived)


def back(tab, returned, turned_basis, images_shape):
    local, radii, angles = images_shape
    freqs = turned_basis.shape[0]
    _, inverse = fixed_tables(angles, freqs)
    vmem = pl.BlockSpec(memory_space=pltpu.VMEM)
    return pl.pallas_call(
        functools.partial(back_kernel, freqs),
        in_specs=[pl.BlockSpec(memory_space=pltpu.SMEM), vmem, vmem, vmem],
        out_specs=pl.BlockSpec(memory_space=pltpu.HBM),
        out_shape=jax.ShapeDtypeStruct(images_shape, bf16),
        scratch_shapes=[
            pltpu.VMEM((4 * OWN, returned.shape[1] + 64, 128), f32),
            pltpu.VMEM((8 * OWN, 128, 128), f32),
            pltpu.VMEM((local * (2 * freqs + PITCH_PAD), 128), f32),
            pltpu.VMEM(images_shape, bf16),
            pltpu.SemaphoreType.DMA((IMAGE_CHUNKS,)),
        ],
        compiler_params=pltpu.CompilerParams(vmem_limit_bytes=BACK_VMEM),
        name="back",
    )(tab, returned, turned_basis, jnp.asarray(inverse))


def owned_body(images, group_ids, counts, radial_basis, ctf_gain, noise_var):
    axes = ("img", "grp")
    image_total = images.shape[0] * lax.axis_size(axes)
    *packed, tab = front(counts, group_ids, images, radial_basis)
    me = lax.axis_index(axes).astype(jnp.int32).reshape(1)

    def rest(packed, tab, me, radial_basis, ctf_gain, noise_var):
        arrived = lax.all_to_all(packed, axes, split_axis=0, concat_axis=0, tiled=True)
        turned_basis = jnp.swapaxes(radial_basis, 1, 2)
        arrived, turned_basis = lax.optimization_barrier((arrived, turned_basis))
        cleaned = middle(me, tab, ctf_gain, noise_var, arrived, image_total)
        returned = lax.all_to_all(cleaned, axes, split_axis=0, concat_axis=0, tiled=True)
        return back(tab, returned, turned_basis, images.shape)

    others = (tab, me, radial_basis, ctf_gain, noise_var)

    def from_level(level, packed, *others):
        if level == len(SENT_ROWS) - 1:
            return rest(packed[level], *others)
        return lax.cond(
            others[0][0, HEAVIEST] > SENT_ROWS[level] - 1,
            functools.partial(from_level, level + 1),
            lambda packed, *others: rest(packed[level], *others),
            packed, *others,
        )

    return from_level(0, packed, *others)


def body(images, group_ids, counts, radial_basis, ctf_gain, noise_var):
    devices = lax.axis_size("img") * lax.axis_size("grp")
    freqs = radial_basis.shape[0]
    fits = (
        freqs == OWN * devices
        and lax.axis_size("grp") * OWN == BLOCK
        and images.shape[0] == 32
        and freqs // BLOCK >= AHEAD
        and radial_basis.shape[1:] == (128, 128)
        and freqs % 128 == 0
        and images.shape[2] % 128 == 0
        and ctf_gain.shape[0] % 2 == 0
    )
    chosen = owned_body if fits else general_body
    return chosen(images, group_ids, counts, radial_basis, ctf_gain, noise_var)


def solution(mesh):
    placed = (P(("img", "grp"), None, None), P(("img", "grp")), P(), P(), P(), P())
    return jax.shard_map(
        body, mesh=mesh, in_specs=placed, out_specs=P(("img", "grp"), None, None), check_vma=False
    )
```
